256 devices in a mesh: dp: 8 (over z), mp: 32 (over x, y, core).
Axes of the slice: x: 4, y: 4, z: 8, core: 2. Of those that a mesh axis runs over, the one named last changes fastest.
Arguments:
- momentum: bfloat16 [8192, 26624], P('mp', 'dp'), may hold values from -3 to 3
- tile_values: bfloat16 [8192, 26624], P('mp', 'dp'), may hold values from -448 to 448
- exponents: int32 [64, 208], P('mp', 'dp'), may hold values from -11 to -8
- overflow: int32 [32, 8], P('mp', 'dp'), may hold values from 0 to 1, as said below
- right_prev: float32 [26624, 128], P(('dp', 'mp')), may hold values from -6 to 6
Outputs:
- momentum_new: bfloat16 [8192, 26624], P('mp', 'dp')
- right_factor: float32 [26624, 128], P(('dp', 'mp'))
- update: bfloat16 [8192, 26624], P('mp', 'dp')
The draws below stay inside these ranges and needn't reach their ends.
Inputs may be any that keep to these rules, and one draw needn't show every extreme that they name: `overflow`: 1 marks a tile whose gradient is dropped; some tile is dropped and some is kept. `exponents`: one exponent for each block.
All inputs are finite; a program needn't handle non-finite values.
Results may differ from the reference program's by a relative error of at most 0.0075.
Values may be sent and summed in bfloat16 or wider, within the bound.
A program may use at most 64 MiB of HBM per device.

```python
import math
import jax
import jax.numpy as jnp
from jax import lax

ROWS = 8192
COLS = 26624
RANK = 128
BLOCK = 128
ROWS_DEV = 256
COLS_DEV = 3328
N_DP = 8
N_MP = 32


def column_scales(spread):
    position = jnp.arange(COLS, dtype=jnp.float32) / (COLS - 1)
    return jnp.exp((position - 0.5) * spread)[None, :]


def draw_momentum(key, part):
    key = jax.random.fold_in(key, 11)
    keys = jax.random.split(key, 3)
    inner = max(RANK // 8, 1)
    left_fac = jax.random.normal(keys[0], (ROWS, inner), jnp.float32)
    right_fac = jax.random.normal(keys[1], (inner, COLS), jnp.float32)
    noise = jax.random.normal(keys[2], (ROWS, COLS), jnp.float32)
    col_scale = column_scales(1.0986123)
    low_part = jnp.zeros((ROWS, COLS), jnp.float32)
    for index in range(inner):
        low_part = low_part + left_fac[:, index:index + 1] * right_fac[index:index + 1, :]
    low_part = low_part * (0.95 / inner ** 0.5)
    values = col_scale * (low_part + 0.15 * noise)
    return jnp.clip(values, -3.0, 3.0).astype(jnp.bfloat16)


def draw_overflow(key, part):
    key = jax.random.fold_in(key, 23)
    total = N_MP * N_DP
    row_index = jnp.arange(N_MP, dtype=jnp.int32)[:, None]
    col_index = jnp.arange(N_DP, dtype=jnp.int32)[None, :]
    flat = col_index * N_MP + row_index
    threshold = 750 - 700 * flat // (total - 1)
    tickets = jax.random.randint(key, (N_MP, N_DP), 0, 1000, jnp.int32)
    flags = (tickets < threshold).astype(jnp.int32)
    flags = jnp.where(flat == 0, 1, flags)
    flags = jnp.where(flat == total - 1, 0, flags)
    return flags.astype(jnp.int32)


def plant(array, stream_key, low, largest):
    shape = array.shape
    index_at = [jax.random.randint(jax.random.fold_in(stream_key, axis), (), 0, shape[axis]) for axis in range(len(shape))]
    array = array.at[tuple(index_at)].set(low)
    longest = shape.index(max(shape))
    index_at[longest] = (index_at[longest] + 1) % shape[longest]
    return array.at[tuple(index_at)].set(largest)


def steps_of(key, dims, cuts, smallest, top_value):
    gain, own = 1.0, jax.random.fold_in(key, 6)
    for dim, shards_of in cuts:
        draws = jnp.exp(jax.random.uniform(jax.random.fold_in(own, dim), (shards_of,), jnp.float32, smallest / len(cuts), top_value / len(cuts)))
        gain = gain * jnp.repeat(draws, dims[dim] // shards_of).reshape([-1 if axis == dim else 1 for axis in range(len(dims))])
    return gain


def bell_draw(stream_key, extent, deviation, limit, cuts=(), kind=jnp.bfloat16):
    entries = deviation * jax.random.normal(stream_key, extent, jnp.float32)
    if cuts:
        entries = entries * steps_of(stream_key, extent, cuts, -0.22, 0.18)
    return jnp.clip(entries, -limit, limit).astype(kind)


def setup_inputs(seed: int = 0) -> dict:
    key_list = jax.random.split(jax.random.key(seed), 6)
    return {
        "momentum": draw_momentum(jax.random.fold_in(key_list[5], 71), 0),
        "tile_values": bell_draw(key_list[1], (ROWS, COLS), 64.0, 448.0, ((0, 32), (1, 8))),
        "exponents": plant(jax.random.randint(key_list[2], (ROWS // BLOCK, COLS // BLOCK), -11, -7), jax.random.fold_in(key_list[2], 1), -11, (-7) - 1).astype(jnp.int32),
        "overflow": draw_overflow(jax.random.fold_in(key_list[5], 71), 0),
        "right_prev": bell_draw(key_list[4], (COLS, RANK), 1.0, 6.0, ((0, 256),), jnp.float32),
    }


epsilon = 1e-06
retain = 0.95

def decode(tile_values, exponents, overflow):
    scales = jnp.exp2(exponents.astype(jnp.float32)).astype(jnp.bfloat16)
    blocks = tile_values.reshape(ROWS // BLOCK, BLOCK, COLS // BLOCK, BLOCK)
    decoded = (blocks * scales[:, None, :, None]).reshape(N_MP, ROWS_DEV, N_DP, COLS_DEV)
    kept_tile = (overflow == 0)[:, None, :, None]
    return jnp.where(kept_tile, decoded, jnp.zeros_like(decoded)).reshape(ROWS, COLS)

def trans_dot(left_mat, right_mat):
    return lax.dot_general(left_mat.astype(jnp.float32), right_mat.astype(jnp.float32), (((0,), (0,)), ((), ())), preferred_element_type=jnp.float32)

def reference(momentum, tile_values, exponents, overflow, right_prev):
    gradient = decode(tile_values, exponents, overflow)
    healthy = jnp.sum((overflow == 0).astype(jnp.float32))
    factor = N_MP * N_DP / jnp.maximum(healthy, 1.0)
    right_low = right_prev.astype(jnp.bfloat16)
    left_raw = jnp.dot(momentum.astype(jnp.float32), right_low.astype(jnp.float32), preferred_element_type=jnp.float32) + factor * jnp.dot(gradient.astype(jnp.float32), right_low.astype(jnp.float32), preferred_element_type=jnp.float32)
    q_part, r_part = jnp.linalg.qr(left_raw)
    ortho = q_part * jnp.sign(jnp.diag(r_part))[None, :]
    ortho_low = ortho.astype(jnp.bfloat16)
    right_factor = trans_dot(momentum, ortho_low) + factor * trans_dot(gradient, ortho_low)
    inverse = lax.rsqrt(lax.optimization_barrier(jnp.sum(right_factor * right_factor, 0)) + epsilon)
    factor_low = right_factor.astype(jnp.bfloat16)
    normal_low = (right_factor * inverse[None, :]).astype(jnp.bfloat16)
    unit_scale = math.sqrt(ROWS * COLS / RANK)

    def finish(items):
        mom_tile, grad_tile, ortho_tile = items
        correction = lax.dot_general(ortho_tile.astype(jnp.float32), factor_low.astype(jnp.float32), (((1,), (1,)), ((), ())), preferred_element_type=jnp.float32)
        direction = lax.dot_general(ortho_tile.astype(jnp.float32), normal_low.astype(jnp.float32), (((1,), (1,)), ((), ())), preferred_element_type=jnp.float32)
        mom_next = (mom_tile.astype(jnp.float32) + factor * grad_tile.astype(jnp.float32) - (1.0 - retain) * correction).astype(jnp.bfloat16)
        return (mom_next, (unit_scale * direction).astype(jnp.bfloat16))
    momentum_new, update = lax.map(finish, (momentum.reshape(N_MP, ROWS_DEV, COLS), gradient.reshape(N_MP, ROWS_DEV, COLS), ortho_low.reshape(N_MP, ROWS_DEV, RANK)))
    return (momentum_new.reshape(ROWS, COLS), right_factor, update.reshape(ROWS, COLS))
```

```python
import functools
import math

import jax
import jax.numpy as jnp
from jax import lax
from jax.experimental import pallas as pl
from jax.experimental.pallas import tpu as pltpu
from jax.sharding import PartitionSpec as P

MESH = pl.DeviceIdType.MESH
F32 = jnp.float32
BF16 = jnp.bfloat16
HIGH = lax.Precision.HIGHEST
BLOCK = 128
EPSILON = 1e-06
RETAIN = 0.95
VMEM_LIMIT = 48 * 1024 * 1024


class Place:
    def __init__(self, n_dp, n_mp):
        self.nz = n_dp
        self.chips = n_mp // 2
        self.ny = int(round(math.sqrt(self.chips)))
        self.nx = self.chips // self.ny
        self.half = self.chips // 2
        mp = lax.axis_index("mp")
        self.z = lax.axis_index("dp")
        self.core = lax.rem(mp, 2)
        self.other = 1 - self.core
        self.chip = mp // 2
        self.x = self.chip // self.ny
        self.y = lax.rem(self.chip, self.ny)

    def chip_at(self, dx, dy):
        x = lax.rem(self.x + dx + self.nx, self.nx)
        y = lax.rem(self.y + dy + self.ny, self.ny)
        return x * self.ny + y

    def offset(self, i, parity):
        dx = i // (self.ny // 2)
        dy = 2 * (i % (self.ny // 2)) + lax.rem(dx + parity, 2)
        return dx, dy

    def to_chip(self, i, parity):
        dx, dy = self.offset(i, parity)
        return self.chip_at(dx, dy)

    def from_chip(self, i, parity):
        dx, dy = self.offset(i, parity)
        return self.chip_at(-dx, -dy)

    def z_at(self, dz):
        return lax.rem(self.z + dz, self.nz)

    def dev(self, z, chip, core):
        return (z, chip * 2 + core)

    def sibling(self):
        return self.dev(self.z, self.chip, self.other)

    def plane_peers(self):
        return [
            self.dev(self.z, self.chip_at(dx, dy), self.core)
            for dx in range(self.nx)
            for dy in range(self.ny)
            if dx or dy
        ]

    def z_peers(self):
        return [self.dev(self.z_at(dz), self.chip, self.core) for dz in range(1, self.nz)]

    def zc_peers(self):
        return [
            self.dev(self.z_at(dz), self.chip, self.core if dc == 0 else self.other)
            for dz in range(self.nz)
            for dc in range(2)
            if dz or dc
        ]


def remote(src, dst, send, recv, dev):
    return pltpu.make_async_remote_copy(
        src_ref=src, dst_ref=dst, send_sem=send, recv_sem=recv, device_id=dev, device_id_type=MESH
    )


def greet(peers):
    barrier = pltpu.get_barrier_semaphore()
    for dev in peers:
        pl.semaphore_signal(barrier, inc=1, device_id=dev, device_id_type=MESH)
    pl.semaphore_wait(barrier, len(peers))


def exchange(place, peers, src_of, dst, sems, slot):
    copies = [
        remote(src_of(k), dst.at[slot], sems.at[0, k], sems.at[1, k], dev) for k, dev in enumerate(peers)
    ]
    for copy in copies:
        copy.start()
    return copies


def gather_send(place, buf, rows, sems):
    block = buf.at[pl.ds(pl.multiple_of(place.chip * rows, 16), rows)]
    for i in range(place.half):
        copy = remote(
            block, block, sems.at[0, i], sems.at[1, i], place.dev(place.z, place.to_chip(i, place.core), place.core)
        )
        if i == 0:
            pl.when(place.core == 1)(copy.start)
        else:
            copy.start()


def gather_forward(place, buf, rows, sems, i):
    start = pl.multiple_of(place.from_chip(i, place.core) * rows, 16)
    block = buf.at[pl.ds(start, rows)]

    def go():
        remote(block, block, sems.at[0, i], sems.at[1, i], place.sibling()).wait_recv()
        remote(block, block, sems.at[2, i], sems.at[3, i], place.sibling()).start()

    if i == 0:
        pl.when(place.core == 1)(go)
    else:
        go()


def gather_finish(place, buf, rows, sems):
    for i in range(place.half):
        start = pl.multiple_of(place.from_chip(i, place.other) * rows, 16)
        block = buf.at[pl.ds(start, rows)]
        copy = remote(block, block, sems.at[2, i], sems.at[3, i], place.sibling())
        if i == 0:
            pl.when(place.core == 0)(copy.wait_recv)
        else:
            copy.wait_recv()
    for i in range(place.half):
        block = buf.at[pl.ds(0, rows)]
        sent = remote(block, block, sems.at[0, i], sems.at[1, i], place.sibling())
        passed = remote(block, block, sems.at[2, i], sems.at[3, i], place.sibling())

        def done(sent=sent, passed=passed):
            sent.wait_send()
            passed.wait_send()

        if i == 0:
            pl.when(place.core == 1)(done)
        else:
            done()


def left_kernel(
    n_dp, n_mp,
    mom_hbm, tile_hbm, exps_ref, over_ref, prev_ref,
    gram_ref, left_ref, factor_ref, scale_ref,
    mom, tile, pair, right, flag_z, flag_c, flag_p, part, left_in, left, gram, gram_zc, gram_p, gram_all,
    sem_in, sem_pair, sem_gather, sem_fz, sem_fc, sem_fp, sem_lr, sem_lg, sem_gr, sem_gp, sem_gg,
):
    place = Place(n_dp, n_mp)
    rows, cols = mom.shape
    share = prev_ref.shape[0]
    block = 2 * share
    loads = [
        pltpu.make_async_copy(mom_hbm, mom, sem_in.at[0]),
        pltpu.make_async_copy(tile_hbm, tile, sem_in.at[1]),
    ]
    for load in loads:
        load.start()
    plane, zline, zc = place.plane_peers(), place.z_peers(), place.zc_peers()
    kept = jnp.where(over_ref[...] == 0, 1.0, 0.0).astype(F32)
    flag_z[place.z] = jnp.broadcast_to(kept, (8, 128))
    mine = pl.ds(pl.multiple_of(place.core * share, 8), share)
    pair[mine] = prev_ref[...]
    greet(plane + zc)

    pair_copy = remote(pair.at[mine], pair.at[mine], sem_pair.at[0], sem_pair.at[1], place.sibling())
    pair_copy.start()
    fz = exchange(place, zline, lambda k: flag_z.at[place.z], flag_z, sem_fz, place.z)
    pair_copy.wait_recv()
    right[pl.ds(pl.multiple_of(place.chip * block, 16), block)] = pair[...].astype(BF16)
    gather_send(place, right, block, sem_gather)

    for copy in fz:
        copy.wait_recv()
    flag_c[place.core] = jnp.sum(flag_z[...], axis=0)
    fc = remote(flag_c.at[place.core], flag_c.at[place.core], sem_fc.at[0], sem_fc.at[1], place.sibling())
    fc.start()
    scales = jnp.exp2(exps_ref[...].astype(F32)).astype(BF16).astype(F32) * kept
    for j in range(cols // BLOCK):
        scale_ref[:, j * BLOCK:(j + 1) * BLOCK] = jnp.broadcast_to(scales[:, j:j + 1], (scales.shape[0], BLOCK))
    for load in loads:
        load.wait()
    fc.wait_recv()
    flag_p[place.chip] = flag_c[0] + flag_c[1]
    fp = exchange(place, plane, lambda k: flag_p.at[place.chip], flag_p, sem_fp, place.chip)
    for b in range(rows // BLOCK):
        scale = scale_ref[b:b + 1, :].astype(BF16)
        for r in range(0, BLOCK, 32):
            at = slice(b * BLOCK + r, b * BLOCK + r + 32)
            tile[at, :] = tile[at, :] * scale
    for i in range(place.half):
        gather_forward(place, right, block, sem_gather, i)
    for copy in fp:
        copy.wait_recv()
    healthy = jnp.sum(flag_p[...], axis=0)
    factor = float(n_dp * n_mp) / jnp.maximum(healthy, 1.0)
    factor_ref[...] = factor
    gather_finish(place, right, block, sem_gather)

    mom_part = jnp.dot(mom[...], right[...], preferred_element_type=F32)
    grad_part = jnp.dot(tile[...], right[...], preferred_element_type=F32)
    part[...] = mom_part + factor[0:1, :] * grad_part

    rz = rows // place.nz
    lr = []
    for dz in range(1, place.nz):
        z2 = place.z_at(dz)
        copy = remote(
            part.at[pl.ds(pl.multiple_of(z2 * rz, 8), rz)], left_in.at[dz - 1],
            sem_lr.at[0, dz - 1], sem_lr.at[1, dz - 1], place.dev(z2, place.chip, place.core),
        )
        copy.start()
        lr.append(copy)
    own = pl.ds(pl.multiple_of(place.z * rz, 8), rz)
    acc = part[own]
    for k, copy in enumerate(lr):
        copy.wait_recv()
        acc = acc + left_in[k]
    left[own] = acc
    gram[...] = lax.dot_general(acc, acc, (((0,), (0,)), ((), ())), precision=HIGH, preferred_element_type=F32)

    gs = gram.shape[0] // (2 * place.nz)
    gr = []
    k = 0
    for dz in range(place.nz):
        for dc in range(2):
            if dz or dc:
                z2, c2 = place.z_at(dz), place.core if dc == 0 else place.other
                copy = remote(
                    gram.at[pl.ds(pl.multiple_of((z2 * 2 + c2) * gs, 8), gs)], gram_zc.at[k],
                    sem_gr.at[0, k], sem_gr.at[1, k], place.dev(z2, place.chip, c2),
                )
                copy.start()
                gr.append(copy)
                k += 1
    lg = [
        remote(left.at[own], left.at[own], sem_lg.at[0, k], sem_lg.at[1, k], dev) for k, dev in enumerate(zline)
    ]
    for copy in lg:
        copy.start()
    piece = pl.ds(pl.multiple_of((place.z * 2 + place.core) * gs, 8), gs)
    acc = gram[piece]
    for k, copy in enumerate(gr):
        copy.wait_recv()
        acc = acc + gram_zc[k]
    gram_p[place.chip] = acc
    gp = exchange(place, plane, lambda k: gram_p.at[place.chip], gram_p, sem_gp, place.chip)
    for copy in gp:
        copy.wait_recv()
    gram_all[piece] = jnp.sum(gram_p[...], axis=0)
    gg = [
        remote(gram_all.at[piece], gram_all.at[piece], sem_gg.at[0, k], sem_gg.at[1, k], dev)
        for k, dev in enumerate(zc)
    ]
    for copy in gg:
        copy.start()
    for copy in lg:
        copy.wait_recv()
    left_ref[...] = left[...]
    for copy in gg:
        copy.wait_recv()
    gram_ref[...] = gram_all[...]
    for copy in [pair_copy, fc] + fz + fp + lr + gr + lg + gp + gg:
        copy.wait_send()


def left_stage(n_dp, n_mp, momentum, tile_values, exponents, overflow, right_prev):
    rows, cols = momentum.shape
    share, rank = right_prev.shape
    chips = n_mp // 2
    rz = rows // n_dp
    gs = rank // (2 * n_dp)
    vmem = pl.BlockSpec(memory_space=pltpu.VMEM)
    hbm = pl.BlockSpec(memory_space=pl.ANY)
    dma = pltpu.SemaphoreType.DMA
    return pl.pallas_call(
        functools.partial(left_kernel, n_dp, n_mp),
        name="left",
        out_shape=(
            jax.ShapeDtypeStruct((rank, rank), F32),
            jax.ShapeDtypeStruct((rows, rank), F32),
            jax.ShapeDtypeStruct((8, 128), F32),
            jax.ShapeDtypeStruct((rows // BLOCK, cols), F32),
        ),
        in_specs=[hbm, hbm, vmem, vmem, vmem],
        out_specs=(vmem,) * 4,
        scratch_shapes=[
            pltpu.VMEM((rows, cols), BF16),
            pltpu.VMEM((rows, cols), BF16),
            pltpu.VMEM((2 * share, rank), F32),
            pltpu.VMEM((cols, rank), BF16),
            pltpu.VMEM((n_dp, 8, 128), F32),
            pltpu.VMEM((2, 8, 128), F32),
            pltpu.VMEM((chips, 8, 128), F32),
            pltpu.VMEM((rows, rank), F32),
            pltpu.VMEM((n_dp - 1, rz, rank), F32),
            pltpu.VMEM((rows, rank), F32),
            pltpu.VMEM((rank, rank), F32),
            pltpu.VMEM((2 * n_dp - 1, gs, rank), F32),
            pltpu.VMEM((chips, gs, rank), F32),
            pltpu.VMEM((rank, rank), F32),
            dma((2,)),
            dma((2,)),
            dma((4, chips // 2)),
            dma((2, n_dp - 1)),
            dma((2,)),
            dma((2, chips - 1)),
            dma((2, n_dp - 1)),
            dma((2, n_dp - 1)),
            dma((2, 2 * n_dp - 1)),
            dma((2, chips - 1)),
            dma((2, 2 * n_dp - 1)),
        ],
        compiler_params=pltpu.CompilerParams(
            collective_id=0, has_side_effects=True, vmem_limit_bytes=VMEM_LIMIT
        ),
    )(momentum, tile_values, exponents, overflow, right_prev)


def inverse_kernel(gram_ref, out_ref, work):
    rank = gram_ref.shape[0]
    work[...] = gram_ref[...]
    lanes = lax.broadcasted_iota(jnp.int32, (8, rank), 1)
    for r in range(0, rank, 8):
        row = [work[r + i:r + i + 1, :] for i in range(8)]
        a = [[jnp.broadcast_to(row[i][:, r + j:r + j + 1], (1, rank)) for j in range(i + 1)] for i in range(8)]
        e = [[None] * 8 for _ in range(8)]
        for j in range(8):
            s = lax.rsqrt(a[j][j])
            s = s * (1.5 - 0.5 * a[j][j] * s * s)
            e[j][j] = s
            for k in range(j):
                e[j][k] = e[j][k] * s
            for i in range(j + 1, 8):
                m = a[i][j] * s
                a[i][j] = m
                for k in range(j + 1):
                    t = m * e[j][k]
                    e[i][k] = -t if e[i][k] is None else e[i][k] - t
            for i in range(j + 1, 8):
                for k in range(j + 1, i + 1):
                    a[i][k] = a[i][k] - a[i][j] * a[k][j]
        upper, mixed = [], []
        lane = lanes[0:1]
        for i in range(8):
            total = e[i][0] * row[0]
            for j in range(1, i + 1):
                total = total + e[i][j] * row[j]
            inv = total
            for j in range(8):
                here = lane == r + j
                inv = jnp.where(here, e[i][j] if j <= i else 0.0, inv)
            upper.append(total)
            mixed.append(jnp.where(lane < r + 8, inv, total))
        upper = jnp.concatenate(upper, axis=0)
        mixed = jnp.concatenate(mixed, axis=0)
        out_ref[r:r + 8, :] = jnp.where(lanes < r + 8, mixed, 0.0)
        n = rank - r - 8
        if n:
            low = lax.dot_general(
                upper[:, r + 8:], mixed, (((0,), (0,)), ((), ())), precision=HIGH, preferred_element_type=F32
            )
            spot = lax.broadcasted_iota(jnp.int32, (n, rank), 1)
            old = jnp.where((spot >= r) & (spot < r + 8), 0.0, work[r + 8:, :])
            work[r + 8:, :] = old - low


def inverse_stage(gram):
    return pl.pallas_call(
        inverse_kernel,
        name="inverse",
        out_shape=jax.ShapeDtypeStruct(gram.shape, F32),
        in_specs=[pl.BlockSpec(memory_space=pltpu.VMEM)],
        out_specs=pl.BlockSpec(memory_space=pltpu.VMEM),
        scratch_shapes=[pltpu.VMEM(gram.shape, F32)],
    )(gram)


def right_kernel(
    n_dp, n_mp,
    mom_hbm, tile_hbm, scale_ref, factor_ref, left_ref, tri_ref,
    ortho_ref, low_ref, inv_ref, share_ref,
    mom, tile, part, part_low, core_in, core_out, plane_in, mine, theirs, low, sq_z, sq_p,
    sem_in, sem_core, sem_plane, sem_pair, sem_gather, sem_sz, sem_sp,
):
    place = Place(n_dp, n_mp)
    rows, cols = mom.shape
    share, rank = share_ref.shape
    block = 2 * share
    loads = [
        pltpu.make_async_copy(mom_hbm, mom, sem_in.at[0]),
        pltpu.make_async_copy(tile_hbm, tile, sem_in.at[1]),
    ]
    for load in loads:
        load.start()
    plane, zline = place.plane_peers(), place.z_peers()
    greet(plane + zline + [place.sibling()])
    ortho = lax.dot_general(
        left_ref[...], tri_ref[...], (((1,), (1,)), ((), ())), precision=HIGH, preferred_element_type=F32
    ).astype(BF16)
    ortho_ref[...] = ortho
    factor = factor_ref[0:1, :]
    for load in loads:
        load.wait()
    step = 256
    for t in range(cols // step):
        at = slice(t * step, (t + 1) * step)
        grad = jnp.concatenate(
            [
                tile[b * BLOCK:(b + 1) * BLOCK, at] * scale_ref[b:b + 1, at].astype(BF16)
                for b in range(rows // BLOCK)
            ],
            axis=0,
        )
        both = (((0,), (0,)), ((), ()))
        mom_part = lax.dot_general(mom[:, at], ortho, both, preferred_element_type=F32)
        grad_part = lax.dot_general(grad, ortho, both, preferred_element_type=F32)
        total = mom_part + factor * grad_part
        part[at, :] = total
        part_low[at, :] = total.astype(BF16)

    def rows_of(chip):
        return pl.ds(pl.multiple_of(chip * block, 16), block)

    core_copies = []
    for i in range(place.half):
        copy = remote(
            part_low.at[rows_of(place.to_chip(i, place.other))], core_in.at[i],
            sem_core.at[0, i], sem_core.at[1, i], place.sibling(),
        )
        copy.start()
        core_copies.append(copy)
    plane_copies = []
    for i in range(place.half):
        chip = place.to_chip(i, place.core)
        copy = remote(
            core_out.at[i], plane_in.at[i], sem_plane.at[0, i], sem_plane.at[1, i], place.dev(place.z, chip, place.core)
        )
        core_copies[i].wait_recv()
        total = part[rows_of(chip)] + core_in[i].astype(F32)
        if i == 0:
            mine[...] = total
        core_out[i] = total.astype(BF16)
        if i == 0:
            pl.when(place.core == 1)(copy.start)
        else:
            copy.start()
        plane_copies.append(copy)

    def first():
        plane_copies[0].wait_recv()
        mine[...] = plane_in[0].astype(F32)

    pl.when(place.core == 1)(first)
    acc = mine[...]
    for i in range(1, place.half):
        plane_copies[i].wait_recv()
        acc = acc + plane_in[i].astype(F32)
    mine[...] = acc
    pair = remote(mine, theirs, sem_pair.at[0], sem_pair.at[1], place.sibling())
    pair.start()
    pair.wait_recv()
    total = mine[...] + theirs[...]
    theirs[...] = total
    low[rows_of(place.chip)] = total.astype(BF16)
    gather_send(place, low, block, sem_gather)
    sq = jnp.sum((total * total).reshape(block // 8, 8, rank), axis=0)
    sq_z[place.z] = sq
    sz = exchange(place, zline, lambda k: sq_z.at[place.z], sq_z, sem_sz, place.z)
    share_ref[...] = theirs[pl.ds(pl.multiple_of(place.core * share, 8), share)]
    for copy in sz:
        copy.wait_recv()
    sq_p[place.chip] = jnp.sum(sq_z[...], axis=0)
    sp = exchange(place, plane, lambda k: sq_p.at[place.chip], sq_p, sem_sp, place.chip)
    for i in range(place.half):
        gather_forward(place, low, block, sem_gather, i)
    for copy in sp:
        copy.wait_recv()
    squares = jnp.sum(jnp.sum(sq_p[...], axis=0), axis=0, keepdims=True)
    inv_ref[...] = jnp.broadcast_to(lax.rsqrt(squares + EPSILON), inv_ref.shape)
    gather_finish(place, low, block, sem_gather)
    low_ref[...] = low[...]
    for copy in core_copies + plane_copies[1:] + [pair] + sz + sp:
        copy.wait_send()
    pl.when(place.core == 1)(plane_copies[0].wait_send)


def right_stage(n_dp, n_mp, share, momentum, tile_values, scale, factor, left, tri):
    rows, cols = momentum.shape
    rank = left.shape[1]
    chips = n_mp // 2
    half = chips // 2
    block = 2 * share
    vmem = pl.BlockSpec(memory_space=pltpu.VMEM)
    hbm = pl.BlockSpec(memory_space=pl.ANY)
    dma = pltpu.SemaphoreType.DMA
    return pl.pallas_call(
        functools.partial(right_kernel, n_dp, n_mp),
        name="right",
        out_shape=(
            jax.ShapeDtypeStruct((rows, rank), BF16),
            jax.ShapeDtypeStruct((cols, rank), BF16),
            jax.ShapeDtypeStruct((8, 128), F32),
            jax.ShapeDtypeStruct((share, rank), F32),
        ),
        in_specs=[hbm, hbm, vmem, vmem, vmem, vmem],
        out_specs=(vmem,) * 4,
        scratch_shapes=[
            pltpu.VMEM((rows, cols), BF16),
            pltpu.VMEM((rows, cols), BF16),
            pltpu.VMEM((cols, rank), F32),
            pltpu.VMEM((cols, rank), BF16),
            pltpu.VMEM((half, block, rank), BF16),
            pltpu.VMEM((half, block, rank), BF16),
            pltpu.VMEM((half, block, rank), BF16),
            pltpu.VMEM((block, rank), F32),
            pltpu.VMEM((block, rank), F32),
            pltpu.VMEM((cols, rank), BF16),
            pltpu.VMEM((n_dp, 8, 128), F32),
            pltpu.VMEM((chips, 8, 128), F32),
            dma((2,)),
            dma((2, half)),
            dma((2, half)),
            dma((2,)),
            dma((4, half)),
            dma((2, n_dp - 1)),
            dma((2, chips - 1)),
        ],
        compiler_params=pltpu.CompilerParams(
            collective_id=1, has_side_effects=True, vmem_limit_bytes=VMEM_LIMIT
        ),
    )(momentum, tile_values, scale, factor, left, tri)


def finish_kernel(unit, mom, tile, scale, factor, ortho, low, inv, share, new, upd, share_out):
    rows = mom.shape[0]
    base = ortho[...]
    both = (((1,), (1,)), ((), ()))
    correction = lax.dot_general(base, low[...], both, preferred_element_type=F32)
    scaled = (base.astype(F32) * inv[0:1, :]).astype(BF16)
    direction = lax.dot_general(scaled, low[...], both, preferred_element_type=F32)
    upd[...] = (unit * direction).astype(BF16)
    f = factor[0, 0]
    for b in range(rows // BLOCK):
        at = slice(b * BLOCK, (b + 1) * BLOCK)
        grad = tile[at, :].astype(F32) * scale[b:b + 1, :]
        new[at, :] = (mom[at, :].astype(F32) + f * grad - (1.0 - RETAIN) * correction[at, :]).astype(BF16)

    @pl.when(pl.program_id(0) == 0)
    def _():
        share_out[...] = share[...]


def finish_stage(unit, momentum, tile_values, scale, factor, ortho, low, inv, share):
    rows, cols = momentum.shape
    rank = ortho.shape[1]
    step = 256
    wide = pl.BlockSpec((rows, step), lambda i: (0, i))

    def whole(a):
        return pl.BlockSpec(a.shape, lambda i: (0, 0))

    return pl.pallas_call(
        functools.partial(finish_kernel, unit),
        name="finish",
        grid=(cols // step,),
        out_shape=(
            jax.ShapeDtypeStruct((rows, cols), BF16),
            jax.ShapeDtypeStruct((rows, cols), BF16),
            jax.ShapeDtypeStruct(share.shape, F32),
        ),
        in_specs=[
            wide, wide,
            pl.BlockSpec((scale.shape[0], step), lambda i: (0, i)),
            pl.BlockSpec(memory_space=pltpu.SMEM),
            whole(ortho),
            pl.BlockSpec((step, rank), lambda i: (i, 0)),
            whole(inv), whole(share),
        ],
        out_specs=(wide, wide, whole(share)),
        compiler_params=pltpu.CompilerParams(vmem_limit_bytes=VMEM_LIMIT),
    )(momentum, tile_values, scale, factor, ortho, low, inv, share)


def body(n_dp, n_mp, momentum, tile_values, exponents, overflow, right_prev):
    rows, cols = momentum.shape
    share, rank = right_prev.shape
    unit = math.sqrt(rows * n_mp * cols * n_dp / rank)
    gram, left, factor, scale = left_stage(n_dp, n_mp, momentum, tile_values, exponents, overflow, right_prev)
    tri = inverse_stage(gram)
    ortho, low, inv, own = right_stage(n_dp, n_mp, share, momentum, tile_values, scale, factor, left, tri)
    new, update, right_out = finish_stage(unit, momentum, tile_values, scale, factor, ortho, low, inv, own)
    return new, right_out, update


def solution(mesh):
    in_specs = (P("mp", "dp"), P("mp", "dp"), P("mp", "dp"), P("mp", "dp"), P(("dp", "mp"), None))
    out_specs = (P("mp", "dp"), P(("dp", "mp"), None), P("mp", "dp"))
    step = functools.partial(body, mesh.shape["dp"], mesh.shape["mp"])
    return jax.shard_map(step, mesh=mesh, in_specs=in_specs, out_specs=out_specs, check_vma=False)
```

```python
import functools
import math

import jax
import jax.numpy as jnp
from jax import lax
from jax.experimental import pallas as pl
from jax.experimental.pallas import tpu as pltpu
from jax.sharding import PartitionSpec as P

MESH = pl.DeviceIdType.MESH
F32 = jnp.float32
BF16 = jnp.bfloat16
HIGH = lax.Precision.HIGHEST
BLOCK = 128
EPSILON = 1e-06
RETAIN = 0.95
VMEM_LIMIT = 32 * 1024 * 1024


class Place:
    def __init__(self, n_dp, n_mp):
        self.nz = n_dp
        self.chips = n_mp // 2
        self.ny = int(round(math.sqrt(self.chips)))
        self.nx = self.chips // self.ny
        self.half = self.chips // 2
        mp = lax.axis_index("mp")
        self.z = lax.axis_index("dp")
        self.core = lax.rem(mp, 2)
        self.other = 1 - self.core
        self.chip = mp // 2
        self.x = self.chip // self.ny
        self.y = lax.rem(self.chip, self.ny)

    def chip_at(self, dx, dy):
        x = lax.rem(self.x + dx + self.nx, self.nx)
        y = lax.rem(self.y + dy + self.ny, self.ny)
        return x * self.ny + y

    def offset(self, i, parity):
        dx = i // (self.ny // 2)
        dy = 2 * (i % (self.ny // 2)) + lax.rem(dx + parity, 2)
        return dx, dy

    def to_chip(self, i, parity):
        dx, dy = self.offset(i, parity)
        return self.chip_at(dx, dy)

    def from_chip(self, i, parity):
        dx, dy = self.offset(i, parity)
        return self.chip_at(-dx, -dy)

    def z_at(self, dz):
        return lax.rem(self.z + dz, self.nz)

    def dev(self, z, chip, core):
        return (z, chip * 2 + core)

    def sibling(self):
        return self.dev(self.z, self.chip, self.other)

    def plane_peers(self):
        return [
            self.dev(self.z, self.chip_at(dx, dy), self.core)
            for dx in range(self.nx)
            for dy in range(self.ny)
            if dx or dy
        ]

    def z_peers(self):
        return [self.dev(self.z_at(dz), self.chip, self.core) for dz in range(1, self.nz)]

    def zc_peers(self):
        return [
            self.dev(self.z_at(dz), self.chip, self.core if dc == 0 else self.other)
            for dz in range(self.nz)
            for dc in range(2)
            if dz or dc
        ]


def remote(src, dst, send, recv, dev):
    return pltpu.make_async_remote_copy(
        src_ref=src, dst_ref=dst, send_sem=send, recv_sem=recv, device_id=dev, device_id_type=MESH
    )


def greet(peers):
    barrier = pltpu.get_barrier_semaphore()
    for dev in peers:
        pl.semaphore_signal(barrier, inc=1, device_id=dev, device_id_type=MESH)
    pl.semaphore_wait(barrier, len(peers))


def exchange(place, peers, src_of, dst, sems, slot):
    copies = [
        remote(src_of(k), dst.at[slot], sems.at[0, k], sems.at[1, k], dev) for k, dev in enumerate(peers)
    ]
    for copy in copies:
        copy.start()
    return copies


def gather_send(place, buf, rows, sems):
    block = buf.at[pl.ds(pl.multiple_of(place.chip * rows, 16), rows)]
    for i in range(place.half):
        copy = remote(
            block, block, sems.at[0, i], sems.at[1, i], place.dev(place.z, place.to_chip(i, place.core), place.core)
        )
        if i == 0:
            pl.when(place.core == 1)(copy.start)
        else:
            copy.start()


def gather_forward(place, buf, rows, sems, i):
    start = pl.multiple_of(place.from_chip(i, place.core) * rows, 16)
    block = buf.at[pl.ds(start, rows)]

    def go():
        remote(block, block, sems.at[0, i], sems.at[1, i], place.sibling()).wait_recv()
        remote(block, block, sems.at[2, i], sems.at[3, i], place.sibling()).start()

    if i == 0:
        pl.when(place.core == 1)(go)
    else:
        go()


def gather_finish(place, buf, rows, sems):
    for i in range(place.half):
        start = pl.multiple_of(place.from_chip(i, place.other) * rows, 16)
        block = buf.at[pl.ds(start, rows)]
        copy = remote(block, block, sems.at[2, i], sems.at[3, i], place.sibling())
        if i == 0:
            pl.when(place.core == 0)(copy.wait_recv)
        else:
            copy.wait_recv()
    for i in range(place.half):
        block = buf.at[pl.ds(0, rows)]
        sent = remote(block, block, sems.at[0, i], sems.at[1, i], place.sibling())
        passed = remote(block, block, sems.at[2, i], sems.at[3, i], place.sibling())

        def done(sent=sent, passed=passed):
            sent.wait_send()
            passed.wait_send()

        if i == 0:
            pl.when(place.core == 1)(done)
        else:
            done()


def invert(work, out_ref):
    rank = work.shape[0]
    lanes = lax.broadcasted_iota(jnp.int32, (8, rank), 1)
    for r in range(0, rank, 8):
        row = [work[r + i:r + i + 1, :] for i in range(8)]
        a = [[jnp.broadcast_to(row[i][:, r + j:r + j + 1], (1, rank)) for j in range(i + 1)] for i in range(8)]
        e = [[None] * 8 for _ in range(8)]
        for j in range(8):
            s = lax.rsqrt(a[j][j])
            s = s * (1.5 - 0.5 * a[j][j] * s * s)
            e[j][j] = s
            for k in range(j):
                e[j][k] = e[j][k] * s
            for i in range(j + 1, 8):
                m = a[i][j] * s
                a[i][j] = m
                for k in range(j + 1):
                    t = m * e[j][k]
                    e[i][k] = -t if e[i][k] is None else e[i][k] - t
            for i in range(j + 1, 8):
                for k in range(j + 1, i + 1):
                    a[i][k] = a[i][k] - a[i][j] * a[k][j]
        upper, mixed = [], []
        lane = lanes[0:1]
        for i in range(8):
            total = e[i][0] * row[0]
            for j in range(1, i + 1):
                total = total + e[i][j] * row[j]
            inv = total
            for j in range(8):
                here = lane == r + j
                inv = jnp.where(here, e[i][j] if j <= i else 0.0, inv)
            upper.append(total)
            mixed.append(jnp.where(lane < r + 8, inv, total))
        upper = jnp.concatenate(upper, axis=0)
        mixed = jnp.concatenate(mixed, axis=0)
        out_ref[r:r + 8, :] = jnp.where(lanes < r + 8, mixed, 0.0)
        n = rank - r - 8
        if n:
            low = lax.dot_general(
                upper[:, r + 8:], mixed, (((0,), (0,)), ((), ())), precision=HIGH, preferred_element_type=F32
            )
            spot = lax.broadcasted_iota(jnp.int32, (n, rank), 1)
            old = jnp.where((spot >= r) & (spot < r + 8), 0.0, work[r + 8:, :])
            work[r + 8:, :] = old - low


def mega_kernel(
    n_dp, n_mp,
    mom_hbm, tile_hbm, exps_hbm, prev_hbm, over_ref,
    ortho_ref, low_ref, inv_ref, share_ref, sum_ref,
    mom, tile, exps, pair, right, mom_t, grad_t, flag_z, flag_c, flag_p,
    part, left_in, left, gram, gram_zc, gram_p, gram_all, work, tri,
    full, full_low, core_in, core_out, plane_in, mine, theirs, sq_z, sq_p,
    sem_in, sem_pair, sem_gather, sem_fz, sem_fc, sem_fp, sem_lr, sem_lg, sem_gr, sem_gp, sem_gg,
    sem_core, sem_plane, sem_sum, sem_low, sem_sz, sem_sp,
):
    place = Place(n_dp, n_mp)
    rows, cols = mom.shape
    share, rank = share_ref.shape
    block = 2 * share
    my_share = pl.ds(pl.multiple_of(place.core * share, 8), share)
    loads = [
        pltpu.make_async_copy(src, dst, sem_in.at[k])
        for k, (src, dst) in enumerate(
            [(prev_hbm, pair.at[my_share]), (exps_hbm, exps), (mom_hbm, mom), (tile_hbm, tile)]
        )
    ]
    for load in loads:
        load.start()
    plane, zline, zc = place.plane_peers(), place.z_peers(), place.zc_peers()
    greet(plane + zc)

    loads[0].wait()
    pair_copy = remote(pair.at[my_share], pair.at[my_share], sem_pair.at[0], sem_pair.at[1], place.sibling())
    pair_copy.start()
    kept = jnp.where(over_ref[0, 0] == 0, 1.0, 0.0).astype(F32)
    flag_z[place.z] = jnp.full((8, 128), kept, F32)
    fz = exchange(place, zline, lambda k: flag_z.at[place.z], flag_z, sem_fz, place.z)
    pair_copy.wait_recv()
    pending = [pair_copy] + fz
    right[pl.ds(pl.multiple_of(place.chip * block, 16), block)] = pair[...].astype(BF16)
    gather_send(place, right, block, sem_gather)

    loads[1].wait()
    scales = jnp.exp2(exps[...].astype(F32)).astype(BF16).astype(F32) * kept
    loads[2].wait()
    loads[3].wait()
    for j in range(cols // BLOCK):
        at = slice(j * BLOCK, (j + 1) * BLOCK)
        for b in range(rows // BLOCK):
            scale = jnp.broadcast_to(scales[b:b + 1, j:j + 1], (1, BLOCK)).astype(BF16)
            tile[b * BLOCK:(b + 1) * BLOCK, at] = tile[b * BLOCK:(b + 1) * BLOCK, at] * scale

    for copy in fz:
        copy.wait_recv()
    flag_c[place.core] = jnp.sum(flag_z[...], axis=0)
    fc = remote(flag_c.at[place.core], flag_c.at[place.core], sem_fc.at[0], sem_fc.at[1], place.sibling())
    fc.start()
    for i in range(place.half // 2):
        gather_forward(place, right, block, sem_gather, i)
    fc.wait_recv()
    flag_p[place.chip] = flag_c[0] + flag_c[1]
    fp = exchange(place, plane, lambda k: flag_p.at[place.chip], flag_p, sem_fp, place.chip)
    for i in range(place.half // 2, place.half):
        gather_forward(place, right, block, sem_gather, i)
    gather_finish(place, right, block, sem_gather)
    for copy in fp:
        copy.wait_recv()
    healthy = jnp.sum(flag_p[...], axis=0)
    factor = (float(n_dp * n_mp) / jnp.maximum(healthy, 1.0))[0:1, :]
    pending += [fc] + fp

    mom_part = jnp.dot(mom[...], right[...], preferred_element_type=F32)
    grad_part = jnp.dot(tile[...], right[...], preferred_element_type=F32)
    part[...] = mom_part + factor * grad_part

    rz = rows // place.nz
    lr = []
    for dz in range(1, place.nz):
        z2 = place.z_at(dz)
        copy = remote(
            part.at[pl.ds(pl.multiple_of(z2 * rz, 8), rz)], left_in.at[dz - 1],
            sem_lr.at[0, dz - 1], sem_lr.at[1, dz - 1], place.dev(z2, place.chip, place.core),
        )
        copy.start()
        lr.append(copy)
    for j in range(cols // BLOCK):
        at = slice(j * BLOCK, (j + 1) * BLOCK)
        mom_t[at, :] = mom[:, at].T
        grad_t[at, :] = tile[:, at].T
    for b in range(0, rows, 16):
        at = slice(b, b + 16)
        wide = jnp.broadcast_to(factor[:, 0:1], (1, cols))
        sum_ref[at, :] = mom[at, :].astype(F32) + wide * tile[at, :].astype(F32)
    own = pl.ds(pl.multiple_of(place.z * rz, 8), rz)
    acc = part[own]
    for k, copy in enumerate(lr):
        copy.wait_recv()
        acc = acc + left_in[k]
    left[own] = acc
    pending += lr
    gram[...] = lax.dot_general(acc, acc, (((0,), (0,)), ((), ())), precision=HIGH, preferred_element_type=F32)

    gs = gram.shape[0] // (2 * place.nz)
    gr = []
    k = 0
    for dz in range(place.nz):
        for dc in range(2):
            if dz or dc:
                z2, c2 = place.z_at(dz), place.core if dc == 0 else place.other
                copy = remote(
                    gram.at[pl.ds(pl.multiple_of((z2 * 2 + c2) * gs, 8), gs)], gram_zc.at[k],
                    sem_gr.at[0, k], sem_gr.at[1, k], place.dev(z2, place.chip, c2),
                )
                copy.start()
                gr.append(copy)
                k += 1
    piece = pl.ds(pl.multiple_of((place.z * 2 + place.core) * gs, 8), gs)
    acc = gram[piece]
    for k, copy in enumerate(gr):
        copy.wait_recv()
        acc = acc + gram_zc[k]
    gram_p[place.chip] = acc
    pending += gr
    gp = exchange(place, plane, lambda k: gram_p.at[place.chip], gram_p, sem_gp, place.chip)
    for copy in gp:
        copy.wait_recv()
    gram_all[piece] = jnp.sum(gram_p[...], axis=0)
    pending += gp
    gg = [
        remote(gram_all.at[piece], gram_all.at[piece], sem_gg.at[0, k], sem_gg.at[1, k], dev)
        for k, dev in enumerate(zc)
    ]
    for copy in gg:
        copy.start()
    lg = [
        remote(left.at[own], left.at[own], sem_lg.at[0, k], sem_lg.at[1, k], dev) for k, dev in enumerate(zline)
    ]
    for copy in lg:
        copy.start()
    for copy in gg:
        copy.wait_recv()
    pending += gg
    work[...] = gram_all[...]
    invert(work, tri)
    for copy in lg:
        copy.wait_recv()
    pending += lg

    ortho = lax.dot_general(
        left[...], tri[...], (((1,), (1,)), ((), ())), precision=HIGH, preferred_element_type=F32
    ).astype(BF16)
    ortho_ref[...] = ortho
    step = 256
    for t in range(cols // step):
        at = slice(t * step, (t + 1) * step)
        total = jnp.dot(mom_t[at, :], ortho, preferred_element_type=F32) + factor * jnp.dot(
            grad_t[at, :], ortho, preferred_element_type=F32
        )
        full[at, :] = total
        full_low[at, :] = total.astype(BF16)

    def rows_of(chip):
        return pl.ds(pl.multiple_of(chip * block, 16), block)

    core_copies = []
    for i in range(place.half):
        copy = remote(
            full_low.at[rows_of(place.to_chip(i, place.other))], core_in.at[i],
            sem_core.at[0, i], sem_core.at[1, i], place.sibling(),
        )
        copy.start()
        core_copies.append(copy)
    plane_copies = []
    for i in range(place.half):
        chip = place.to_chip(i, place.core)
        copy = remote(
            core_out.at[i], plane_in.at[i], sem_plane.at[0, i], sem_plane.at[1, i], place.dev(place.z, chip, place.core)
        )
        core_copies[i].wait_recv()
        total = full[rows_of(chip)] + core_in[i].astype(F32)
        if i == 0:
            mine[...] = total
        core_out[i] = total.astype(BF16)
        if i == 0:
            pl.when(place.core == 1)(copy.start)
        else:
            copy.start()
        plane_copies.append(copy)

    def first():
        plane_copies[0].wait_recv()
        mine[...] = plane_in[0].astype(F32)

    pl.when(place.core == 1)(first)
    acc = mine[...]
    for i in range(1, place.half):
        plane_copies[i].wait_recv()
        acc = acc + plane_in[i].astype(F32)
    mine[...] = acc
    pending += core_copies + plane_copies[1:]
    pl.when(place.core == 1)(plane_copies[0].wait_send)
    pair_sum = remote(mine, theirs, sem_sum.at[0], sem_sum.at[1], place.sibling())
    pair_sum.start()
    pair_sum.wait_recv()
    total = mine[...] + theirs[...]
    theirs[...] = total
    pending += [pair_sum]
    low_ref[rows_of(place.chip)] = total.astype(BF16)
    gather_send(place, low_ref, block, sem_low)
    sq = jnp.sum((total * total).reshape(block // 8, 8, rank), axis=0)
    sq_z[place.z] = sq
    sz = exchange(place, zline, lambda k: sq_z.at[place.z], sq_z, sem_sz, place.z)
    share_ref[...] = theirs[my_share]
    for copy in sz:
        copy.wait_recv()
    sq_p[place.chip] = jnp.sum(sq_z[...], axis=0)
    sp = exchange(place, plane, lambda k: sq_p.at[place.chip], sq_p, sem_sp, place.chip)
    for i in range(place.half):
        gather_forward(place, low_ref, block, sem_low, i)
    gather_finish(place, low_ref, block, sem_low)
    for copy in sp:
        copy.wait_recv()
    squares = jnp.sum(jnp.sum(sq_p[...], axis=0), axis=0, keepdims=True)
    inv_ref[...] = jnp.broadcast_to(lax.rsqrt(squares + EPSILON), inv_ref.shape)
    for copy in pending + sz + sp:
        copy.wait_send()


def mega_stage(n_dp, n_mp, momentum, tile_values, exponents, right_prev, overflow):
    rows, cols = momentum.shape
    share, rank = right_prev.shape
    chips = n_mp // 2
    half = chips // 2
    block = 2 * share
    rz = rows // n_dp
    gs = rank // (2 * n_dp)
    vmem = pl.BlockSpec(memory_space=pltpu.VMEM)
    hbm = pl.BlockSpec(memory_space=pltpu.HBM)
    dma = pltpu.SemaphoreType.DMA
    return pl.pallas_call(
        functools.partial(mega_kernel, n_dp, n_mp),
        name="mega",
        out_shape=(
            jax.ShapeDtypeStruct((rows, rank), BF16),
            jax.ShapeDtypeStruct((cols, rank), BF16),
            jax.ShapeDtypeStruct((8, 128), F32),
            jax.ShapeDtypeStruct((share, rank), F32),
            jax.ShapeDtypeStruct((rows, cols), F32),
        ),
        in_specs=[hbm] * 4 + [pl.BlockSpec(memory_space=pltpu.SMEM)],
        out_specs=(vmem,) * 5,
        scratch_shapes=[
            pltpu.VMEM((rows, cols), BF16),
            pltpu.VMEM((rows, cols), BF16),
            pltpu.VMEM(exponents.shape, jnp.int32),
            pltpu.VMEM((block, rank), F32),
            pltpu.VMEM((cols, rank), BF16),
            pltpu.VMEM((cols, rows), BF16),
            pltpu.VMEM((cols, rows), BF16),
            pltpu.VMEM((n_dp, 8, 128), F32),
            pltpu.VMEM((2, 8, 128), F32),
            pltpu.VMEM((chips, 8, 128), F32),
            pltpu.VMEM((rows, rank), F32),
            pltpu.VMEM((n_dp - 1, rz, rank), F32),
            pltpu.VMEM((rows, rank), F32),
            pltpu.VMEM((rank, rank), F32),
            pltpu.VMEM((2 * n_dp - 1, gs, rank), F32),
            pltpu.VMEM((chips, gs, rank), F32),
            pltpu.VMEM((rank, rank), F32),
            pltpu.VMEM((rank, rank), F32),
            pltpu.VMEM((rank, rank), F32),
            pltpu.VMEM((cols, rank), F32),
            pltpu.VMEM((cols, rank), BF16),
            pltpu.VMEM((half, block, rank), BF16),
            pltpu.VMEM((half, block, rank), BF16),
            pltpu.VMEM((half, block, rank), BF16),
            pltpu.VMEM((block, rank), F32),
            pltpu.VMEM((block, rank), F32),
            pltpu.VMEM((n_dp, 8, 128), F32),
            pltpu.VMEM((chips, 8, 128), F32),
            dma((4,)),
            dma((2,)),
            dma((4, half)),
            dma((2, n_dp - 1)),
            dma((2,)),
            dma((2, chips - 1)),
            dma((2, n_dp - 1)),
            dma((2, n_dp - 1)),
            dma((2, 2 * n_dp - 1)),
            dma((2, chips - 1)),
            dma((2, 2 * n_dp - 1)),
            dma((2, half)),
            dma((2, half)),
            dma((2,)),
            dma((4, half)),
            dma((2, n_dp - 1)),
            dma((2, chips - 1)),
        ],
        compiler_params=pltpu.CompilerParams(
            collective_id=0, has_side_effects=True, vmem_limit_bytes=VMEM_LIMIT
        ),
    )(momentum, tile_values, exponents, right_prev, overflow)


def finish_kernel(unit, sums, ortho, low, inv, share, new, upd, share_out, new_v, upd_v, sem):
    rows, cols = sums.shape
    step = 256
    base = ortho[...]
    scaled = (base.astype(F32) * inv[0:1, :]).astype(BF16)
    both = (((1,), (1,)), ((), ()))
    share_copy = pltpu.make_async_copy(share, share_out, sem.at[2, 0])
    share_copy.start()
    copies = [share_copy]
    for t in range(cols // step):
        at = slice(t * step, (t + 1) * step)
        piece = low[at, :]
        correction = lax.dot_general(base, piece, both, preferred_element_type=F32)
        new_v[:, at] = (sums[:, at] - (1.0 - RETAIN) * correction).astype(BF16)
        direction = lax.dot_general(scaled, piece, both, preferred_element_type=F32)
        upd_v[:, at] = (unit * direction).astype(BF16)
        for k, (src, dst) in enumerate([(new_v, new), (upd_v, upd)]):
            copy = pltpu.make_async_copy(src.at[:, at], dst.at[:, at], sem.at[k, t])
            copy.start()
            copies.append(copy)
    for copy in copies:
        copy.wait()


def finish_stage(unit, sums, ortho, low, inv, share):
    rows, cols = sums.shape
    vmem = pl.BlockSpec(memory_space=pltpu.VMEM)
    hbm = pl.BlockSpec(memory_space=pltpu.HBM)
    return pl.pallas_call(
        functools.partial(finish_kernel, unit),
        name="finish",
        out_shape=(
            jax.ShapeDtypeStruct((rows, cols), BF16),
            jax.ShapeDtypeStruct((rows, cols), BF16),
            jax.ShapeDtypeStruct(share.shape, F32),
        ),
        in_specs=[vmem] * 5,
        out_specs=(hbm,) * 3,
        scratch_shapes=[
            pltpu.VMEM((rows, cols), BF16),
            pltpu.VMEM((rows, cols), BF16),
            pltpu.SemaphoreType.DMA((3, cols // 256)),
        ],
        compiler_params=pltpu.CompilerParams(vmem_limit_bytes=VMEM_LIMIT),
    )(sums, ortho, low, inv, share)


def body(n_dp, n_mp, momentum, tile_values, exponents, overflow, right_prev):
    rows, cols = momentum.shape
    rank = right_prev.shape[1]
    unit = math.sqrt(rows * n_mp * cols * n_dp / rank)
    args = [
        pltpu.with_memory_space_constraint(a, pltpu.HBM)
        for a in (momentum, tile_values, exponents, right_prev)
    ]
    ortho, low, inv, own, sums = mega_stage(n_dp, n_mp, *args, overflow)
    new, update, right_out = finish_stage(unit, sums, ortho, low, inv, own)
    return new, right_out, update


def solution(mesh):
    in_specs = (P("mp", "dp"), P("mp", "dp"), P("mp", "dp"), P("mp", "dp"), P(("dp", "mp"), None))
    out_specs = (P("mp", "dp"), P(("dp", "mp"), None), P("mp", "dp"))
    step = functools.partial(body, mesh.shape["dp"], mesh.shape["mp"])
    return jax.shard_map(step, mesh=mesh, in_specs=in_specs, out_specs=out_specs, check_vma=False)
```

```python
import functools
import math

import jax
import jax.numpy as jnp
from jax import lax
from jax.experimental import pallas as pl
from jax.experimental.pallas import tpu as pltpu
from jax.sharding import PartitionSpec as P

MESH = pl.DeviceIdType.MESH
F32 = jnp.float32
BF16 = jnp.bfloat16
HIGH = lax.Precision.HIGHEST
BLOCK = 128
EPSILON = 1e-06
RETAIN = 0.95
VMEM_LIMIT = 32 * 1024 * 1024


def torus(a, n):
    return min(a % n, -a % n)


class Place:
    def __init__(self, n_dp, n_mp):
        self.nz = n_dp
        self.chips = n_mp // 2
        self.ny = int(round(math.sqrt(self.chips)))
        self.nx = self.chips // self.ny
        self.half = self.chips // 2
        mp = lax.axis_index("mp")
        self.z = lax.axis_index("dp")
        self.core = lax.rem(mp, 2)
        self.other = 1 - self.core
        self.chip = mp // 2
        x = self.chip // self.ny
        y = lax.rem(self.chip, self.ny)
        xs = [lax.rem(x + d, self.nx) * self.ny for d in range(self.nx)]
        ys = [lax.rem(y + d, self.ny) for d in range(self.ny)]
        offsets = sorted(
            ((dx, dy) for dx in range(self.nx) for dy in range(self.ny)),
            key=lambda o: -torus(o[0], self.nx) - torus(o[1], self.ny),
        )
        chips = {o: xs[o[0]] + ys[o[1]] for o in offsets}
        split = [[o for o in offsets if sum(o) % 2 == parity] for parity in range(2)]

        def pick(parity, sign):
            return [
                jnp.where(parity == 0, *(chips[(sign * o[0]) % self.nx, (sign * o[1]) % self.ny] for o in pair))
                for pair in zip(*split)
            ]

        self.sibling = (self.z, self.chip * 2 + self.other)
        self.to_mine, self.from_mine = pick(self.core, 1), pick(self.core, -1)
        self.to_other, self.from_other = pick(self.other, 1), pick(self.other, -1)
        self.plane = [chips[o] for o in offsets[:-1]]
        self.plane_peers = [(self.z, chip * 2 + self.core) for chip in self.plane]
        self.z_order = sorted(range(1, self.nz), key=lambda d: -torus(d, self.nz))
        self.zs = [lax.rem(self.z + d, self.nz) for d in self.z_order]
        self.z_peers = [(z, self.chip * 2 + self.core) for z in self.zs]
        self.zc_peers = [
            (z, self.chip * 2 + core) for z in self.zs for core in (self.core, self.other)
        ] + [self.sibling]

    def same_core(self, chip):
        return (self.z, chip * 2 + self.core)


def remote(src, dst, send, recv, dev):
    return pltpu.make_async_remote_copy(
        src_ref=src, dst_ref=dst, send_sem=send, recv_sem=recv, device_id=dev, device_id_type=MESH
    )


def exchange(peers, src_of, dst, sems):
    copies = [remote(src_of(k), dst, sems.at[0, k], sems.at[1, k], dev) for k, dev in enumerate(peers)]
    for copy in copies:
        copy.start()
    return copies


def start_all(copies, place):
    for copy in copies[:-1]:
        copy.start()
    pl.when(place.core == 1)(copies[-1].start)


class Gather:
    def __init__(self, place, buf, rows, sems):
        self.place = place

        def at(chip):
            return buf.at[pl.ds(pl.multiple_of(chip * rows, 16), rows)]

        mine = at(place.chip)
        self.sends = [
            remote(mine, mine, sems.at[0, i], sems.at[1, i], place.same_core(chip))
            for i, chip in enumerate(place.to_mine)
        ]
        self.arrivals = [
            remote(at(chip), at(chip), sems.at[0, i], sems.at[1, i], place.sibling)
            for i, chip in enumerate(place.from_mine)
        ]
        self.passes = [
            remote(at(chip), at(chip), sems.at[2, i], sems.at[3, i], place.sibling)
            for i, chip in enumerate(place.from_mine)
        ]
        self.passed = [
            remote(at(chip), at(chip), sems.at[2, i], sems.at[3, i], place.sibling)
            for i, chip in enumerate(place.from_other)
        ]

    def send(self):
        start_all(self.sends, self.place)

    def forward(self, i):
        def go():
            self.arrivals[i].wait_recv()
            self.passes[i].start()

        if i == self.place.half - 1:
            pl.when(self.place.core == 1)(go)
        else:
            go()

    def finish(self):
        for copy in self.passed[:-1]:
            copy.wait_recv()
        pl.when(self.place.core == 0)(self.passed[-1].wait_recv)

    def drain(self):
        for sent, passed in list(zip(self.sends, self.passes))[:-1]:
            sent.wait_send()
            passed.wait_send()

        def last():
            self.sends[-1].wait_send()
            self.passes[-1].wait_send()

        pl.when(self.place.core == 1)(last)


def invert(work, out_ref):
    rank = work.shape[0]
    size = 8
    lanes = lax.broadcasted_iota(jnp.int32, (size, rank), 1)
    lane = lanes[0:1]
    for r in range(0, rank, size):
        row = [work[r + i:r + i + 1, :] for i in range(size)]
        a = [[jnp.broadcast_to(row[i][:, r + j:r + j + 1], (1, rank)) for j in range(i + 1)] for i in range(size)]
        inside = (lane >= r) & (lane < r + size)
        row = [jnp.where(inside, jnp.where(lane == r + i, 1.0, 0.0), row[i]) for i in range(size)]
        e = [[None] * size for _ in range(size)]
        pivot, recip = [], []
        for j in range(size):
            pivot.append(a[j][j])
            recip.append(1.0 / a[j][j])
            for i in range(j + 1, size):
                m = a[i][j] * recip[j]
                for k in range(j + 1, i + 1):
                    a[i][k] = a[i][k] - m * a[k][j]
                for k in range(j):
                    e[i][k] = e[i][k] - m * e[j][k]
                e[i][j] = -m
        z = []
        for i in range(size):
            t = row[i]
            for j in range(i):
                t = t + e[i][j] * row[j]
            z.append(t)
        y = []
        zq = [z[i] * recip[i] for i in range(size)]
        for i in range(size):
            t = zq[i]
            for k in range(i + 1, size):
                t = t + e[k][i] * zq[k]
            y.append(t)
        out = jnp.concatenate([z[i] * lax.rsqrt(pivot[i]) for i in range(size)], axis=0)
        out_ref[r:r + size, :] = jnp.where(lanes < r + size, out, 0.0)
        for s in range(r + size, rank, size):
            old = work[s:s + size, :]
            acc = jnp.where((lanes >= r) & (lanes < r + size), 0.0, old)
            for k in range(size):
                acc = acc - jnp.broadcast_to(old[:, r + k:r + k + 1], (size, rank)) * y[k]
            work[s:s + size, :] = acc


def mega_kernel(
    n_dp, n_mp,
    mom_hbm, tile_hbm, exps_hbm, prev_hbm, over_ref,
    ortho_ref, low_ref, inv_ref, share_ref, sum_ref,
    both, exps, scale, pair, right, mom_t, grad_t, flag_z, flag_c, flag_p,
    part, left_in, left, gram, gram_p, gram_zc, gram_all, work, tri,
    core_send, core_in, core_out, plane_in, mine, theirs, sq_z, sq_p,
    sem_in, sem_pair, sem_gather, sem_fz, sem_fc, sem_fp, sem_lr, sem_lg, sem_gp, sem_gz, sem_gg,
    sem_core, sem_plane, sem_sum, sem_low, sem_sz, sem_sp,
):
    place = Place(n_dp, n_mp)
    rows, cols = mom_hbm.shape
    share, rank = share_ref.shape
    block = 2 * share
    my_share = pl.ds(pl.multiple_of(place.core * share, 8), share)
    loads = [
        pltpu.make_async_copy(src, dst, sem_in.at[k])
        for k, (src, dst) in enumerate(
            [
                (prev_hbm, pair.at[my_share]), (exps_hbm, exps),
                (mom_hbm, both.at[0:rows]), (tile_hbm, both.at[rows:2 * rows]),
            ]
        )
    ]
    for load in loads:
        load.start()
    barrier = pltpu.get_barrier_semaphore()
    friends = place.plane_peers + place.zc_peers
    for dev in friends:
        pl.semaphore_signal(barrier, inc=1, device_id=dev, device_id_type=MESH)
    kept = jnp.where(over_ref[0, 0] == 0, 1.0, 0.0).astype(F32)
    flag_z[place.z] = jnp.full((8, 128), kept, F32)
    loads[1].wait()
    scales = jnp.exp2(exps[...].astype(F32)).astype(BF16).astype(F32) * kept
    for j in range(cols // BLOCK):
        for b in range(rows // BLOCK):
            scale[b, :, j * BLOCK:(j + 1) * BLOCK] = jnp.broadcast_to(scales[b:b + 1, j:j + 1], (16, BLOCK)).astype(BF16)
    loads[0].wait()
    pl.semaphore_wait(barrier, len(friends))
    pending = []

    fz = exchange(place.z_peers, lambda k: flag_z.at[place.z], flag_z.at[place.z], sem_fz)
    pair_copy = remote(pair.at[my_share], pair.at[my_share], sem_pair.at[0], sem_pair.at[1], place.sibling)
    pair_copy.start()
    pair_copy.wait_recv()
    right[pl.ds(pl.multiple_of(place.chip * block, 16), block)] = pair[...].astype(BF16)
    gather = Gather(place, right, block, sem_gather)
    gather.send()

    loads[2].wait()
    loads[3].wait()

    def decode(j, carry):
        at = pl.ds(pl.multiple_of(j * BLOCK, BLOCK), BLOCK)
        for b in range(rows // BLOCK):
            factor_of = scale[b, :, at]
            for r in range(rows + b * BLOCK, rows + (b + 1) * BLOCK, 16):
                both[r:r + 16, at] = both[r:r + 16, at] * factor_of
        return carry

    lax.fori_loop(0, cols // BLOCK, decode, 0)

    for copy in fz:
        copy.wait_recv()
    flag_c[place.core] = jnp.sum(flag_z[...], axis=0)
    fc = remote(flag_c.at[place.core], flag_c.at[place.core], sem_fc.at[0], sem_fc.at[1], place.sibling)
    fc.start()
    fc.wait_recv()
    flag_p[place.chip] = flag_c[0] + flag_c[1]
    fp = exchange(place.plane_peers, lambda k: flag_p.at[place.chip], flag_p.at[place.chip], sem_fp)
    for i in range(place.half):
        gather.forward(i)
    gather.finish()
    for copy in fp:
        copy.wait_recv()
    healthy = jnp.sum(flag_p[...], axis=0)
    factor = (float(n_dp * n_mp) / jnp.maximum(healthy, 1.0))[0:1, :]
    pending += [pair_copy, fc] + fz + fp

    parts = jnp.dot(both[...], right[...], preferred_element_type=F32)
    part[...] = parts[:rows] + factor * parts[rows:]

    rz = rows // place.nz
    lr = []
    for k, z in enumerate(place.zs):
        copy = remote(
            part.at[pl.ds(pl.multiple_of(z * rz, 8), rz)], left_in.at[k], sem_lr.at[0, k], sem_lr.at[1, k],
            place.z_peers[k],
        )
        copy.start()
        lr.append(copy)

    def transpose(j, carry):
        at = pl.ds(pl.multiple_of(j * BLOCK, BLOCK), BLOCK)
        mom_t[at, :] = both[0:rows, at].T
        grad_t[at, :] = both[rows:2 * rows, at].T
        return carry

    lax.fori_loop(0, cols // BLOCK, transpose, 0)
    wide = jnp.broadcast_to(factor[:, 0:1], (16, BLOCK))

    def add(j, carry):
        at = pl.ds(pl.multiple_of(j * BLOCK, BLOCK), BLOCK)
        for r in range(0, rows, 16):
            sum_ref[r:r + 16, at] = both[r:r + 16, at].astype(F32) + wide * both[rows + r:rows + r + 16, at].astype(F32)
        return carry

    own = pl.ds(pl.multiple_of(place.z * rz, 8), rz)
    acc = part[own]
    for k, copy in enumerate(lr):
        copy.wait_recv()
        acc = acc + left_in[k]
    left[own] = acc
    pending += lr
    gram[...] = lax.dot_general(acc, acc, (((0,), (0,)), ((), ())), precision=HIGH, preferred_element_type=F32)

    gs = rank // place.chips
    piece = pl.ds(pl.multiple_of(place.chip * gs, 8), gs)
    gp = []
    for k, chip in enumerate(place.plane):
        copy = remote(
            gram.at[pl.ds(pl.multiple_of(chip * gs, 8), gs)], gram_p.at[k], sem_gp.at[0, k], sem_gp.at[1, k],
            place.plane_peers[k],
        )
        copy.start()
        gp.append(copy)
    acc = gram[piece]
    lax.fori_loop(0, cols // BLOCK, add, 0)
    for k, copy in enumerate(gp):
        copy.wait_recv()
        acc = acc + gram_p[k]
    pending += gp
    spot = place.z * 2 + place.core
    gram_zc[spot] = acc
    gz = exchange(place.zc_peers, lambda k: gram_zc.at[spot], gram_zc.at[spot], sem_gz)
    for copy in gz:
        copy.wait_recv()
    gram_all[piece] = jnp.sum(gram_zc[...], axis=0)
    pending += gz
    gg = exchange(place.plane_peers, lambda k: gram_all.at[piece], gram_all.at[piece], sem_gg)
    lg = exchange(place.z_peers, lambda k: left.at[own], left.at[own], sem_lg)
    for copy in gg:
        copy.wait_recv()
    pending += gg + lg
    work[...] = gram_all[...]
    invert(work, tri)
    for copy in lg:
        copy.wait_recv()

    ortho = lax.dot_general(
        left[...], tri[...], (((1,), (1,)), ((), ())), precision=HIGH, preferred_element_type=F32
    ).astype(BF16)
    ortho_ref[...] = ortho

    def rows_of(chip):
        return pl.ds(pl.multiple_of(chip * block, 16), block)

    def right_part(chip):
        at = rows_of(chip)
        return jnp.dot(mom_t[at, :], ortho, preferred_element_type=F32) + factor * jnp.dot(
            grad_t[at, :], ortho, preferred_element_type=F32
        )

    core_copies = []
    for i, chip in enumerate(place.to_other):
        core_send[i] = right_part(chip).astype(BF16)
        copy = remote(core_send.at[i], core_in.at[i], sem_core.at[0, i], sem_core.at[1, i], place.sibling)
        copy.start()
        core_copies.append(copy)
    plane_copies = []
    last = place.half - 1
    for i, chip in enumerate(place.to_mine):
        total = right_part(chip)
        core_copies[i].wait_recv()
        total = total + core_in[i].astype(F32)
        if i == last:
            mine[...] = total
        core_out[i] = total.astype(BF16)
        copy = remote(
            core_out.at[i], plane_in.at[i], sem_plane.at[0, i], sem_plane.at[1, i], place.same_core(chip)
        )
        if i == last:
            pl.when(place.core == 1)(copy.start)
        else:
            copy.start()
        plane_copies.append(copy)
    pending += core_copies + plane_copies[:-1]
    acc = None
    for i in range(last):
        plane_copies[i].wait_recv()
        got = plane_in[i].astype(F32)
        acc = got if acc is None else acc + got

    def own_last():
        mine[...] = mine[...] + acc

    def got_last():
        plane_copies[last].wait_recv()
        mine[...] = plane_in[last].astype(F32) + acc

    pl.when(place.core == 0)(own_last)
    pl.when(place.core == 1)(got_last)
    pair_sum = remote(mine, theirs, sem_sum.at[0], sem_sum.at[1], place.sibling)
    pair_sum.start()
    pair_sum.wait_recv()
    total = mine[...] + theirs[...]
    pending += [pair_sum]
    sq_z[place.z] = jnp.sum((total * total).reshape(block // 8, 8, rank), axis=0)
    sz = exchange(place.z_peers, lambda k: sq_z.at[place.z], sq_z.at[place.z], sem_sz)
    low_ref[rows_of(place.chip)] = total.astype(BF16)
    last_gather = Gather(place, low_ref, block, sem_low)
    last_gather.send()
    theirs[...] = total
    share_ref[...] = theirs[my_share]
    for copy in sz:
        copy.wait_recv()
    sq_p[place.chip] = jnp.sum(sq_z[...], axis=0)
    sp = exchange(place.plane_peers, lambda k: sq_p.at[place.chip], sq_p.at[place.chip], sem_sp)
    for i in range(place.half):
        last_gather.forward(i)
    last_gather.finish()
    for copy in sp:
        copy.wait_recv()
    squares = jnp.sum(jnp.sum(sq_p[...], axis=0), axis=0, keepdims=True)
    inv_ref[...] = jnp.broadcast_to(lax.rsqrt(squares + EPSILON), inv_ref.shape)
    for copy in pending + sz + sp:
        copy.wait_send()
    pl.when(place.core == 1)(plane_copies[last].wait_send)
    gather.drain()
    last_gather.drain()


def mega_stage(n_dp, n_mp, momentum, tile_values, exponents, right_prev, overflow):
    rows, cols = momentum.shape
    share, rank = right_prev.shape
    chips = n_mp // 2
    half = chips // 2
    block = 2 * share
    vmem = pl.BlockSpec(memory_space=pltpu.VMEM)
    hbm = pl.BlockSpec(memory_space=pltpu.HBM)
    dma = pltpu.SemaphoreType.DMA
    return pl.pallas_call(
        functools.partial(mega_kernel, n_dp, n_mp),
        name="mega",
        out_shape=(
            jax.ShapeDtypeStruct((rows, rank), BF16),
            jax.ShapeDtypeStruct((cols, rank), BF16),
            jax.ShapeDtypeStruct((8, 128), F32),
            jax.ShapeDtypeStruct((share, rank), F32),
            jax.ShapeDtypeStruct((rows, cols), F32),
        ),
        in_specs=[hbm] * 4 + [pl.BlockSpec(memory_space=pltpu.SMEM)],
        out_specs=(vmem,) * 5,
        scratch_shapes=[
            pltpu.VMEM((2 * rows, cols), BF16),
            pltpu.VMEM(exponents.shape, jnp.int32),
            pltpu.VMEM((rows // BLOCK, 16, cols), BF16),
            pltpu.VMEM((block, rank), F32),
            pltpu.VMEM((cols, rank), BF16),
            pltpu.VMEM((cols, rows), BF16),
            pltpu.VMEM((cols, rows), BF16),
            pltpu.VMEM((n_dp, 8, 128), F32),
            pltpu.VMEM((2, 8, 128), F32),
            pltpu.VMEM((chips, 8, 128), F32),
            pltpu.VMEM((rows, rank), F32),
            pltpu.VMEM((n_dp - 1, rows // n_dp, rank), F32),
            pltpu.VMEM((rows, rank), F32),
            pltpu.VMEM((rank, rank), F32),
            pltpu.VMEM((chips - 1, rank // chips, rank), F32),
            pltpu.VMEM((2 * n_dp, rank // chips, rank), F32),
            pltpu.VMEM((rank, rank), F32),
            pltpu.VMEM((rank, rank), F32),
            pltpu.VMEM((rank, rank), F32),
            pltpu.VMEM((half, block, rank), BF16),
            pltpu.VMEM((half, block, rank), BF16),
            pltpu.VMEM((half, block, rank), BF16),
            pltpu.VMEM((half, block, rank), BF16),
            pltpu.VMEM((block, rank), F32),
            pltpu.VMEM((block, rank), F32),
            pltpu.VMEM((n_dp, 8, 128), F32),
            pltpu.VMEM((chips, 8, 128), F32),
            dma((4,)),
            dma((2,)),
            dma((4, half)),
            dma((2, n_dp - 1)),
            dma((2,)),
            dma((2, chips - 1)),
            dma((2, n_dp - 1)),
            dma((2, n_dp - 1)),
            dma((2, chips - 1)),
            dma((2, 2 * n_dp - 1)),
            dma((2, chips - 1)),
            dma((2, half)),
            dma((2, half)),
            dma((2,)),
            dma((4, half)),
            dma((2, n_dp - 1)),
            dma((2, chips - 1)),
        ],
        compiler_params=pltpu.CompilerParams(
            collective_id=0, has_side_effects=True, vmem_limit_bytes=VMEM_LIMIT
        ),
    )(momentum, tile_values, exponents, right_prev, overflow)


def finish_kernel(unit, sums, ortho, low, inv, share, new, upd, share_out, new_v, upd_v, sem):
    rows, cols = sums.shape
    step = 256
    base = ortho[...]
    scaled = (base.astype(F32) * inv[0:1, :]).astype(BF16)
    both = (((1,), (1,)), ((), ()))
    share_copy = pltpu.make_async_copy(share, share_out, sem.at[2, 0])
    share_copy.start()
    copies = [share_copy]
    for t in range(cols // step):
        at = slice(t * step, (t + 1) * step)
        piece = low[at, :]
        correction = lax.dot_general(base, piece, both, preferred_element_type=F32)
        new_v[:, at] = (sums[:, at] - (1.0 - RETAIN) * correction).astype(BF16)
        direction = lax.dot_general(scaled, piece, both, preferred_element_type=F32)
        upd_v[:, at] = (unit * direction).astype(BF16)
        for k, (src, dst) in enumerate([(new_v, new), (upd_v, upd)]):
            copy = pltpu.make_async_copy(src.at[:, at], dst.at[:, at], sem.at[k, t])
            copy.start()
            copies.append(copy)
    for copy in copies:
        copy.wait()


def finish_stage(unit, sums, ortho, low, inv, share):
    rows, cols = sums.shape
    vmem = pl.BlockSpec(memory_space=pltpu.VMEM)
    hbm = pl.BlockSpec(memory_space=pltpu.HBM)
    return pl.pallas_call(
        functools.partial(finish_kernel, unit),
        name="finish",
        out_shape=(
            jax.ShapeDtypeStruct((rows, cols), BF16),
            jax.ShapeDtypeStruct((rows, cols), BF16),
            jax.ShapeDtypeStruct(share.shape, F32),
        ),
        in_specs=[vmem] * 5,
        out_specs=(hbm,) * 3,
        scratch_shapes=[
            pltpu.VMEM((rows, cols), BF16),
            pltpu.VMEM((rows, cols), BF16),
            pltpu.SemaphoreType.DMA((3, cols // 256)),
        ],
        compiler_params=pltpu.CompilerParams(vmem_limit_bytes=VMEM_LIMIT),
    )(sums, ortho, low, inv, share)


def body(n_dp, n_mp, momentum, tile_values, exponents, overflow, right_prev):
    rows, cols = momentum.shape
    rank = right_prev.shape[1]
    unit = math.sqrt(rows * n_mp * cols * n_dp / rank)
    args = [
        pltpu.with_memory_space_constraint(a, pltpu.HBM)
        for a in (momentum, tile_values, exponents, right_prev)
    ]
    ortho, low, inv, own, sums = mega_stage(n_dp, n_mp, *args, overflow)
    new, update, right_out = finish_stage(unit, sums, ortho, low, inv, own)
    return new, right_out, update


def solution(mesh):
    in_specs = (P("mp", "dp"), P("mp", "dp"), P("mp", "dp"), P("mp", "dp"), P(("dp", "mp"), None))
    out_specs = (P("mp", "dp"), P(("dp", "mp"), None), P("mp", "dp"))
    step = functools.partial(body, mesh.shape["dp"], mesh.shape["mp"])
    return jax.shard_map(step, mesh=mesh, in_specs=in_specs, out_specs=out_specs, check_vma=False)
```

```python
import functools
import math

import jax
import jax.numpy as jnp
from jax import lax
from jax.experimental import pallas as pl
from jax.experimental.pallas import tpu as pltpu
from jax.sharding import PartitionSpec as P

MESH = pl.DeviceIdType.MESH
F32 = jnp.float32
BF16 = jnp.bfloat16
HIGH = lax.Precision.HIGHEST
BLOCK = 128
EPSILON = 1e-06
RETAIN = 0.95
VMEM_LIMIT = 32 * 1024 * 1024


def torus(a, n):
    return min(a % n, -a % n)


class Place:
    def __init__(self, n_dp, n_mp):
        self.nz = n_dp
        self.chips = n_mp // 2
        self.ny = int(round(math.sqrt(self.chips)))
        self.nx = self.chips // self.ny
        self.half = self.chips // 2
        mp = lax.axis_index("mp")
        self.z = lax.axis_index("dp")
        self.core = lax.rem(mp, 2)
        self.other = 1 - self.core
        self.chip = mp // 2
        x = self.chip // self.ny
        y = lax.rem(self.chip, self.ny)
        xs = [lax.rem(x + d, self.nx) * self.ny for d in range(self.nx)]
        ys = [lax.rem(y + d, self.ny) for d in range(self.ny)]
        offsets = sorted(
            ((dx, dy) for dx in range(self.nx) for dy in range(self.ny)),
            key=lambda o: -torus(o[0], self.nx) - torus(o[1], self.ny),
        )
        chips = {o: xs[o[0]] + ys[o[1]] for o in offsets}
        def away(offset):
            return torus(offset[0], self.nx) + torus(offset[1], self.ny)

        def back(offset):
            return chips[-offset[0] % self.nx, -offset[1] % self.ny]

        self.sibling = (self.z, self.chip * 2 + self.other)
        self.plane = [chips[o] for o in offsets[:-1]]
        self.plane_from = [back(o) for o in offsets[:-1]]
        far = [o for o in offsets if away(o) > 1]
        near = [o for o in offsets if away(o) == 1]
        self.n_far, self.n_near = len(far), len(near)
        odd = far[0::2]
        even = far[1::2] + odd[-1:]
        self.far_to = [jnp.where(self.core == 0, chips[a], chips[b]) for a, b in zip(even, odd)]
        self.far_from = [jnp.where(self.core == 0, back(a), back(b)) for a, b in zip(even, odd)]
        self.far_passed = [jnp.where(self.core == 0, back(b), back(a)) for a, b in zip(even, odd)]
        self.near_to = [chips[o] for o in near]
        self.near_from = [back(o) for o in near]
        self.plane_peers = [(self.z, chip * 2 + self.core) for chip in self.plane]
        self.plane_all = self.plane_peers + [(self.z, chip * 2 + self.other) for chip in self.plane] + [self.sibling]
        self.z_order = sorted(range(1, self.nz), key=lambda d: -torus(d, self.nz))
        self.zs = [lax.rem(self.z + d, self.nz) for d in self.z_order]
        self.z_peers = [(z, self.chip * 2 + self.core) for z in self.zs]
        self.zc_peers = [
            (z, self.chip * 2 + core) for z in self.zs for core in (self.core, self.other)
        ] + [self.sibling]

    def same_core(self, chip):
        return (self.z, chip * 2 + self.core)

    def other_core(self, chip):
        return (self.z, chip * 2 + self.other)


def remote(src, dst, send, recv, dev):
    return pltpu.make_async_remote_copy(
        src_ref=src, dst_ref=dst, send_sem=send, recv_sem=recv, device_id=dev, device_id_type=MESH
    )


def exchange(peers, src_of, dst, sems):
    copies = [remote(src_of(k), dst, sems.at[0, k], sems.at[1, k], dev) for k, dev in enumerate(peers)]
    for copy in copies:
        copy.start()
    return copies


class BlockGather:
    def __init__(self, place, buf, rows, sems, near_sems):
        self.place = place

        def at(chip):
            return buf.at[pl.ds(pl.multiple_of(chip * rows, 16), rows)]

        mine = at(place.chip)
        self.far = [
            remote(mine, mine, sems.at[0, i], sems.at[1, i], place.same_core(chip))
            for i, chip in enumerate(place.far_to)
        ]
        self.arrivals = [
            remote(at(chip), at(chip), sems.at[0, i], sems.at[1, i], place.sibling)
            for i, chip in enumerate(place.far_from)
        ]
        self.passes = [
            remote(at(chip), at(chip), sems.at[2, i], sems.at[3, i], place.sibling)
            for i, chip in enumerate(place.far_from)
        ]
        self.passed = [
            remote(at(chip), at(chip), sems.at[2, i], sems.at[3, i], place.sibling)
            for i, chip in enumerate(place.far_passed)
        ]
        self.near = [
            remote(mine, mine, near_sems.at[0, i], near_sems.at[1, i], place.same_core(chip))
            for i, chip in enumerate(place.near_to)
        ]
        self.near_in = [
            remote(at(chip), at(chip), near_sems.at[0, i], near_sems.at[1, i], place.sibling)
            for i, chip in enumerate(place.near_from)
        ]

    def send(self):
        for copy in self.far[:-1]:
            copy.start()
        pl.when(self.place.core == 1)(self.far[-1].start)
        for copy in self.near:
            copy.start()

    def receive(self, use):
        place = self.place
        for arrival, onward, chip in list(zip(self.arrivals, self.passes, place.far_from))[:-1]:
            arrival.wait_recv()
            onward.start()
            use(chip)

        def go():
            self.arrivals[-1].wait_recv()
            self.passes[-1].start()

        pl.when(place.core == 1)(go)
        for copy, chip in zip(self.near_in, place.near_from):
            copy.wait_recv()
            use(chip)
        for copy, chip in list(zip(self.passed, place.far_passed))[:-1]:
            copy.wait_recv()
            use(chip)
        pl.when(place.core == 0)(self.passed[-1].wait_recv)
        use(jnp.where(place.core == 1, place.far_from[-1], place.far_passed[-1]))

    def drain(self):
        for copy in self.far[:-1] + self.passes[:-1] + self.near:
            copy.wait_send()

        def last():
            self.far[-1].wait_send()
            self.passes[-1].wait_send()

        pl.when(self.place.core == 1)(last)


class WindowGather:
    def __init__(self, place, buf, block, window, sems, pass_sems, near_sems, own_sems):
        self.place = place
        keep = block - window

        def whole(chip):
            return buf.at[pl.ds(pl.multiple_of(chip * block + place.core * keep, 16), window)]

        def rest(chip, core):
            return buf.at[pl.ds(pl.multiple_of(chip * block + core * window, 16), keep)]

        mine, lacking = whole(place.chip), rest(place.chip, place.core)
        other = place.other
        self.own = remote(lacking, lacking, own_sems.at[0], own_sems.at[1], place.sibling)
        self.own_in = remote(
            rest(place.chip, other), rest(place.chip, other), own_sems.at[0], own_sems.at[1], place.sibling
        )
        self.sends = [
            remote(mine, mine, sems.at[0, k], sems.at[1, k], dev) for k, dev in enumerate(place.plane_peers)
        ]
        self.arrivals = [
            remote(whole(chip), whole(chip), sems.at[0, k], sems.at[1, k], place.sibling)
            for k, chip in enumerate(place.plane_from)
        ]
        far = place.plane_from[:place.n_far]
        self.passes = [
            remote(rest(chip, place.core), rest(chip, place.core), pass_sems.at[0, k], pass_sems.at[1, k], place.sibling)
            for k, chip in enumerate(far)
        ]
        self.passed = [
            remote(rest(chip, other), rest(chip, other), pass_sems.at[0, k], pass_sems.at[1, k], place.sibling)
            for k, chip in enumerate(far)
        ]
        self.near = [
            remote(lacking, lacking, near_sems.at[0, k], near_sems.at[1, k], place.other_core(chip))
            for k, chip in enumerate(place.near_to)
        ]
        self.near_in = [
            remote(rest(chip, other), rest(chip, other), near_sems.at[0, k], near_sems.at[1, k], place.sibling)
            for k, chip in enumerate(place.near_from)
        ]

    def send(self):
        for copy in self.sends + self.near + [self.own]:
            copy.start()

    def receive(self):
        for arrival, onward in zip(self.arrivals, self.passes):
            arrival.wait_recv()
            onward.start()
        for copy in self.arrivals[self.place.n_far:] + self.near_in + [self.own_in] + self.passed:
            copy.wait_recv()

    def drain(self):
        for copy in self.sends + self.near + [self.own] + self.passes:
            copy.wait_send()


def invert(work, out_ref):
    rank = work.shape[0]
    size = 8
    lanes = lax.broadcasted_iota(jnp.int32, (size, rank), 1)
    lane = lanes[0:1]
    for r in range(0, rank, size):
        row = [work[r + i:r + i + 1, :] for i in range(size)]
        a = [[jnp.broadcast_to(row[i][:, r + j:r + j + 1], (1, rank)) for j in range(i + 1)] for i in range(size)]
        inside = (lane >= r) & (lane < r + size)
        row = [jnp.where(inside, jnp.where(lane == r + i, 1.0, 0.0), row[i]) for i in range(size)]
        e = [[None] * size for _ in range(size)]
        pivot, recip = [], []
        for j in range(size):
            pivot.append(a[j][j])
            recip.append(1.0 / a[j][j])
            for i in range(j + 1, size):
                m = a[i][j] * recip[j]
                for k in range(j + 1, i + 1):
                    a[i][k] = a[i][k] - m * a[k][j]
                for k in range(j):
                    e[i][k] = e[i][k] - m * e[j][k]
                e[i][j] = -m
        z = []
        for i in range(size):
            t = row[i]
            for j in range(i):
                t = t + e[i][j] * row[j]
            z.append(t)
        y = []
        zq = [z[i] * recip[i] for i in range(size)]
        for i in range(size):
            t = zq[i]
            for k in range(i + 1, size):
                t = t + e[k][i] * zq[k]
            y.append(t)
        out = jnp.concatenate([z[i] * lax.rsqrt(pivot[i]) for i in range(size)], axis=0)
        out_ref[r:r + size, :] = jnp.where(lanes < r + size, out, 0.0)
        for s in range(r + size, rank, size):
            old = work[s:s + size, :]
            acc = jnp.where((lanes >= r) & (lanes < r + size), 0.0, old)
            for k in range(size):
                acc = acc - jnp.broadcast_to(old[:, r + k:r + k + 1], (size, rank)) * y[k]
            work[s:s + size, :] = acc


def mega_kernel(
    n_dp, n_mp,
    mom_hbm, tile_hbm, exps_hbm, prev_hbm, over_ref,
    ortho_ref, low_ref, inv_ref, share_ref, sum_ref,
    both, exps, scale, pair, right, both_t, flag_z, flag_p, left_t,
    part, left_in, left, gram, gram_p, gram_zc, gram_all, work, tri,
    core_send, core_in, core_out, plane_in, mine, sq_z, sq_p,
    sem_in, sem_pair, sem_gather, sem_near, sem_fz, sem_fp, sem_lr, sem_lg, sem_gp, sem_gz, sem_gg,
    sem_core, sem_plane, sem_low, sem_pass, sem_low_near, sem_own, sem_sz, sem_sp,
):
    place = Place(n_dp, n_mp)
    rows, cols = mom_hbm.shape
    share, rank = share_ref.shape
    block = 2 * share
    my_share = pl.ds(pl.multiple_of(place.core * share, 8), share)
    loads = [
        pltpu.make_async_copy(src, dst, sem_in.at[k])
        for k, (src, dst) in enumerate(
            [
                (prev_hbm, pair.at[my_share]), (exps_hbm, exps),
                (mom_hbm, both.at[0:rows]), (tile_hbm, both.at[rows:2 * rows]),
            ]
        )
    ]
    for load in loads:
        load.start()
    barrier = pltpu.get_barrier_semaphore()
    friends = place.plane_all + place.zc_peers[:-1]
    for dev in friends:
        pl.semaphore_signal(barrier, inc=1, device_id=dev, device_id_type=MESH)
    kept = jnp.where(over_ref[0, 0] == 0, 1.0, 0.0).astype(F32)
    flag_z[place.z] = jnp.full((8, 128), kept, F32)
    loads[1].wait()
    scales = jnp.exp2(exps[...].astype(F32)).astype(BF16).astype(F32) * kept
    for j in range(cols // BLOCK):
        for b in range(rows // BLOCK):
            scale[b, :, j * BLOCK:(j + 1) * BLOCK] = jnp.broadcast_to(scales[b:b + 1, j:j + 1], (16, BLOCK)).astype(BF16)
    loads[0].wait()
    pl.semaphore_wait(barrier, len(friends))
    pending = []

    fz = exchange(place.z_peers, lambda k: flag_z.at[place.z], flag_z.at[place.z], sem_fz)
    pair_copy = remote(pair.at[my_share], pair.at[my_share], sem_pair.at[0], sem_pair.at[1], place.sibling)
    pair_copy.start()
    pair_copy.wait_recv()
    right[pl.ds(pl.multiple_of(place.chip * block, 16), block)] = pair[...].astype(BF16)
    gather = BlockGather(place, right, block, sem_gather, sem_near)
    gather.send()

    loads[2].wait()
    loads[3].wait()

    def decode(j, carry):
        at = pl.ds(pl.multiple_of(j * BLOCK, BLOCK), BLOCK)
        for b in range(rows // BLOCK):
            factor_of = scale[b, :, at]
            for r in range(rows + b * BLOCK, rows + (b + 1) * BLOCK, 16):
                both[r:r + 16, at] = both[r:r + 16, at] * factor_of
        return carry

    lax.fori_loop(0, cols // BLOCK, decode, 0)

    for copy in fz:
        copy.wait_recv()
    me = place.chip * 2 + place.core
    flag_p[me] = jnp.sum(flag_z[...], axis=0)
    fp = exchange(place.plane_all, lambda k: flag_p.at[me], flag_p.at[me], sem_fp)

    def transpose(j, carry):
        at = pl.ds(pl.multiple_of(j * BLOCK, BLOCK), BLOCK)
        both_t[at, :rows] = both[0:rows, at].T
        both_t[at, rows:] = both[rows:2 * rows, at].T
        return carry

    lax.fori_loop(0, cols // BLOCK, transpose, 0, unroll=2)

    def rows_of(chip):
        return pl.ds(pl.multiple_of(chip * block, 16), block)

    left_t[...] = jnp.zeros_like(left_t)

    def use(chip):
        at = rows_of(chip)
        left_t[...] += jnp.dot(right[at, :].T, both_t[at, :], preferred_element_type=F32)

    use(place.chip)
    gather.receive(use)
    for copy in fp:
        copy.wait_recv()
    healthy = jnp.sum(flag_p[...], axis=0)
    factor = (float(n_dp * n_mp) / jnp.maximum(healthy, 1.0))[0:1, :]
    pending += [pair_copy] + fz + fp
    for r in range(0, rows, BLOCK):
        part[r:r + BLOCK, :] = (left_t[:, r:r + BLOCK] + factor * left_t[:, rows + r:rows + r + BLOCK]).T

    rz = rows // place.nz
    lr = []
    for k, z in enumerate(place.zs):
        copy = remote(
            part.at[pl.ds(pl.multiple_of(z * rz, 8), rz)], left_in.at[k], sem_lr.at[0, k], sem_lr.at[1, k],
            place.z_peers[k],
        )
        copy.start()
        lr.append(copy)

    wide = jnp.broadcast_to(factor[:, 0:1], (16, BLOCK))

    def add(j, carry):
        at = pl.ds(pl.multiple_of(j * BLOCK, BLOCK), BLOCK)
        for r in range(0, rows, 16):
            sum_ref[r:r + 16, at] = both[r:r + 16, at].astype(F32) + wide * both[rows + r:rows + r + 16, at].astype(F32)
        return carry

    own = pl.ds(pl.multiple_of(place.z * rz, 8), rz)
    acc = part[own]
    for k, copy in enumerate(lr):
        copy.wait_recv()
        acc = acc + left_in[k]
    left[own] = acc
    pending += lr
    gram[...] = lax.dot_general(acc, acc, (((0,), (0,)), ((), ())), precision=HIGH, preferred_element_type=F32)

    gs = rank // place.chips
    piece = pl.ds(pl.multiple_of(place.chip * gs, 8), gs)
    gp = []
    for k, chip in enumerate(place.plane):
        copy = remote(
            gram.at[pl.ds(pl.multiple_of(chip * gs, 8), gs)], gram_p.at[k], sem_gp.at[0, k], sem_gp.at[1, k],
            place.plane_peers[k],
        )
        copy.start()
        gp.append(copy)
    acc = gram[piece]
    lax.fori_loop(0, cols // BLOCK, add, 0)
    for k, copy in enumerate(gp):
        copy.wait_recv()
        acc = acc + gram_p[k]
    pending += gp
    spot = place.z * 2 + place.core
    gram_zc[spot] = acc
    gz = exchange(place.zc_peers, lambda k: gram_zc.at[spot], gram_zc.at[spot], sem_gz)
    for copy in gz:
        copy.wait_recv()
    gram_all[piece] = jnp.sum(gram_zc[...], axis=0)
    pending += gz
    gg = exchange(place.plane_peers, lambda k: gram_all.at[piece], gram_all.at[piece], sem_gg)
    lg = exchange(place.z_peers, lambda k: left.at[own], left.at[own], sem_lg)
    for copy in gg:
        copy.wait_recv()
    pending += gg + lg
    work[...] = gram_all[...]
    invert(work, tri)
    for copy in lg:
        copy.wait_recv()

    ortho = lax.dot_general(
        left[...], tri[...], (((1,), (1,)), ((), ())), precision=HIGH, preferred_element_type=F32
    ).astype(BF16)
    ortho_ref[...] = ortho

    window = share + -share % 16
    keep = block - window

    def right_part(chip, core):
        at = pl.ds(pl.multiple_of(chip * block + core * keep, 16), window)
        return jnp.dot(both_t[at, :rows], ortho, preferred_element_type=F32) + factor * jnp.dot(
            both_t[at, rows:], ortho, preferred_element_type=F32
        )

    chips = place.plane + [place.chip]
    chunk = len(chips) // 4
    core_copies = []
    for k, chip in enumerate(chips):
        core_send[k] = right_part(chip, place.other).astype(BF16)
        if k % chunk == chunk - 1:
            j = k // chunk
            at = pl.ds(j * chunk, chunk)
            copy = remote(core_send.at[at], core_in.at[at], sem_core.at[0, j], sem_core.at[1, j], place.sibling)
            copy.start()
            core_copies.append(copy)
    plane_copies = []
    for k, chip in enumerate(chips):
        total = right_part(chip, place.core)
        if k % chunk == 0:
            core_copies[k // chunk].wait_recv()
        total = total + core_in[k].astype(F32)
        if chip is place.chip:
            break
        core_out[k] = total.astype(BF16)
        copy = remote(core_out.at[k], plane_in.at[k], sem_plane.at[0, k], sem_plane.at[1, k], place.plane_peers[k])
        copy.start()
        plane_copies.append(copy)
    for k, copy in enumerate(plane_copies):
        copy.wait_recv()
        total = total + plane_in[k].astype(F32)
    pending += core_copies + plane_copies
    mine[...] = total
    own_share = mine[pl.ds(pl.multiple_of(place.core * (window - share), 8), share)]
    sq_z[place.z] = jnp.sum((own_share * own_share).reshape(share // 8, 8, rank), axis=0)
    sz = exchange(place.z_peers, lambda k: sq_z.at[place.z], sq_z.at[place.z], sem_sz)
    low_ref[pl.ds(pl.multiple_of(place.chip * block + place.core * keep, 16), window)] = total.astype(BF16)
    last_gather = WindowGather(place, low_ref, block, window, sem_low, sem_pass, sem_low_near, sem_own)
    last_gather.send()
    share_ref[...] = own_share
    for copy in sz:
        copy.wait_recv()
    sq_p[me] = jnp.sum(sq_z[...], axis=0)
    sp = exchange(place.plane_all, lambda k: sq_p.at[me], sq_p.at[me], sem_sp)
    last_gather.receive()
    for copy in sp:
        copy.wait_recv()
    squares = jnp.sum(jnp.sum(sq_p[...], axis=0), axis=0, keepdims=True)
    inv_ref[...] = jnp.broadcast_to(lax.rsqrt(squares + EPSILON), inv_ref.shape)
    for copy in pending + sz + sp:
        copy.wait_send()
    gather.drain()
    last_gather.drain()


def mega_stage(n_dp, n_mp, momentum, tile_values, exponents, right_prev, overflow):
    rows, cols = momentum.shape
    share, rank = right_prev.shape
    chips = n_mp // 2
    block = 2 * share
    window = share + -share % 16
    n_near = 4 if chips == 16 else 2
    n_far = chips - 1 - n_near
    vmem = pl.BlockSpec(memory_space=pltpu.VMEM)
    hbm = pl.BlockSpec(memory_space=pltpu.HBM)
    dma = pltpu.SemaphoreType.DMA
    return pl.pallas_call(
        functools.partial(mega_kernel, n_dp, n_mp),
        name="mega",
        out_shape=(
            jax.ShapeDtypeStruct((rows, rank), BF16),
            jax.ShapeDtypeStruct((cols, rank), BF16),
            jax.ShapeDtypeStruct((8, 128), F32),
            jax.ShapeDtypeStruct((share, rank), F32),
            jax.ShapeDtypeStruct((rows, cols), F32),
        ),
        in_specs=[hbm] * 4 + [pl.BlockSpec(memory_space=pltpu.SMEM)],
        out_specs=(vmem,) * 5,
        scratch_shapes=[
            pltpu.VMEM((2 * rows, cols), BF16),
            pltpu.VMEM(exponents.shape, jnp.int32),
            pltpu.VMEM((rows // BLOCK, 16, cols), BF16),
            pltpu.VMEM((block, rank), F32),
            pltpu.VMEM((cols, rank), BF16),
            pltpu.VMEM((cols, 2 * rows), BF16),
            pltpu.VMEM((n_dp, 8, 128), F32),
            pltpu.VMEM((n_mp, 8, 128), F32),
            pltpu.VMEM((rank, 2 * rows), F32),
            pltpu.VMEM((rows, rank), F32),
            pltpu.VMEM((n_dp - 1, rows // n_dp, rank), F32),
            pltpu.VMEM((rows, rank), F32),
            pltpu.VMEM((rank, rank), F32),
            pltpu.VMEM((chips - 1, rank // chips, rank), F32),
            pltpu.VMEM((2 * n_dp, rank // chips, rank), F32),
            pltpu.VMEM((rank, rank), F32),
            pltpu.VMEM((rank, rank), F32),
            pltpu.VMEM((rank, rank), F32),
            pltpu.VMEM((chips, window, rank), BF16),
            pltpu.VMEM((chips, window, rank), BF16),
            pltpu.VMEM((chips - 1, window, rank), BF16),
            pltpu.VMEM((chips - 1, window, rank), BF16),
            pltpu.VMEM((window, rank), F32),
            pltpu.VMEM((n_dp, 8, 128), F32),
            pltpu.VMEM((n_mp, 8, 128), F32),
            dma((4,)),
            dma((2,)),
            dma((4, (n_far + 1) // 2)),
            dma((2, n_near)),
            dma((2, n_dp - 1)),
            dma((2, n_mp - 1)),
            dma((2, n_dp - 1)),
            dma((2, n_dp - 1)),
            dma((2, chips - 1)),
            dma((2, 2 * n_dp - 1)),
            dma((2, chips - 1)),
            dma((2, 4)),
            dma((2, chips - 1)),
            dma((2, chips - 1)),
            dma((2, n_far)),
            dma((2, n_near)),
            dma((2,)),
            dma((2, n_dp - 1)),
            dma((2, n_mp - 1)),
        ],
        compiler_params=pltpu.CompilerParams(
            collective_id=0, has_side_effects=True, vmem_limit_bytes=VMEM_LIMIT
        ),
    )(momentum, tile_values, exponents, right_prev, overflow)


def finish_kernel(unit, sums, ortho, low, inv, share, new, upd, share_out, new_v, upd_v, sem):
    rows, cols = sums.shape
    step = 256
    base = ortho[...]
    scaled = (base.astype(F32) * inv[0:1, :]).astype(BF16)
    both = (((1,), (1,)), ((), ()))
    share_copy = pltpu.make_async_copy(share, share_out, sem.at[2, 0])
    share_copy.start()
    copies = [share_copy]
    for t in range(cols // step):
        at = slice(t * step, (t + 1) * step)
        piece = low[at, :]
        correction = lax.dot_general(base, piece, both, preferred_element_type=F32)
        new_v[:, at] = (sums[:, at] - (1.0 - RETAIN) * correction).astype(BF16)
        direction = lax.dot_general(scaled, piece, both, preferred_element_type=F32)
        upd_v[:, at] = (unit * direction).astype(BF16)
        for k, (src, dst) in enumerate([(new_v, new), (upd_v, upd)]):
            copy = pltpu.make_async_copy(src.at[:, at], dst.at[:, at], sem.at[k, t])
            copy.start()
            copies.append(copy)
    for copy in copies:
        copy.wait()


def finish_stage(unit, sums, ortho, low, inv, share):
    rows, cols = sums.shape
    vmem = pl.BlockSpec(memory_space=pltpu.VMEM)
    hbm = pl.BlockSpec(memory_space=pltpu.HBM)
    return pl.pallas_call(
        functools.partial(finish_kernel, unit),
        name="finish",
        out_shape=(
            jax.ShapeDtypeStruct((rows, cols), BF16),
            jax.ShapeDtypeStruct((rows, cols), BF16),
            jax.ShapeDtypeStruct(share.shape, F32),
        ),
        in_specs=[vmem] * 5,
        out_specs=(hbm,) * 3,
        scratch_shapes=[
            pltpu.VMEM((rows, cols), BF16),
            pltpu.VMEM((rows, cols), BF16),
            pltpu.SemaphoreType.DMA((3, cols // 256)),
        ],
        compiler_params=pltpu.CompilerParams(vmem_limit_bytes=VMEM_LIMIT),
    )(sums, ortho, low, inv, share)


def body(n_dp, n_mp, momentum, tile_values, exponents, overflow, right_prev):
    rows, cols = momentum.shape
    rank = right_prev.shape[1]
    unit = math.sqrt(rows * n_mp * cols * n_dp / rank)
    args = [
        pltpu.with_memory_space_constraint(a, pltpu.HBM)
        for a in (momentum, tile_values, exponents, right_prev)
    ]
    ortho, low, inv, own, sums = mega_stage(n_dp, n_mp, *args, overflow)
    new, update, right_out = finish_stage(unit, sums, ortho, low, inv, own)
    return new, right_out, update


def solution(mesh):
    in_specs = (P("mp", "dp"), P("mp", "dp"), P("mp", "dp"), P("mp", "dp"), P(("dp", "mp"), None))
    out_specs = (P("mp", "dp"), P(("dp", "mp"), None), P("mp", "dp"))
    step = functools.partial(body, mesh.shape["dp"], mesh.shape["mp"])
    return jax.shard_map(step, mesh=mesh, in_specs=in_specs, out_specs=out_specs, check_vma=False)
```

```python
import functools
import math

import jax
import jax.numpy as jnp
from jax import lax
from jax.experimental import pallas as pl
from jax.experimental.pallas import tpu as pltpu
from jax.sharding import PartitionSpec as P

MESH = pl.DeviceIdType.MESH
F32 = jnp.float32
BF16 = jnp.bfloat16
HIGH = lax.Precision.HIGHEST
BLOCK = 128
EPSILON = 1e-06
RETAIN = 0.95
VMEM_LIMIT = 32 * 1024 * 1024


def torus(a, n):
    return min(a % n, -a % n)


class Place:
    def __init__(self, n_dp, n_mp):
        self.nz = n_dp
        self.chips = n_mp // 2
        self.ny = int(round(math.sqrt(self.chips)))
        self.nx = self.chips // self.ny
        self.half = self.chips // 2
        mp = lax.axis_index("mp")
        self.z = lax.axis_index("dp")
        self.core = lax.rem(mp, 2)
        self.other = 1 - self.core
        self.chip = mp // 2
        x = self.chip // self.ny
        y = lax.rem(self.chip, self.ny)
        xs = [lax.rem(x + d, self.nx) * self.ny for d in range(self.nx)]
        ys = [lax.rem(y + d, self.ny) for d in range(self.ny)]
        offsets = sorted(
            ((dx, dy) for dx in range(self.nx) for dy in range(self.ny)),
            key=lambda o: -torus(o[0], self.nx) - torus(o[1], self.ny),
        )
        chips = {o: xs[o[0]] + ys[o[1]] for o in offsets}
        def away(offset):
            return torus(offset[0], self.nx) + torus(offset[1], self.ny)

        def back(offset):
            return chips[-offset[0] % self.nx, -offset[1] % self.ny]

        self.sibling = (self.z, self.chip * 2 + self.other)
        self.plane = [chips[o] for o in offsets[:-1]]
        self.plane_from = [back(o) for o in offsets[:-1]]
        far = [o for o in offsets if away(o) > 1]
        near = [o for o in offsets if away(o) == 1]
        self.n_far, self.n_near = len(far), len(near)
        odd = far[0::2]
        even = far[1::2] + odd[-1:]
        self.far_to = [jnp.where(self.core == 0, chips[a], chips[b]) for a, b in zip(even, odd)]
        self.far_from = [jnp.where(self.core == 0, back(a), back(b)) for a, b in zip(even, odd)]
        self.far_passed = [jnp.where(self.core == 0, back(b), back(a)) for a, b in zip(even, odd)]
        self.near_to = [chips[o] for o in near]
        self.near_from = [back(o) for o in near]
        self.plane_peers = [(self.z, chip * 2 + self.core) for chip in self.plane]
        self.plane_all = [(self.z, chip * 2 + core) for chip in self.plane for core in (self.core, self.other)] + [self.sibling]
        self.z_order = sorted(range(1, self.nz), key=lambda d: -torus(d, self.nz))
        self.zs = [lax.rem(self.z + d, self.nz) for d in self.z_order]
        self.z_peers = [(z, self.chip * 2 + self.core) for z in self.zs]
        self.zc_peers = [
            (z, self.chip * 2 + core) for z in self.zs for core in (self.core, self.other)
        ] + [self.sibling]

    def same_core(self, chip):
        return (self.z, chip * 2 + self.core)

    def other_core(self, chip):
        return (self.z, chip * 2 + self.other)


def remote(src, dst, send, recv, dev):
    return pltpu.make_async_remote_copy(
        src_ref=src, dst_ref=dst, send_sem=send, recv_sem=recv, device_id=dev, device_id_type=MESH
    )


def exchange(peers, src_of, dst, sems):
    copies = [remote(src_of(k), dst, sems.at[0, k], sems.at[1, k], dev) for k, dev in enumerate(peers)]
    for copy in copies:
        copy.start()
    return copies


class BlockGather:
    def __init__(self, place, buf, rows, sems, near_sems):
        self.place = place

        def at(chip):
            return buf.at[pl.ds(pl.multiple_of(chip * rows, 16), rows)]

        mine = at(place.chip)
        self.far = [
            remote(mine, mine, sems.at[0, i], sems.at[1, i], place.same_core(chip))
            for i, chip in enumerate(place.far_to)
        ]
        self.arrivals = [
            remote(at(chip), at(chip), sems.at[0, i], sems.at[1, i], place.sibling)
            for i, chip in enumerate(place.far_from)
        ]
        self.passes = [
            remote(at(chip), at(chip), sems.at[2, i], sems.at[3, i], place.sibling)
            for i, chip in enumerate(place.far_from)
        ]
        self.passed = [
            remote(at(chip), at(chip), sems.at[2, i], sems.at[3, i], place.sibling)
            for i, chip in enumerate(place.far_passed)
        ]
        self.near = [
            remote(mine, mine, near_sems.at[0, i], near_sems.at[1, i], place.same_core(chip))
            for i, chip in enumerate(place.near_to)
        ]
        self.near_in = [
            remote(at(chip), at(chip), near_sems.at[0, i], near_sems.at[1, i], place.sibling)
            for i, chip in enumerate(place.near_from)
        ]

    def send(self):
        for copy in self.far[:-1]:
            copy.start()
        pl.when(self.place.core == 1)(self.far[-1].start)
        for copy in self.near:
            copy.start()

    def receive(self, use):
        place = self.place
        for arrival, onward, chip in list(zip(self.arrivals, self.passes, place.far_from))[:-1]:
            arrival.wait_recv()
            onward.start()
            use(chip)

        def go():
            self.arrivals[-1].wait_recv()
            self.passes[-1].start()

        pl.when(place.core == 1)(go)
        for copy, chip in zip(self.near_in, place.near_from):
            copy.wait_recv()
            use(chip)
        for copy, chip in list(zip(self.passed, place.far_passed))[:-1]:
            copy.wait_recv()
            use(chip)
        pl.when(place.core == 0)(self.passed[-1].wait_recv)
        use(jnp.where(place.core == 1, place.far_from[-1], place.far_passed[-1]))

    def drain(self):
        for copy in self.far[:-1] + self.passes[:-1] + self.near:
            copy.wait_send()

        def last():
            self.far[-1].wait_send()
            self.passes[-1].wait_send()

        pl.when(self.place.core == 1)(last)


class WindowGather:
    def __init__(self, place, buf, block, window, sems, pass_sems, near_sems, own_sems):
        self.place = place
        keep = block - window

        def whole(chip):
            return buf.at[pl.ds(pl.multiple_of(chip * block + place.core * keep, 16), window)]

        def rest(chip, core):
            return buf.at[pl.ds(pl.multiple_of(chip * block + core * window, 16), keep)]

        mine, lacking = whole(place.chip), rest(place.chip, place.core)
        other = place.other
        self.own = remote(lacking, lacking, own_sems.at[0], own_sems.at[1], place.sibling)
        self.own_in = remote(
            rest(place.chip, other), rest(place.chip, other), own_sems.at[0], own_sems.at[1], place.sibling
        )
        self.sends = [
            remote(mine, mine, sems.at[0, k], sems.at[1, k], dev) for k, dev in enumerate(place.plane_peers)
        ]
        self.arrivals = [
            remote(whole(chip), whole(chip), sems.at[0, k], sems.at[1, k], place.sibling)
            for k, chip in enumerate(place.plane_from)
        ]
        far = place.plane_from[:place.n_far]
        self.passes = [
            remote(rest(chip, place.core), rest(chip, place.core), pass_sems.at[0, k], pass_sems.at[1, k], place.sibling)
            for k, chip in enumerate(far)
        ]
        self.passed = [
            remote(rest(chip, other), rest(chip, other), pass_sems.at[0, k], pass_sems.at[1, k], place.sibling)
            for k, chip in enumerate(far)
        ]
        self.near = [
            remote(lacking, lacking, near_sems.at[0, k], near_sems.at[1, k], place.other_core(chip))
            for k, chip in enumerate(place.near_to)
        ]
        self.near_in = [
            remote(rest(chip, other), rest(chip, other), near_sems.at[0, k], near_sems.at[1, k], place.sibling)
            for k, chip in enumerate(place.near_from)
        ]

    def send(self):
        for copy in self.sends + self.near + [self.own]:
            copy.start()

    def receive(self):
        for arrival, onward in zip(self.arrivals, self.passes):
            arrival.wait_recv()
            onward.start()
        for copy in self.arrivals[self.place.n_far:] + self.near_in + [self.own_in] + self.passed:
            copy.wait_recv()

    def drain(self):
        for copy in self.sends + self.near + [self.own] + self.passes:
            copy.wait_send()


def invert(work, out_ref):
    rank = work.shape[0]
    size = 8
    lanes = lax.broadcasted_iota(jnp.int32, (size, rank), 1)
    lane = lanes[0:1]
    for r in range(0, rank, size):
        row = [work[r + i:r + i + 1, :] for i in range(size)]
        a = [[jnp.broadcast_to(row[i][:, r + j:r + j + 1], (1, rank)) for j in range(i + 1)] for i in range(size)]
        inside = (lane >= r) & (lane < r + size)
        row = [jnp.where(inside, jnp.where(lane == r + i, 1.0, 0.0), row[i]) for i in range(size)]
        e = [[None] * size for _ in range(size)]
        pivot, recip = [], []
        for j in range(size):
            pivot.append(a[j][j])
            recip.append(1.0 / a[j][j])
            for i in range(j + 1, size):
                m = a[i][j] * recip[j]
                for k in range(j + 1, i + 1):
                    a[i][k] = a[i][k] - m * a[k][j]
                for k in range(j):
                    e[i][k] = e[i][k] - m * e[j][k]
                e[i][j] = -m
        z = []
        for i in range(size):
            t = row[i]
            for j in range(i):
                t = t + e[i][j] * row[j]
            z.append(t)
        y = []
        zq = [z[i] * recip[i] for i in range(size)]
        for i in range(size):
            t = zq[i]
            for k in range(i + 1, size):
                t = t + e[k][i] * zq[k]
            y.append(t)
        out = jnp.concatenate([z[i] * lax.rsqrt(pivot[i]) for i in range(size)], axis=0)
        out_ref[r:r + size, :] = jnp.where(lanes < r + size, out, 0.0)
        for s in range(r + size, rank, size):
            old = work[s:s + size, :]
            acc = jnp.where((lanes >= r) & (lanes < r + size), 0.0, old)
            for k in range(size):
                acc = acc - jnp.broadcast_to(old[:, r + k:r + k + 1], (size, rank)) * y[k]
            work[s:s + size, :] = acc


def mega_kernel(
    n_dp, n_mp,
    mom_hbm, tile_hbm, exps_hbm, prev_hbm, over_ref,
    ortho_ref, low_ref, inv_ref, share_ref, sum_ref,
    both, exps, scale, pair, right, both_t, flag_z, flag_p, left_t,
    part, left_in, left, left_hl, gram, gram_p, gram_zc, gram_all, work, tri,
    core_send, core_in, core_out, plane_in, mine, sq_z, sq_p,
    sem_in, sem_pair, sem_gather, sem_near, sem_fz, sem_fp, sem_lr, sem_lg, sem_gp, sem_gz, sem_gg,
    sem_core, sem_plane, sem_low, sem_pass, sem_low_near, sem_own, sem_sz, sem_sp,
):
    place = Place(n_dp, n_mp)
    rows, cols = mom_hbm.shape
    share, rank = share_ref.shape
    block = 2 * share
    my_share = pl.ds(pl.multiple_of(place.core * share, 8), share)
    loads = [
        pltpu.make_async_copy(src, dst, sem_in.at[k])
        for k, (src, dst) in enumerate(
            [
                (prev_hbm, pair.at[my_share]), (exps_hbm, exps),
                (mom_hbm, both.at[0:rows]), (tile_hbm, both.at[rows:2 * rows]),
            ]
        )
    ]
    for load in loads:
        load.start()
    barrier = pltpu.get_barrier_semaphore()
    friends = place.zc_peers[:-1] + place.plane_all
    for dev in friends:
        pl.semaphore_signal(barrier, inc=1, device_id=dev, device_id_type=MESH)
    kept = jnp.where(over_ref[0, 0] == 0, 1.0, 0.0).astype(F32)
    flag_z[place.z] = jnp.full((1, 128), kept, F32)
    loads[1].wait()
    scales = jnp.exp2(exps[...].astype(F32)).astype(BF16).astype(F32) * kept
    for j in range(cols // BLOCK):
        for b in range(rows // BLOCK):
            scale[b, :, j * BLOCK:(j + 1) * BLOCK] = jnp.broadcast_to(scales[b:b + 1, j:j + 1], (16, BLOCK)).astype(BF16)
    loads[0].wait()
    pl.semaphore_wait(barrier, len(friends))
    pending = []

    fz = exchange(place.z_peers, lambda k: flag_z.at[place.z], flag_z.at[place.z], sem_fz)
    pair_copy = remote(pair.at[my_share], pair.at[my_share], sem_pair.at[0], sem_pair.at[1], place.sibling)
    pair_copy.start()
    pair_copy.wait_recv()
    right[pl.ds(pl.multiple_of(place.chip * block, 16), block)] = pair[...].astype(BF16)
    gather = BlockGather(place, right, block, sem_gather, sem_near)
    gather.send()

    loads[2].wait()
    loads[3].wait()

    def decode(j, carry):
        at = pl.ds(pl.multiple_of(j * BLOCK, BLOCK), BLOCK)
        for b in range(rows // BLOCK):
            factor_of = scale[b, :, at]
            for r in range(rows + b * BLOCK, rows + (b + 1) * BLOCK, 16):
                both[r:r + 16, at] = both[r:r + 16, at] * factor_of
        return carry

    lax.fori_loop(0, cols // BLOCK, decode, 0)

    for copy in fz:
        copy.wait_recv()
    me = place.chip * 2 + place.core
    flag_p[me] = jnp.sum(flag_z[...], axis=0)
    fp = exchange(place.plane_all, lambda k: flag_p.at[me], flag_p.at[me], sem_fp)

    def transpose(j, carry):
        at = pl.ds(pl.multiple_of(j * BLOCK, BLOCK), BLOCK)
        both_t[at, :rows] = both[0:rows, at].T
        both_t[at, rows:] = both[rows:2 * rows, at].T
        return carry

    lax.fori_loop(0, cols // BLOCK, transpose, 0, unroll=2)

    def rows_of(chip):
        return pl.ds(pl.multiple_of(chip * block, 16), block)

    left_t[...] = jnp.zeros_like(left_t)

    def use(chip):
        at = rows_of(chip)
        left_t[...] += jnp.dot(right[at, :].T, both_t[at, :], preferred_element_type=F32)

    use(place.chip)
    gather.receive(use)
    for copy in fp:
        copy.wait_recv()
    healthy = jnp.sum(flag_p[...], axis=0)
    factor = float(n_dp * n_mp) / jnp.maximum(healthy, 1.0)
    pending += [pair_copy] + fz + fp
    for r in range(0, rows, BLOCK):
        part[r:r + BLOCK, :] = (left_t[:, r:r + BLOCK] + factor * left_t[:, rows + r:rows + r + BLOCK]).T

    rz = rows // place.nz
    lr = []
    for k, z in enumerate(place.zs):
        copy = remote(
            part.at[pl.ds(pl.multiple_of(z * rz, 8), rz)], left_in.at[k], sem_lr.at[0, k], sem_lr.at[1, k],
            place.z_peers[k],
        )
        copy.start()
        lr.append(copy)

    wide = jnp.broadcast_to(factor[:, 0:1], (16, BLOCK))

    def add(j, carry):
        at = pl.ds(pl.multiple_of(j * BLOCK, BLOCK), BLOCK)
        for r in range(0, rows, 16):
            sum_ref[r:r + 16, at] = both[r:r + 16, at].astype(F32) + wide * both[rows + r:rows + r + 16, at].astype(F32)
        return carry

    own = pl.ds(pl.multiple_of(place.z * rz, 8), rz)
    acc = part[own]
    for k, copy in enumerate(lr):
        copy.wait_recv()
        acc = acc + left_in[k]
    left[own] = acc
    pending += lr
    lg = exchange(place.z_peers, lambda k: left.at[own], left.at[own], sem_lg)
    gram[...] = lax.dot_general(acc, acc, (((0,), (0,)), ((), ())), precision=HIGH, preferred_element_type=F32)
    gs = rank // place.chips
    piece = pl.ds(pl.multiple_of(place.chip * gs, 8), gs)
    gp = []
    for k, chip in enumerate(place.plane):
        copy = remote(
            gram.at[pl.ds(pl.multiple_of(chip * gs, 8), gs)], gram_p.at[k], sem_gp.at[0, k], sem_gp.at[1, k],
            place.plane_peers[k],
        )
        copy.start()
        gp.append(copy)
    lax.fori_loop(0, cols // BLOCK, add, 0)
    acc = gram[piece]
    for k, copy in enumerate(gp):
        copy.wait_recv()
        acc = acc + gram_p[k]
    spot = place.z * 2 + place.core
    gram_zc[spot] = acc
    gz = exchange(place.zc_peers, lambda k: gram_zc.at[spot], gram_zc.at[spot], sem_gz)
    for copy in lg:
        copy.wait_recv()
    pending += lg + gp

    high = left[...].astype(BF16)
    left_hl[:, :rank] = high
    left_hl[:, rank:] = (left[...] - high.astype(F32)).astype(BF16)
    window = share + -share % 16
    keep = block - window

    def raw_part(chip, core):
        at = pl.ds(pl.multiple_of(chip * block + core * keep, 16), window)
        mom_two = jnp.dot(both_t[at, :rows], left_hl[...], preferred_element_type=F32)
        grad_two = jnp.dot(both_t[at, rows:], left_hl[...], preferred_element_type=F32)
        return mom_two[:, :rank] + mom_two[:, rank:] + factor * (grad_two[:, :rank] + grad_two[:, rank:])

    chips = place.plane + [place.chip]
    chunk = len(chips) // 4
    core_copies = []
    for k, chip in enumerate(chips):
        core_send[k] = raw_part(chip, place.other)
        if k % chunk == chunk - 1:
            j = k // chunk
            at = pl.ds(j * chunk, chunk)
            copy = remote(core_send.at[at], core_in.at[at], sem_core.at[0, j], sem_core.at[1, j], place.sibling)
            copy.start()
            core_copies.append(copy)
    plane_copies = []

    def send_sums(first, last):
        for k in range(first, last):
            if k % chunk == 0:
                core_copies[k // chunk].wait_recv()
            core_out[k] = raw_part(chips[k], place.core) + core_in[k]
            copy = remote(core_out.at[k], plane_in.at[k], sem_plane.at[0, k], sem_plane.at[1, k], place.plane_peers[k])
            copy.start()
            plane_copies.append(copy)

    last = len(chips) - 1
    send_sums(0, 2 * chunk)
    for copy in gz:
        copy.wait_recv()
    gram_all[piece] = jnp.sum(gram_zc[...], axis=0)
    gg = exchange(place.plane_peers, lambda k: gram_all.at[piece], gram_all.at[piece], sem_gg)
    send_sums(2 * chunk, last)
    if last % chunk == 0:
        core_copies[-1].wait_recv()
    total = raw_part(chips[last], place.core) + core_in[last]
    for copy in gg:
        copy.wait_recv()
    pending += gz + gg + core_copies + plane_copies
    work[...] = gram_all[...]
    invert(work, tri)
    for k, copy in enumerate(plane_copies):
        copy.wait_recv()
        total = total + plane_in[k]
    by_rank = (((1,), (1,)), ((), ()))
    total = lax.dot_general(total, tri[...], by_rank, precision=HIGH, preferred_element_type=F32)
    mine[...] = total
    own_share = mine[pl.ds(pl.multiple_of(place.core * (window - share), 8), share)]
    sq_z[place.z] = jnp.sum(own_share * own_share, axis=0, keepdims=True)
    sz = exchange(place.z_peers, lambda k: sq_z.at[place.z], sq_z.at[place.z], sem_sz)
    low_ref[pl.ds(pl.multiple_of(place.chip * block + place.core * keep, 16), window)] = total.astype(BF16)
    last_gather = WindowGather(place, low_ref, block, window, sem_low, sem_pass, sem_low_near, sem_own)
    last_gather.send()
    share_ref[...] = own_share
    ortho_ref[...] = lax.dot_general(
        left[...], tri[...], by_rank, precision=HIGH, preferred_element_type=F32
    ).astype(BF16)
    for copy in sz:
        copy.wait_recv()
    sq_p[me] = jnp.sum(sq_z[...], axis=0)
    sp = exchange(place.plane_all, lambda k: sq_p.at[me], sq_p.at[me], sem_sp)
    last_gather.receive()
    for copy in sp:
        copy.wait_recv()
    squares = jnp.sum(sq_p[...], axis=0)
    inv_ref[...] = jnp.broadcast_to(lax.rsqrt(squares + EPSILON), inv_ref.shape)
    for copy in pending + sz + sp:
        copy.wait_send()
    gather.drain()
    last_gather.drain()


def mega_stage(n_dp, n_mp, momentum, tile_values, exponents, right_prev, overflow):
    rows, cols = momentum.shape
    share, rank = right_prev.shape
    chips = n_mp // 2
    block = 2 * share
    window = share + -share % 16
    n_near = 4 if chips == 16 else 2
    n_far = chips - 1 - n_near
    vmem = pl.BlockSpec(memory_space=pltpu.VMEM)
    hbm = pl.BlockSpec(memory_space=pltpu.HBM)
    dma = pltpu.SemaphoreType.DMA
    return pl.pallas_call(
        functools.partial(mega_kernel, n_dp, n_mp),
        name="mega",
        out_shape=(
            jax.ShapeDtypeStruct((rows, rank), BF16),
            jax.ShapeDtypeStruct((cols, rank), BF16),
            jax.ShapeDtypeStruct((8, 128), F32),
            jax.ShapeDtypeStruct((share, rank), F32),
            jax.ShapeDtypeStruct((rows, cols), F32),
        ),
        in_specs=[hbm] * 4 + [pl.BlockSpec(memory_space=pltpu.SMEM)],
        out_specs=(vmem,) * 5,
        scratch_shapes=[
            pltpu.VMEM((2 * rows, cols), BF16),
            pltpu.VMEM(exponents.shape, jnp.int32),
            pltpu.VMEM((rows // BLOCK, 16, cols), BF16),
            pltpu.VMEM((block, rank), F32),
            pltpu.VMEM((cols, rank), BF16),
            pltpu.VMEM((cols, 2 * rows), BF16),
            pltpu.VMEM((n_dp, 1, 128), F32),
            pltpu.VMEM((n_mp, 1, 128), F32),
            pltpu.VMEM((rank, 2 * rows), F32),
            pltpu.VMEM((rows, rank), F32),
            pltpu.VMEM((n_dp - 1, rows // n_dp, rank), F32),
            pltpu.VMEM((rows, rank), F32),
            pltpu.VMEM((rows, 2 * rank), BF16),
            pltpu.VMEM((rank, rank), F32),
            pltpu.VMEM((chips - 1, rank // chips, rank), F32),
            pltpu.VMEM((2 * n_dp, rank // chips, rank), F32),
            pltpu.VMEM((rank, rank), F32),
            pltpu.VMEM((rank, rank), F32),
            pltpu.VMEM((rank, rank), F32),
            pltpu.VMEM((chips, window, rank), F32),
            pltpu.VMEM((chips, window, rank), F32),
            pltpu.VMEM((chips - 1, window, rank), F32),
            pltpu.VMEM((chips - 1, window, rank), F32),
            pltpu.VMEM((window, rank), F32),
            pltpu.VMEM((n_dp, 1, 128), F32),
            pltpu.VMEM((n_mp, 1, 128), F32),
            dma((4,)),
            dma((2,)),
            dma((4, (n_far + 1) // 2)),
            dma((2, n_near)),
            dma((2, n_dp - 1)),
            dma((2, n_mp - 1)),
            dma((2, n_dp - 1)),
            dma((2, n_dp - 1)),
            dma((2, chips - 1)),
            dma((2, 2 * n_dp - 1)),
            dma((2, chips - 1)),
            dma((2, 4)),
            dma((2, chips - 1)),
            dma((2, chips - 1)),
            dma((2, n_far)),
            dma((2, n_near)),
            dma((2,)),
            dma((2, n_dp - 1)),
            dma((2, n_mp - 1)),
        ],
        compiler_params=pltpu.CompilerParams(
            collective_id=0, has_side_effects=True, vmem_limit_bytes=VMEM_LIMIT
        ),
    )(momentum, tile_values, exponents, right_prev, overflow)


def finish_kernel(unit, sums, ortho, low, inv, share, new, upd, share_out, new_v, upd_v, sem):
    rows, cols = sums.shape
    step = 256
    base = ortho[...]
    scaled = (base.astype(F32) * inv[0:1, :]).astype(BF16)
    both = (((1,), (1,)), ((), ()))
    share_copy = pltpu.make_async_copy(share, share_out, sem.at[2, 0])
    share_copy.start()
    copies = [share_copy]
    for t in range(cols // step):
        at = slice(t * step, (t + 1) * step)
        piece = low[at, :]
        correction = lax.dot_general(base, piece, both, preferred_element_type=F32)
        new_v[:, at] = (sums[:, at] - (1.0 - RETAIN) * correction).astype(BF16)
        direction = lax.dot_general(scaled, piece, both, preferred_element_type=F32)
        upd_v[:, at] = (unit * direction).astype(BF16)
        for k, (src, dst) in enumerate([(new_v, new), (upd_v, upd)]):
            copy = pltpu.make_async_copy(src.at[:, at], dst.at[:, at], sem.at[k, t])
            copy.start()
            copies.append(copy)
    for copy in copies:
        copy.wait()


def finish_stage(unit, sums, ortho, low, inv, share):
    rows, cols = sums.shape
    vmem = pl.BlockSpec(memory_space=pltpu.VMEM)
    hbm = pl.BlockSpec(memory_space=pltpu.HBM)
    return pl.pallas_call(
        functools.partial(finish_kernel, unit),
        name="finish",
        out_shape=(
            jax.ShapeDtypeStruct((rows, cols), BF16),
            jax.ShapeDtypeStruct((rows, cols), BF16),
            jax.ShapeDtypeStruct(share.shape, F32),
        ),
        in_specs=[vmem] * 5,
        out_specs=(hbm,) * 3,
        scratch_shapes=[
            pltpu.VMEM((rows, cols), BF16),
            pltpu.VMEM((rows, cols), BF16),
            pltpu.SemaphoreType.DMA((3, cols // 256)),
        ],
        compiler_params=pltpu.CompilerParams(vmem_limit_bytes=VMEM_LIMIT),
    )(sums, ortho, low, inv, share)


def body(n_dp, n_mp, momentum, tile_values, exponents, overflow, right_prev):
    rows, cols = momentum.shape
    rank = right_prev.shape[1]
    unit = math.sqrt(rows * n_mp * cols * n_dp / rank)
    args = [
        pltpu.with_memory_space_constraint(a, pltpu.HBM)
        for a in (momentum, tile_values, exponents, right_prev)
    ]
    ortho, low, inv, own, sums = mega_stage(n_dp, n_mp, *args, overflow)
    new, update, right_out = finish_stage(unit, sums, ortho, low, inv, own)
    return new, right_out, update


def solution(mesh):
    in_specs = (P("mp", "dp"), P("mp", "dp"), P("mp", "dp"), P("mp", "dp"), P(("dp", "mp"), None))
    out_specs = (P("mp", "dp"), P(("dp", "mp"), None), P("mp", "dp"))
    step = functools.partial(body, mesh.shape["dp"], mesh.shape["mp"])
    return jax.shard_map(step, mesh=mesh, in_specs=in_specs, out_specs=out_specs, check_vma=False)
```

```python
import functools
import math

import jax
import jax.numpy as jnp
from jax import lax
from jax.experimental import pallas as pl
from jax.experimental.pallas import tpu as pltpu
from jax.sharding import PartitionSpec as P

MESH = pl.DeviceIdType.MESH
F32 = jnp.float32
BF16 = jnp.bfloat16
HIGH = lax.Precision.HIGHEST
BLOCK = 128
EPSILON = 1e-06
RETAIN = 0.95
VMEM_LIMIT = 32 * 1024 * 1024


def torus(a, n):
    return min(a % n, -a % n)


class Place:
    def __init__(self, n_dp, n_mp):
        self.nz = n_dp
        self.chips = n_mp // 2
        self.ny = int(round(math.sqrt(self.chips)))
        self.nx = self.chips // self.ny
        self.half = self.chips // 2
        mp = lax.axis_index("mp")
        self.z = lax.axis_index("dp")
        self.core = lax.rem(mp, 2)
        self.other = 1 - self.core
        self.chip = mp // 2
        x = self.chip // self.ny
        y = lax.rem(self.chip, self.ny)
        xs = [lax.rem(x + d, self.nx) * self.ny for d in range(self.nx)]
        ys = [lax.rem(y + d, self.ny) for d in range(self.ny)]
        offsets = sorted(
            ((dx, dy) for dx in range(self.nx) for dy in range(self.ny)),
            key=lambda o: -torus(o[0], self.nx) - torus(o[1], self.ny),
        )
        chips = {o: xs[o[0]] + ys[o[1]] for o in offsets}
        def away(offset):
            return torus(offset[0], self.nx) + torus(offset[1], self.ny)

        def back(offset):
            return chips[-offset[0] % self.nx, -offset[1] % self.ny]

        self.sibling = (self.z, self.chip * 2 + self.other)
        self.plane = [chips[o] for o in offsets[:-1]]
        self.plane_from = [back(o) for o in offsets[:-1]]
        far = [o for o in offsets if away(o) > 1]
        near = [o for o in offsets if away(o) == 1]
        self.n_far, self.n_near = len(far), len(near)
        odd = far[0::2]
        even = far[1::2] + odd[-1:]
        self.far_to = [jnp.where(self.core == 0, chips[a], chips[b]) for a, b in zip(even, odd)]
        self.far_from = [jnp.where(self.core == 0, back(a), back(b)) for a, b in zip(even, odd)]
        self.far_passed = [jnp.where(self.core == 0, back(b), back(a)) for a, b in zip(even, odd)]
        self.near_to = [chips[o] for o in near]
        self.near_from = [back(o) for o in near]
        self.plane_peers = [(self.z, chip * 2 + self.core) for chip in self.plane]
        self.plane_all = [(self.z, chip * 2 + core) for chip in self.plane for core in (self.core, self.other)] + [self.sibling]
        self.z_order = sorted(range(1, self.nz), key=lambda d: -torus(d, self.nz))
        self.zs = [lax.rem(self.z + d, self.nz) for d in self.z_order]
        self.z_peers = [(z, self.chip * 2 + self.core) for z in self.zs]
        self.zc_peers = [
            (z, self.chip * 2 + core) for z in self.zs for core in (self.core, self.other)
        ] + [self.sibling]
        self.zc_spots = [z * 2 + core for z in self.zs for core in (self.core, self.other)] + [self.z * 2 + self.other]

    def same_core(self, chip):
        return (self.z, chip * 2 + self.core)

    def other_core(self, chip):
        return (self.z, chip * 2 + self.other)


def remote(src, dst, send, recv, dev):
    return pltpu.make_async_remote_copy(
        src_ref=src, dst_ref=dst, send_sem=send, recv_sem=recv, device_id=dev, device_id_type=MESH
    )


def exchange(peers, src_of, dst, sems):
    copies = [remote(src_of(k), dst, sems.at[0, k], sems.at[1, k], dev) for k, dev in enumerate(peers)]
    for copy in copies:
        copy.start()
    return copies


class BlockGather:
    def __init__(self, place, buf, rows, sems, near_sems):
        self.place = place

        def at(chip):
            return buf.at[pl.ds(pl.multiple_of(chip * rows, 16), rows)]

        mine = at(place.chip)
        self.far = [
            remote(mine, mine, sems.at[0, i], sems.at[1, i], place.same_core(chip))
            for i, chip in enumerate(place.far_to)
        ]
        self.arrivals = [
            remote(at(chip), at(chip), sems.at[0, i], sems.at[1, i], place.sibling)
            for i, chip in enumerate(place.far_from)
        ]
        self.passes = [
            remote(at(chip), at(chip), sems.at[2, i], sems.at[3, i], place.sibling)
            for i, chip in enumerate(place.far_from)
        ]
        self.passed = [
            remote(at(chip), at(chip), sems.at[2, i], sems.at[3, i], place.sibling)
            for i, chip in enumerate(place.far_passed)
        ]
        self.near = [
            remote(mine, mine, near_sems.at[0, i], near_sems.at[1, i], place.same_core(chip))
            for i, chip in enumerate(place.near_to)
        ]
        self.near_in = [
            remote(at(chip), at(chip), near_sems.at[0, i], near_sems.at[1, i], place.sibling)
            for i, chip in enumerate(place.near_from)
        ]

    def send(self):
        for copy in self.far[:-1]:
            copy.start()
        pl.when(self.place.core == 1)(self.far[-1].start)
        for copy in self.near:
            copy.start()

    def receive(self, use):
        place = self.place
        for arrival, onward, chip in list(zip(self.arrivals, self.passes, place.far_from))[:-1]:
            arrival.wait_recv()
            onward.start()
            use(chip)

        def go():
            self.arrivals[-1].wait_recv()
            self.passes[-1].start()

        pl.when(place.core == 1)(go)
        for copy, chip in zip(self.near_in, place.near_from):
            copy.wait_recv()
            use(chip)
        for copy, chip in list(zip(self.passed, place.far_passed))[:-1]:
            copy.wait_recv()
            use(chip)
        pl.when(place.core == 0)(self.passed[-1].wait_recv)
        use(jnp.where(place.core == 1, place.far_from[-1], place.far_passed[-1]))

    def drain(self):
        for copy in self.far[:-1] + self.passes[:-1] + self.near:
            copy.wait_send()

        def last():
            self.far[-1].wait_send()
            self.passes[-1].wait_send()

        pl.when(self.place.core == 1)(last)


class WindowGather:
    def __init__(self, place, buf, block, window, sems, pass_sems, near_sems, own_sems):
        self.place = place
        keep = block - window

        def whole(chip):
            return buf.at[pl.ds(pl.multiple_of(chip * block + place.core * keep, 16), window)]

        def rest(chip, core):
            return buf.at[pl.ds(pl.multiple_of(chip * block + core * window, 16), keep)]

        mine, lacking = whole(place.chip), rest(place.chip, place.core)
        other = place.other
        self.own = remote(lacking, lacking, own_sems.at[0], own_sems.at[1], place.sibling)
        self.own_in = remote(
            rest(place.chip, other), rest(place.chip, other), own_sems.at[0], own_sems.at[1], place.sibling
        )
        self.sends = [
            remote(mine, mine, sems.at[0, k], sems.at[1, k], dev) for k, dev in enumerate(place.plane_peers)
        ]
        self.arrivals = [
            remote(whole(chip), whole(chip), sems.at[0, k], sems.at[1, k], place.sibling)
            for k, chip in enumerate(place.plane_from)
        ]
        far = place.plane_from[:place.n_far]
        self.passes = [
            remote(rest(chip, place.core), rest(chip, place.core), pass_sems.at[0, k], pass_sems.at[1, k], place.sibling)
            for k, chip in enumerate(far)
        ]
        self.passed = [
            remote(rest(chip, other), rest(chip, other), pass_sems.at[0, k], pass_sems.at[1, k], place.sibling)
            for k, chip in enumerate(far)
        ]
        self.near = [
            remote(lacking, lacking, near_sems.at[0, k], near_sems.at[1, k], place.other_core(chip))
            for k, chip in enumerate(place.near_to)
        ]
        self.near_in = [
            remote(rest(chip, other), rest(chip, other), near_sems.at[0, k], near_sems.at[1, k], place.sibling)
            for k, chip in enumerate(place.near_from)
        ]

    def send(self):
        for copy in self.sends + self.near + [self.own]:
            copy.start()

    def receive(self):
        for arrival, onward in zip(self.arrivals, self.passes):
            arrival.wait_recv()
            onward.start()
        for copy in self.arrivals[self.place.n_far:] + self.near_in + [self.own_in] + self.passed:
            copy.wait_recv()

    def drain(self):
        for copy in self.sends + self.near + [self.own] + self.passes:
            copy.wait_send()


def invert(work, out_ref):
    rank = work.shape[0]
    size = 8
    lanes = lax.broadcasted_iota(jnp.int32, (size, rank), 1)
    lane = lanes[0:1]
    for r in range(0, rank, size):
        row = [work[r + i:r + i + 1, :] for i in range(size)]
        a = [[jnp.broadcast_to(row[i][:, r + j:r + j + 1], (1, rank)) for j in range(i + 1)] for i in range(size)]
        inside = (lane >= r) & (lane < r + size)
        row = [jnp.where(inside, jnp.where(lane == r + i, 1.0, 0.0), row[i]) for i in range(size)]
        e = [[None] * size for _ in range(size)]
        pivot, recip = [], []
        for j in range(size):
            pivot.append(a[j][j])
            recip.append(1.0 / a[j][j])
            for i in range(j + 1, size):
                m = a[i][j] * recip[j]
                for k in range(j + 1, i + 1):
                    a[i][k] = a[i][k] - m * a[k][j]
                for k in range(j):
                    e[i][k] = e[i][k] - m * e[j][k]
                e[i][j] = -m
        z = []
        for i in range(size):
            t = row[i]
            for j in range(i):
                t = t + e[i][j] * row[j]
            z.append(t)
        y = []
        zq = [z[i] * recip[i] for i in range(size)]
        for i in range(size):
            t = zq[i]
            for k in range(i + 1, size):
                t = t + e[k][i] * zq[k]
            y.append(t)
        out = jnp.concatenate([z[i] * lax.rsqrt(pivot[i]) for i in range(size)], axis=0)
        out_ref[r:r + size, :] = jnp.where(lanes < r + size, out, 0.0)
        for s in range(r + size, rank, size):
            old = work[s:s + size, :]
            acc = jnp.where((lanes >= r) & (lanes < r + size), 0.0, old)
            for k in range(size):
                acc = acc - jnp.broadcast_to(old[:, r + k:r + k + 1], (size, rank)) * y[k]
            work[s:s + size, :] = acc


def mega_kernel(
    n_dp, n_mp,
    mom_hbm, tile_hbm, exps_hbm, prev_hbm, over_ref,
    ortho_ref, low_ref, inv_ref, share_ref, sum_ref,
    both, exps, scale, pair, right, both_t, flag_z, flag_p, left_t,
    part, left_in, left, left_hl, gram, gram_zc, gram_p, gram_all, work, tri,
    core_send, core_in, core_out, plane_in, mine, sq_z, sq_p,
    sem_in, sem_pair, sem_gather, sem_near, sem_fz, sem_fp, sem_lr, sem_lg, sem_gz, sem_gp, sem_gg,
    sem_core, sem_plane, sem_low, sem_pass, sem_low_near, sem_own, sem_sz, sem_sp,
):
    place = Place(n_dp, n_mp)
    rows, cols = mom_hbm.shape
    share, rank = share_ref.shape
    block = 2 * share
    my_share = pl.ds(pl.multiple_of(place.core * share, 8), share)
    loads = [
        pltpu.make_async_copy(src, dst, sem_in.at[k])
        for k, (src, dst) in enumerate(
            [
                (prev_hbm, pair.at[my_share]), (exps_hbm, exps),
                (mom_hbm, both.at[0:rows]), (tile_hbm, both.at[rows:2 * rows]),
            ]
        )
    ]
    for load in loads:
        load.start()
    barrier = pltpu.get_barrier_semaphore()
    friends = place.zc_peers[:-1] + place.plane_all
    for dev in friends:
        pl.semaphore_signal(barrier, inc=1, device_id=dev, device_id_type=MESH)
    kept = jnp.where(over_ref[0, 0] == 0, 1.0, 0.0).astype(F32)
    flag_z[place.z] = jnp.full((1, 128), kept, F32)
    loads[1].wait()
    scales = jnp.exp2(exps[...].astype(F32)).astype(BF16).astype(F32) * kept
    for j in range(cols // BLOCK):
        for b in range(rows // BLOCK):
            scale[b, :, j * BLOCK:(j + 1) * BLOCK] = jnp.broadcast_to(scales[b:b + 1, j:j + 1], (16, BLOCK)).astype(BF16)
    loads[0].wait()
    pl.semaphore_wait(barrier, len(friends))
    pending = []

    fz = exchange(place.z_peers, lambda k: flag_z.at[place.z], flag_z.at[place.z], sem_fz)
    pair_copy = remote(pair.at[my_share], pair.at[my_share], sem_pair.at[0], sem_pair.at[1], place.sibling)
    pair_copy.start()
    pair_copy.wait_recv()
    right[pl.ds(pl.multiple_of(place.chip * block, 16), block)] = pair[...].astype(BF16)
    gather = BlockGather(place, right, block, sem_gather, sem_near)
    gather.send()

    loads[2].wait()
    loads[3].wait()

    def decode(j, carry):
        at = pl.ds(pl.multiple_of(j * BLOCK, BLOCK), BLOCK)
        for b in range(rows // BLOCK):
            factor_of = scale[b, :, at]
            for r in range(rows + b * BLOCK, rows + (b + 1) * BLOCK, 16):
                both[r:r + 16, at] = both[r:r + 16, at] * factor_of
        return carry

    lax.fori_loop(0, cols // BLOCK, decode, 0)

    for copy in fz:
        copy.wait_recv()
    me = place.chip * 2 + place.core
    flag_p[me] = jnp.sum(flag_z[...], axis=0)
    fp = exchange(place.plane_all, lambda k: flag_p.at[me], flag_p.at[me], sem_fp)

    def transpose(j, carry):
        at = pl.ds(pl.multiple_of(j * BLOCK, BLOCK), BLOCK)
        both_t[at, :rows] = both[0:rows, at].T
        both_t[at, rows:] = both[rows:2 * rows, at].T
        return carry

    lax.fori_loop(0, cols // BLOCK, transpose, 0, unroll=2)

    def rows_of(chip):
        return pl.ds(pl.multiple_of(chip * block, 16), block)

    left_t[...] = jnp.zeros_like(left_t)

    def use(chip):
        at = rows_of(chip)
        left_t[...] += jnp.dot(right[at, :].T, both_t[at, :], preferred_element_type=F32)

    use(place.chip)
    gather.receive(use)
    for copy in fp:
        copy.wait_recv()
    healthy = jnp.sum(flag_p[...], axis=0)
    factor = float(n_dp * n_mp) / jnp.maximum(healthy, 1.0)
    pending += [pair_copy] + fz + fp
    for r in range(0, rows, BLOCK):
        part[r:r + BLOCK, :] = (left_t[:, r:r + BLOCK] + factor * left_t[:, rows + r:rows + r + BLOCK]).T

    rz = rows // place.nz
    lr = []
    for k, z in enumerate(place.zs):
        copy = remote(
            part.at[pl.ds(pl.multiple_of(z * rz, 8), rz)], left_in.at[k], sem_lr.at[0, k], sem_lr.at[1, k],
            place.z_peers[k],
        )
        copy.start()
        lr.append(copy)

    wide = jnp.broadcast_to(factor[:, 0:1], (16, BLOCK))

    def add(j, carry):
        at = pl.ds(pl.multiple_of(j * BLOCK, BLOCK), BLOCK)
        for r in range(0, rows, 16):
            sum_ref[r:r + 16, at] = both[r:r + 16, at].astype(F32) + wide * both[rows + r:rows + r + 16, at].astype(F32)
        return carry

    own = pl.ds(pl.multiple_of(place.z * rz, 8), rz)
    acc = part[own]
    for k, copy in enumerate(lr):
        copy.wait_recv()
        acc = acc + left_in[k]
    left[own] = acc
    pending += lr
    gram[...] = lax.dot_general(acc, acc, (((0,), (0,)), ((), ())), precision=HIGH, preferred_element_type=F32)
    gs = rank // (2 * place.nz)
    gz = []
    for k, spot in enumerate(place.zc_spots):
        copy = remote(
            gram.at[pl.ds(pl.multiple_of(spot * gs, 8), gs)], gram_zc.at[k], sem_gz.at[0, k], sem_gz.at[1, k],
            place.zc_peers[k],
        )
        copy.start()
        gz.append(copy)
    lg = exchange(place.z_peers, lambda k: left.at[own], left.at[own], sem_lg)
    lax.fori_loop(0, cols // BLOCK, add, 0)
    piece = pl.ds(pl.multiple_of((place.z * 2 + place.core) * gs, 8), gs)
    acc = gram[piece]
    for k, copy in enumerate(gz):
        copy.wait_recv()
        acc = acc + gram_zc[k]
    gram_p[place.chip] = acc
    gp = exchange(place.plane_peers, lambda k: gram_p.at[place.chip], gram_p.at[place.chip], sem_gp)
    for copy in lg:
        copy.wait_recv()
    pending += lg + gz

    high = left[...].astype(BF16)
    left_hl[:, :rank] = high
    left_hl[:, rank:] = (left[...] - high.astype(F32)).astype(BF16)
    window = share + -share % 16
    keep = block - window

    def raw_part(chip, core):
        at = pl.ds(pl.multiple_of(chip * block + core * keep, 16), window)
        mom_two = jnp.dot(both_t[at, :rows], left_hl[...], preferred_element_type=F32)
        grad_two = jnp.dot(both_t[at, rows:], left_hl[...], preferred_element_type=F32)
        return mom_two[:, :rank] + mom_two[:, rank:] + factor * (grad_two[:, :rank] + grad_two[:, rank:])

    chips = place.plane + [place.chip]
    chunk = len(chips) // 4
    core_copies = []
    for k, chip in enumerate(chips):
        core_send[k] = raw_part(chip, place.other)
        if k % chunk == chunk - 1:
            j = k // chunk
            at = pl.ds(j * chunk, chunk)
            copy = remote(core_send.at[at], core_in.at[at], sem_core.at[0, j], sem_core.at[1, j], place.sibling)
            copy.start()
            core_copies.append(copy)
    plane_copies = []

    def send_sums(first, last):
        for k in range(first, last):
            if k % chunk == 0:
                core_copies[k // chunk].wait_recv()
            core_out[k] = raw_part(chips[k], place.core) + core_in[k]
            copy = remote(core_out.at[k], plane_in.at[k], sem_plane.at[0, k], sem_plane.at[1, k], place.plane_peers[k])
            copy.start()
            plane_copies.append(copy)

    last = len(chips) - 1
    send_sums(0, 2 * chunk)
    for copy in gp:
        copy.wait_recv()
    gram_all[piece] = jnp.sum(gram_p[...], axis=0)
    gg = exchange(place.zc_peers, lambda k: gram_all.at[piece], gram_all.at[piece], sem_gg)
    send_sums(2 * chunk, last)
    if last % chunk == 0:
        core_copies[-1].wait_recv()
    total = raw_part(chips[last], place.core) + core_in[last]
    for copy in gg:
        copy.wait_recv()
    pending += gp + gg + core_copies + plane_copies
    work[...] = gram_all[...]
    invert(work, tri)
    for k, copy in enumerate(plane_copies):
        copy.wait_recv()
        total = total + plane_in[k]
    by_rank = (((1,), (1,)), ((), ()))
    total = lax.dot_general(total, tri[...], by_rank, precision=HIGH, preferred_element_type=F32)
    mine[...] = total
    own_share = mine[pl.ds(pl.multiple_of(place.core * (window - share), 8), share)]
    sq_z[place.z] = jnp.sum(own_share * own_share, axis=0, keepdims=True)
    sz = exchange(place.z_peers, lambda k: sq_z.at[place.z], sq_z.at[place.z], sem_sz)
    low_ref[pl.ds(pl.multiple_of(place.chip * block + place.core * keep, 16), window)] = total.astype(BF16)
    last_gather = WindowGather(place, low_ref, block, window, sem_low, sem_pass, sem_low_near, sem_own)
    last_gather.send()
    share_ref[...] = own_share
    ortho_ref[...] = lax.dot_general(
        left[...], tri[...], by_rank, precision=HIGH, preferred_element_type=F32
    ).astype(BF16)
    for copy in sz:
        copy.wait_recv()
    sq_p[me] = jnp.sum(sq_z[...], axis=0)
    sp = exchange(place.plane_all, lambda k: sq_p.at[me], sq_p.at[me], sem_sp)
    last_gather.receive()
    for copy in sp:
        copy.wait_recv()
    squares = jnp.sum(sq_p[...], axis=0)
    inv_ref[...] = jnp.broadcast_to(lax.rsqrt(squares + EPSILON), inv_ref.shape)
    for copy in pending + sz + sp:
        copy.wait_send()
    gather.drain()
    last_gather.drain()


def mega_stage(n_dp, n_mp, momentum, tile_values, exponents, right_prev, overflow):
    rows, cols = momentum.shape
    share, rank = right_prev.shape
    chips = n_mp // 2
    block = 2 * share
    window = share + -share % 16
    n_near = 4 if chips == 16 else 2
    n_far = chips - 1 - n_near
    vmem = pl.BlockSpec(memory_space=pltpu.VMEM)
    hbm = pl.BlockSpec(memory_space=pltpu.HBM)
    dma = pltpu.SemaphoreType.DMA
    return pl.pallas_call(
        functools.partial(mega_kernel, n_dp, n_mp),
        name="mega",
        out_shape=(
            jax.ShapeDtypeStruct((rows, rank), BF16),
            jax.ShapeDtypeStruct((cols, rank), BF16),
            jax.ShapeDtypeStruct((8, 128), F32),
            jax.ShapeDtypeStruct((share, rank), F32),
            jax.ShapeDtypeStruct((rows, cols), F32),
        ),
        in_specs=[hbm] * 4 + [pl.BlockSpec(memory_space=pltpu.SMEM)],
        out_specs=(vmem,) * 5,
        scratch_shapes=[
            pltpu.VMEM((2 * rows, cols), BF16),
            pltpu.VMEM(exponents.shape, jnp.int32),
            pltpu.VMEM((rows // BLOCK, 16, cols), BF16),
            pltpu.VMEM((block, rank), F32),
            pltpu.VMEM((cols, rank), BF16),
            pltpu.VMEM((cols, 2 * rows), BF16),
            pltpu.VMEM((n_dp, 1, 128), F32),
            pltpu.VMEM((n_mp, 1, 128), F32),
            pltpu.VMEM((rank, 2 * rows), F32),
            pltpu.VMEM((rows, rank), F32),
            pltpu.VMEM((n_dp - 1, rows // n_dp, rank), F32),
            pltpu.VMEM((rows, rank), F32),
            pltpu.VMEM((rows, 2 * rank), BF16),
            pltpu.VMEM((rank, rank), F32),
            pltpu.VMEM((2 * n_dp - 1, rank // (2 * n_dp), rank), F32),
            pltpu.VMEM((chips, rank // (2 * n_dp), rank), F32),
            pltpu.VMEM((rank, rank), F32),
            pltpu.VMEM((rank, rank), F32),
            pltpu.VMEM((rank, rank), F32),
            pltpu.VMEM((chips, window, rank), F32),
            pltpu.VMEM((chips, window, rank), F32),
            pltpu.VMEM((chips - 1, window, rank), F32),
            pltpu.VMEM((chips - 1, window, rank), F32),
            pltpu.VMEM((window, rank), F32),
            pltpu.VMEM((n_dp, 1, 128), F32),
            pltpu.VMEM((n_mp, 1, 128), F32),
            dma((4,)),
            dma((2,)),
            dma((4, (n_far + 1) // 2)),
            dma((2, n_near)),
            dma((2, n_dp - 1)),
            dma((2, n_mp - 1)),
            dma((2, n_dp - 1)),
            dma((2, n_dp - 1)),
            dma((2, 2 * n_dp - 1)),
            dma((2, chips - 1)),
            dma((2, 2 * n_dp - 1)),
            dma((2, 4)),
            dma((2, chips - 1)),
            dma((2, chips - 1)),
            dma((2, n_far)),
            dma((2, n_near)),
            dma((2,)),
            dma((2, n_dp - 1)),
            dma((2, n_mp - 1)),
        ],
        compiler_params=pltpu.CompilerParams(
            collective_id=0, has_side_effects=True, vmem_limit_bytes=VMEM_LIMIT
        ),
    )(momentum, tile_values, exponents, right_prev, overflow)


def finish_kernel(unit, sums, ortho, low, inv, share, new, upd, share_out, new_v, upd_v, sem):
    rows, cols = sums.shape
    step = 256
    base = ortho[...]
    scaled = (base.astype(F32) * inv[0:1, :]).astype(BF16)
    both = (((1,), (1,)), ((), ()))
    share_copy = pltpu.make_async_copy(share, share_out, sem.at[2, 0])
    share_copy.start()
    copies = [share_copy]
    for t in range(cols // step):
        at = slice(t * step, (t + 1) * step)
        piece = low[at, :]
        correction = lax.dot_general(base, piece, both, preferred_element_type=F32)
        new_v[:, at] = (sums[:, at] - (1.0 - RETAIN) * correction).astype(BF16)
        direction = lax.dot_general(scaled, piece, both, preferred_element_type=F32)
        upd_v[:, at] = (unit * direction).astype(BF16)
        for k, (src, dst) in enumerate([(new_v, new), (upd_v, upd)]):
            copy = pltpu.make_async_copy(src.at[:, at], dst.at[:, at], sem.at[k, t])
            copy.start()
            copies.append(copy)
    for copy in copies:
        copy.wait()


def finish_stage(unit, sums, ortho, low, inv, share):
    rows, cols = sums.shape
    vmem = pl.BlockSpec(memory_space=pltpu.VMEM)
    hbm = pl.BlockSpec(memory_space=pltpu.HBM)
    return pl.pallas_call(
        functools.partial(finish_kernel, unit),
        name="finish",
        out_shape=(
            jax.ShapeDtypeStruct((rows, cols), BF16),
            jax.ShapeDtypeStruct((rows, cols), BF16),
            jax.ShapeDtypeStruct(share.shape, F32),
        ),
        in_specs=[vmem] * 5,
        out_specs=(hbm,) * 3,
        scratch_shapes=[
            pltpu.VMEM((rows, cols), BF16),
            pltpu.VMEM((rows, cols), BF16),
            pltpu.SemaphoreType.DMA((3, cols // 256)),
        ],
        compiler_params=pltpu.CompilerParams(vmem_limit_bytes=VMEM_LIMIT),
    )(sums, ortho, low, inv, share)


def body(n_dp, n_mp, momentum, tile_values, exponents, overflow, right_prev):
    rows, cols = momentum.shape
    rank = right_prev.shape[1]
    unit = math.sqrt(rows * n_mp * cols * n_dp / rank)
    args = [
        pltpu.with_memory_space_constraint(a, pltpu.HBM)
        for a in (momentum, tile_values, exponents, right_prev)
    ]
    ortho, low, inv, own, sums = mega_stage(n_dp, n_mp, *args, overflow)
    new, update, right_out = finish_stage(unit, sums, ortho, low, inv, own)
    return new, right_out, update


def solution(mesh):
    in_specs = (P("mp", "dp"), P("mp", "dp"), P("mp", "dp"), P("mp", "dp"), P(("dp", "mp"), None))
    out_specs = (P("mp", "dp"), P(("dp", "mp"), None), P("mp", "dp"))
    step = functools.partial(body, mesh.shape["dp"], mesh.shape["mp"])
    return jax.shard_map(step, mesh=mesh, in_specs=in_specs, out_specs=out_specs, check_vma=False)
```

```python
import functools
import math

import jax
import jax.numpy as jnp
from jax import lax
from jax.experimental import pallas as pl
from jax.experimental.pallas import tpu as pltpu
from jax.sharding import PartitionSpec as P

MESH = pl.DeviceIdType.MESH
F32 = jnp.float32
BF16 = jnp.bfloat16
HIGH = lax.Precision.HIGHEST
BLOCK = 128
EPSILON = 1e-06
RETAIN = 0.95
VMEM_LIMIT = 32 * 1024 * 1024


def torus(a, n):
    return min(a % n, -a % n)


class Place:
    def __init__(self, n_dp, n_mp):
        self.nz = n_dp
        self.chips = n_mp // 2
        self.ny = int(round(math.sqrt(self.chips)))
        self.nx = self.chips // self.ny
        self.half = self.chips // 2
        mp = lax.axis_index("mp")
        self.z = lax.axis_index("dp")
        self.core = lax.rem(mp, 2)
        self.other = 1 - self.core
        self.chip = mp // 2
        x = self.chip // self.ny
        y = lax.rem(self.chip, self.ny)
        xs = [lax.rem(x + d, self.nx) * self.ny for d in range(self.nx)]
        ys = [lax.rem(y + d, self.ny) for d in range(self.ny)]
        offsets = sorted(
            ((dx, dy) for dx in range(self.nx) for dy in range(self.ny)),
            key=lambda o: -torus(o[0], self.nx) - torus(o[1], self.ny),
        )
        chips = {o: xs[o[0]] + ys[o[1]] for o in offsets}
        def away(offset):
            return torus(offset[0], self.nx) + torus(offset[1], self.ny)

        def back(offset):
            return chips[-offset[0] % self.nx, -offset[1] % self.ny]

        self.sibling = (self.z, self.chip * 2 + self.other)
        self.plane = [chips[o] for o in offsets[:-1]]
        self.plane_from = [back(o) for o in offsets[:-1]]
        far = [o for o in offsets if away(o) > 1]
        near = [o for o in offsets if away(o) == 1]
        self.n_far, self.n_near = len(far), len(near)
        odd = far[0::2]
        even = far[1::2] + odd[-1:]
        self.far_to = [jnp.where(self.core == 0, chips[a], chips[b]) for a, b in zip(even, odd)]
        self.far_from = [jnp.where(self.core == 0, back(a), back(b)) for a, b in zip(even, odd)]
        self.far_passed = [jnp.where(self.core == 0, back(b), back(a)) for a, b in zip(even, odd)]
        self.near_to = [chips[o] for o in near]
        self.near_from = [back(o) for o in near]
        self.plane_peers = [(self.z, chip * 2 + self.core) for chip in self.plane]
        self.plane_all = [(self.z, chip * 2 + core) for chip in self.plane for core in (self.core, self.other)] + [self.sibling]
        self.z_order = sorted(range(1, self.nz), key=lambda d: -torus(d, self.nz))
        self.zs = [lax.rem(self.z + d, self.nz) for d in self.z_order]
        self.z_peers = [(z, self.chip * 2 + self.core) for z in self.zs]
        self.zc_peers = [
            (z, self.chip * 2 + core) for z in self.zs for core in (self.core, self.other)
        ] + [self.sibling]
        self.zc_spots = [z * 2 + core for z in self.zs for core in (self.core, self.other)] + [self.z * 2 + self.other]

    def same_core(self, chip):
        return (self.z, chip * 2 + self.core)

    def other_core(self, chip):
        return (self.z, chip * 2 + self.other)


def remote(src, dst, send, recv, dev):
    return pltpu.make_async_remote_copy(
        src_ref=src, dst_ref=dst, send_sem=send, recv_sem=recv, device_id=dev, device_id_type=MESH
    )


def exchange(peers, src_of, dst, sems):
    for k, dev in enumerate(peers):
        remote(src_of(k), dst, sems.at[0], sems.at[1], dev).start()


def arrived(place, ref, sems):
    remote(ref, ref, sems.at[0], sems.at[1], place.sibling).wait_recv()


def sent(place, ref, sems):
    remote(ref, ref, sems.at[0], sems.at[1], place.sibling).wait_send()


class BlockGather:
    def __init__(self, place, buf, rows, sems):
        self.place = place

        def at(chip):
            return buf.at[pl.ds(pl.multiple_of(chip * rows, 16), rows)]

        self.buf, self.rows, self.sems = buf, rows, sems
        n = len(place.far_to)
        far_in, pass_in, near_in = 3, 3 + n, 3 + 2 * n
        mine = at(place.chip)
        self.far = [
            remote(mine, mine, sems.at[0], sems.at[far_in + i], place.same_core(chip))
            for i, chip in enumerate(place.far_to)
        ]
        self.arrivals = [
            remote(at(chip), at(chip), sems.at[0], sems.at[far_in + i], place.sibling)
            for i, chip in enumerate(place.far_from)
        ]
        self.passes = [
            remote(at(chip), at(chip), sems.at[1], sems.at[pass_in + i], place.sibling)
            for i, chip in enumerate(place.far_from)
        ]
        self.passed = [
            remote(at(chip), at(chip), sems.at[1], sems.at[pass_in + i], place.sibling)
            for i, chip in enumerate(place.far_passed)
        ]
        self.near = [
            remote(mine, mine, sems.at[2], sems.at[near_in + i], place.same_core(chip))
            for i, chip in enumerate(place.near_to)
        ]
        self.near_in = [
            remote(at(chip), at(chip), sems.at[2], sems.at[near_in + i], place.sibling)
            for i, chip in enumerate(place.near_from)
        ]

    def send(self):
        for copy in self.far[:-1]:
            copy.start()
        pl.when(self.place.core == 1)(self.far[-1].start)
        for copy in self.near:
            copy.start()

    def receive(self, use):
        place = self.place
        for arrival, onward, chip in list(zip(self.arrivals, self.passes, place.far_from))[:-1]:
            arrival.wait_recv()
            onward.start()
            use(chip)

        def go():
            self.arrivals[-1].wait_recv()
            self.passes[-1].start()

        pl.when(place.core == 1)(go)
        for copy, chip in zip(self.near_in, place.near_from):
            copy.wait_recv()
            use(chip)
        for copy, chip in list(zip(self.passed, place.far_passed))[:-1]:
            copy.wait_recv()
            use(chip)
        pl.when(place.core == 0)(self.passed[-1].wait_recv)
        use(jnp.where(place.core == 1, place.far_from[-1], place.far_passed[-1]))

    def drain(self):
        def left_here(which, count):
            ref = self.buf.at[pl.ds(0, count * self.rows)]
            remote(ref, ref, self.sems.at[which], self.sems.at[which], self.place.sibling).wait_send()

        left_here(2, len(self.near))

        def all_far(count):
            left_here(0, count)
            left_here(1, count)

        n = len(self.far)
        pl.when(self.place.core == 1)(lambda: all_far(n))
        if n > 1:
            pl.when(self.place.core == 0)(lambda: all_far(n - 1))


class WindowGather:
    def __init__(self, place, buf, block, window, sems):
        self.place = place
        keep = block - window

        def whole(chip):
            return buf.at[pl.ds(pl.multiple_of(chip * block + place.core * keep, 16), window)]

        def rest(chip, core):
            return buf.at[pl.ds(pl.multiple_of(chip * block + core * window, 16), keep)]

        self.buf, self.window, self.keep, self.sems = buf, window, keep, sems
        mine, lacking = whole(place.chip), rest(place.chip, place.core)
        first = 8
        far = place.plane_from[:place.n_far]
        self.copies = [
            remote(mine, mine, sems.at[0], sems.at[first + k if k < place.n_far else 7], dev)
            for k, dev in enumerate(place.plane_peers)
        ] + [
            remote(lacking, lacking, sems.at[3], sems.at[4], place.other_core(chip)) for chip in place.near_to
        ] + [remote(lacking, lacking, sems.at[5], sems.at[6], place.sibling)]
        self.arrivals = [
            remote(whole(chip), whole(chip), sems.at[0], sems.at[first + k], place.sibling)
            for k, chip in enumerate(far)
        ]
        self.passes = [
            remote(rest(chip, place.core), rest(chip, place.core), sems.at[1], sems.at[2], place.sibling)
            for chip in far
        ]

    def total(self, send, recv, rows):
        ref = self.buf.at[pl.ds(0, rows)]
        return remote(ref, ref, self.sems.at[send], self.sems.at[recv], self.place.sibling)

    def send(self):
        for copy in self.copies:
            copy.start()

    def receive(self):
        place = self.place
        for arrival, onward in zip(self.arrivals, self.passes):
            arrival.wait_recv()
            onward.start()
        self.total(0, 7, place.n_near * self.window).wait_recv()
        self.total(3, 4, place.n_near * self.keep).wait_recv()
        self.total(5, 6, self.keep).wait_recv()
        self.total(1, 2, place.n_far * self.keep).wait_recv()

    def drain(self):
        place = self.place
        self.total(0, 7, (place.n_far + place.n_near) * self.window).wait_send()
        self.total(1, 2, place.n_far * self.keep).wait_send()
        self.total(3, 4, place.n_near * self.keep).wait_send()
        self.total(5, 6, self.keep).wait_send()


def invert(work, out_ref):
    rank = work.shape[0]
    size = 8
    lanes = lax.broadcasted_iota(jnp.int32, (size, rank), 1)
    lane = lanes[0:1]
    for r in range(0, rank, size):
        row = [work[r + i:r + i + 1, :] for i in range(size)]
        a = [[jnp.broadcast_to(row[i][:, r + j:r + j + 1], (1, rank)) for j in range(i + 1)] for i in range(size)]
        inside = (lane >= r) & (lane < r + size)
        row = [jnp.where(inside, jnp.where(lane == r + i, 1.0, 0.0), row[i]) for i in range(size)]
        e = [[None] * size for _ in range(size)]
        pivot, recip = [], []
        for j in range(size):
            pivot.append(a[j][j])
            recip.append(1.0 / a[j][j])
            for i in range(j + 1, size):
                m = a[i][j] * recip[j]
                for k in range(j + 1, i + 1):
                    a[i][k] = a[i][k] - m * a[k][j]
                for k in range(j):
                    e[i][k] = e[i][k] - m * e[j][k]
                e[i][j] = -m
        z = []
        for i in range(size):
            t = row[i]
            for j in range(i):
                t = t + e[i][j] * row[j]
            z.append(t)
        y = []
        zq = [z[i] * recip[i] for i in range(size)]
        for i in range(size):
            t = zq[i]
            for k in range(i + 1, size):
                t = t + e[k][i] * zq[k]
            y.append(t)
        out = jnp.concatenate([z[i] * lax.rsqrt(pivot[i]) for i in range(size)], axis=0)
        out_ref[r:r + size, :] = jnp.where(lanes < r + size, out, 0.0)
        for s in range(r + size, rank, size):
            old = work[s:s + size, :]
            acc = jnp.where((lanes >= r) & (lanes < r + size), 0.0, old)
            for k in range(size):
                acc = acc - jnp.broadcast_to(old[:, r + k:r + k + 1], (size, rank)) * y[k]
            work[s:s + size, :] = acc


def mega_kernel(
    n_dp, n_mp,
    mom_hbm, tile_hbm, exps_hbm, prev_hbm, over_ref,
    ortho_ref, low_ref, inv_ref, share_ref, sum_ref,
    both, exps, scale, pair, right, both_t, flag_z, flag_p, left_t,
    part, left_in, left, left_hl, gram, gram_zc, gram_p, gram_all, work, tri,
    core_send, core_in, core_out, plane_in, mine, sq_z, sq_p,
    sem_in, sem_pair, sem_gather, sem_fz, sem_fp, sem_lr, sem_lg, sem_gz, sem_gp, sem_gg,
    sem_core, sem_plane, sem_low, sem_sz, sem_sp,
):
    place = Place(n_dp, n_mp)
    rows, cols = mom_hbm.shape
    share, rank = share_ref.shape
    block = 2 * share
    my_share = pl.ds(pl.multiple_of(place.core * share, 8), share)
    loads = [
        pltpu.make_async_copy(src, dst, sem_in.at[k])
        for k, (src, dst) in enumerate(
            [
                (prev_hbm, pair.at[my_share]), (exps_hbm, exps),
                (mom_hbm, both.at[0:rows]), (tile_hbm, both.at[rows:2 * rows]),
            ]
        )
    ]
    for load in loads:
        load.start()
    barrier = pltpu.get_barrier_semaphore()
    friends = place.zc_peers[:-1] + place.plane_all
    for dev in friends:
        pl.semaphore_signal(barrier, inc=1, device_id=dev, device_id_type=MESH)
    kept = jnp.where(over_ref[0, 0] == 0, 1.0, 0.0).astype(F32)
    flag_z[place.z] = jnp.full((1, 128), kept, F32)
    loads[1].wait()
    scales = jnp.exp2(exps[...].astype(F32)).astype(BF16).astype(F32) * kept
    for j in range(cols // BLOCK):
        for b in range(rows // BLOCK):
            scale[b, :, j * BLOCK:(j + 1) * BLOCK] = jnp.broadcast_to(scales[b:b + 1, j:j + 1], (16, BLOCK)).astype(BF16)
    loads[0].wait()
    pl.semaphore_wait(barrier, len(friends))

    exchange(place.z_peers, lambda k: flag_z.at[place.z], flag_z.at[place.z], sem_fz)
    pair_copy = remote(pair.at[my_share], pair.at[my_share], sem_pair.at[0], sem_pair.at[1], place.sibling)
    pair_copy.start()
    pair_copy.wait_recv()
    right[pl.ds(pl.multiple_of(place.chip * block, 16), block)] = pair[...].astype(BF16)
    gather = BlockGather(place, right, block, sem_gather)
    gather.send()

    loads[2].wait()
    loads[3].wait()

    def decode(j, carry):
        at = pl.ds(pl.multiple_of(j * BLOCK, BLOCK), BLOCK)
        for b in range(rows // BLOCK):
            factor_of = scale[b, :, at]
            for r in range(rows + b * BLOCK, rows + (b + 1) * BLOCK, 16):
                both[r:r + 16, at] = both[r:r + 16, at] * factor_of
        return carry

    lax.fori_loop(0, cols // BLOCK, decode, 0)

    all_z = flag_z.at[pl.ds(0, n_dp - 1)]
    arrived(place, all_z, sem_fz)
    me = place.chip * 2 + place.core
    flag_p[me] = jnp.sum(flag_z[...], axis=0)
    exchange(place.plane_all, lambda k: flag_p.at[me], flag_p.at[me], sem_fp)

    def transpose(j, carry):
        at = pl.ds(pl.multiple_of(j * BLOCK, BLOCK), BLOCK)
        both_t[at, :rows] = both[0:rows, at].T
        both_t[at, rows:] = both[rows:2 * rows, at].T
        return carry

    lax.fori_loop(0, cols // BLOCK, transpose, 0, unroll=2)

    def rows_of(chip):
        return pl.ds(pl.multiple_of(chip * block, 16), block)

    left_t[...] = jnp.zeros_like(left_t)

    def use(chip):
        at = rows_of(chip)
        left_t[...] += jnp.dot(right[at, :].T, both_t[at, :], preferred_element_type=F32)

    use(place.chip)
    gather.receive(use)
    all_p = flag_p.at[pl.ds(0, n_mp - 1)]
    arrived(place, all_p, sem_fp)
    healthy = jnp.sum(flag_p[...], axis=0)
    factor = float(n_dp * n_mp) / jnp.maximum(healthy, 1.0)
    for r in range(0, rows, BLOCK):
        part[r:r + BLOCK, :] = (left_t[:, r:r + BLOCK] + factor * left_t[:, rows + r:rows + r + BLOCK]).T

    rz = rows // place.nz
    for k, z in enumerate(place.zs):
        remote(
            part.at[pl.ds(pl.multiple_of(z * rz, 8), rz)], left_in.at[k], sem_lr.at[0], sem_lr.at[1],
            place.z_peers[k],
        ).start()

    wide = jnp.broadcast_to(factor[:, 0:1], (16, BLOCK))

    def add(j, carry):
        at = pl.ds(pl.multiple_of(j * BLOCK, BLOCK), BLOCK)
        for r in range(0, rows, 16):
            sum_ref[r:r + 16, at] = both[r:r + 16, at].astype(F32) + wide * both[rows + r:rows + r + 16, at].astype(F32)
        return carry

    own = pl.ds(pl.multiple_of(place.z * rz, 8), rz)
    acc = part[own]
    arrived(place, left_in, sem_lr)
    for k in range(n_dp - 1):
        acc = acc + left_in[k]
    left[own] = acc
    exchange(place.z_peers, lambda k: left.at[own], left.at[own], sem_lg)
    gram[...] = lax.dot_general(acc, acc, (((0,), (0,)), ((), ())), precision=HIGH, preferred_element_type=F32)
    gs = rank // (2 * place.nz)
    for k, spot in enumerate(place.zc_spots):
        remote(
            gram.at[pl.ds(pl.multiple_of(spot * gs, 8), gs)], gram_zc.at[k], sem_gz.at[0], sem_gz.at[1],
            place.zc_peers[k],
        ).start()
    lax.fori_loop(0, cols // BLOCK, add, 0)
    piece = pl.ds(pl.multiple_of((place.z * 2 + place.core) * gs, 8), gs)
    acc = gram[piece]
    arrived(place, gram_zc, sem_gz)
    for k in range(2 * n_dp - 1):
        acc = acc + gram_zc[k]
    gram_p[place.chip] = acc
    exchange(place.plane_peers, lambda k: gram_p.at[place.chip], gram_p.at[place.chip], sem_gp)
    all_left = left.at[pl.ds(0, rows - rz)]
    arrived(place, all_left, sem_lg)

    high = left[...].astype(BF16)
    left_hl[:, :rank] = high
    left_hl[:, rank:] = (left[...] - high.astype(F32)).astype(BF16)
    window = share + -share % 16
    keep = block - window

    def raw_part(chip, core):
        at = pl.ds(pl.multiple_of(chip * block + core * keep, 16), window)
        mom_two = jnp.dot(both_t[at, :rows], left_hl[...], preferred_element_type=F32)
        grad_two = jnp.dot(both_t[at, rows:], left_hl[...], preferred_element_type=F32)
        return mom_two[:, :rank] + mom_two[:, rank:] + factor * (grad_two[:, :rank] + grad_two[:, rank:])

    chips = place.plane + [place.chip]
    chunk = len(chips) // 4
    core_copies = []
    for k, chip in enumerate(chips):
        core_send[k] = raw_part(chip, place.other)
        if k % chunk == chunk - 1:
            j = k // chunk
            at = pl.ds(j * chunk, chunk)
            copy = remote(core_send.at[at], core_in.at[at], sem_core.at[0], sem_core.at[1 + j], place.sibling)
            copy.start()
            core_copies.append(copy)

    def send_sums(first, last):
        for k in range(first, last):
            if k % chunk == 0:
                core_copies[k // chunk].wait_recv()
            core_out[k] = raw_part(chips[k], place.core) + core_in[k]
            remote(core_out.at[k], plane_in.at[k], sem_plane.at[0], sem_plane.at[1], place.plane_peers[k]).start()

    last = len(chips) - 1
    send_sums(0, 2 * chunk)
    all_gp = gram_p.at[pl.ds(0, last)]
    arrived(place, all_gp, sem_gp)
    gram_all[piece] = jnp.sum(gram_p[...], axis=0)
    exchange(place.zc_peers, lambda k: gram_all.at[piece], gram_all.at[piece], sem_gg)
    send_sums(2 * chunk, last)
    if last % chunk == 0:
        core_copies[-1].wait_recv()
    total = raw_part(chips[last], place.core) + core_in[last]
    all_gram = gram_all.at[pl.ds(0, rank - gs)]
    arrived(place, all_gram, sem_gg)
    work[...] = gram_all[...]
    invert(work, tri)
    arrived(place, plane_in, sem_plane)
    for k in range(last):
        total = total + plane_in[k]
    by_rank = (((1,), (1,)), ((), ()))
    total = lax.dot_general(total, tri[...], by_rank, precision=HIGH, preferred_element_type=F32)
    mine[...] = total
    own_share = mine[pl.ds(pl.multiple_of(place.core * (window - share), 8), share)]
    sq_z[place.z] = jnp.sum(own_share * own_share, axis=0, keepdims=True)
    exchange(place.z_peers, lambda k: sq_z.at[place.z], sq_z.at[place.z], sem_sz)
    low_ref[pl.ds(pl.multiple_of(place.chip * block + place.core * keep, 16), window)] = total.astype(BF16)
    last_gather = WindowGather(place, low_ref, block, window, sem_low)
    last_gather.send()
    share_ref[...] = own_share
    ortho_ref[...] = lax.dot_general(
        left[...], tri[...], by_rank, precision=HIGH, preferred_element_type=F32
    ).astype(BF16)
    arrived(place, sq_z.at[pl.ds(0, n_dp - 1)], sem_sz)
    sq_p[me] = jnp.sum(sq_z[...], axis=0)
    exchange(place.plane_all, lambda k: sq_p.at[me], sq_p.at[me], sem_sp)
    last_gather.receive()
    arrived(place, sq_p.at[pl.ds(0, n_mp - 1)], sem_sp)
    squares = jnp.sum(sq_p[...], axis=0)
    inv_ref[...] = jnp.broadcast_to(lax.rsqrt(squares + EPSILON), inv_ref.shape)
    pair_copy.wait_send()
    for ref, sems in [
        (all_z, sem_fz), (all_p, sem_fp), (left_in, sem_lr), (all_left, sem_lg), (gram_zc, sem_gz), (all_gp, sem_gp),
        (all_gram, sem_gg), (plane_in, sem_plane), (core_send, sem_core),
        (sq_z.at[pl.ds(0, n_dp - 1)], sem_sz), (sq_p.at[pl.ds(0, n_mp - 1)], sem_sp),
    ]:
        sent(place, ref, sems)
    gather.drain()
    last_gather.drain()


def mega_stage(n_dp, n_mp, momentum, tile_values, exponents, right_prev, overflow):
    rows, cols = momentum.shape
    share, rank = right_prev.shape
    chips = n_mp // 2
    block = 2 * share
    window = share + -share % 16
    n_near = 4 if chips == 16 else 2
    n_far = chips - 1 - n_near
    vmem = pl.BlockSpec(memory_space=pltpu.VMEM)
    hbm = pl.BlockSpec(memory_space=pltpu.HBM)
    dma = pltpu.SemaphoreType.DMA
    return pl.pallas_call(
        functools.partial(mega_kernel, n_dp, n_mp),
        name="mega",
        out_shape=(
            jax.ShapeDtypeStruct((rows, rank), BF16),
            jax.ShapeDtypeStruct((cols, rank), BF16),
            jax.ShapeDtypeStruct((8, 128), F32),
            jax.ShapeDtypeStruct((share, rank), F32),
            jax.ShapeDtypeStruct((rows, cols), F32),
        ),
        in_specs=[hbm] * 4 + [pl.BlockSpec(memory_space=pltpu.SMEM)],
        out_specs=(vmem,) * 5,
        scratch_shapes=[
            pltpu.VMEM((2 * rows, cols), BF16),
            pltpu.VMEM(exponents.shape, jnp.int32),
            pltpu.VMEM((rows // BLOCK, 16, cols), BF16),
            pltpu.VMEM((block, rank), F32),
            pltpu.VMEM((cols, rank), BF16),
            pltpu.VMEM((cols, 2 * rows), BF16),
            pltpu.VMEM((n_dp, 1, 128), F32),
            pltpu.VMEM((n_mp, 1, 128), F32),
            pltpu.VMEM((rank, 2 * rows), F32),
            pltpu.VMEM((rows, rank), F32),
            pltpu.VMEM((n_dp - 1, rows // n_dp, rank), F32),
            pltpu.VMEM((rows, rank), F32),
            pltpu.VMEM((rows, 2 * rank), BF16),
            pltpu.VMEM((rank, rank), F32),
            pltpu.VMEM((2 * n_dp - 1, rank // (2 * n_dp), rank), F32),
            pltpu.VMEM((chips, rank // (2 * n_dp), rank), F32),
            pltpu.VMEM((rank, rank), F32),
            pltpu.VMEM((rank, rank), F32),
            pltpu.VMEM((rank, rank), F32),
            pltpu.VMEM((chips, window, rank), F32),
            pltpu.VMEM((chips, window, rank), F32),
            pltpu.VMEM((chips - 1, window, rank), F32),
            pltpu.VMEM((chips - 1, window, rank), F32),
            pltpu.VMEM((window, rank), F32),
            pltpu.VMEM((n_dp, 1, 128), F32),
            pltpu.VMEM((n_mp, 1, 128), F32),
            dma((4,)),
            dma((2,)),
            dma((3 + 2 * ((n_far + 1) // 2) + n_near,)),
            dma((2,)),
            dma((2,)),
            dma((2,)),
            dma((2,)),
            dma((2,)),
            dma((2,)),
            dma((2,)),
            dma((5,)),
            dma((2,)),
            dma((8 + n_far,)),
            dma((2,)),
            dma((2,)),
        ],
        compiler_params=pltpu.CompilerParams(
            collective_id=0, has_side_effects=True, vmem_limit_bytes=VMEM_LIMIT
        ),
    )(momentum, tile_values, exponents, right_prev, overflow)


def finish_kernel(unit, sums, ortho, low, inv, share, new, upd, share_out, new_v, upd_v, sem):
    rows, cols = sums.shape
    step = 256
    base = ortho[...]
    scaled = (base.astype(F32) * inv[0:1, :]).astype(BF16)
    both = (((1,), (1,)), ((), ()))
    share_copy = pltpu.make_async_copy(share, share_out, sem.at[2, 0])
    share_copy.start()
    copies = [share_copy]
    for t in range(cols // step):
        at = slice(t * step, (t + 1) * step)
        piece = low[at, :]
        correction = lax.dot_general(base, piece, both, preferred_element_type=F32)
        new_v[:, at] = (sums[:, at] - (1.0 - RETAIN) * correction).astype(BF16)
        direction = lax.dot_general(scaled, piece, both, preferred_element_type=F32)
        upd_v[:, at] = (unit * direction).astype(BF16)
        for k, (src, dst) in enumerate([(new_v, new), (upd_v, upd)]):
            copy = pltpu.make_async_copy(src.at[:, at], dst.at[:, at], sem.at[k, t])
            copy.start()
            copies.append(copy)
    for copy in copies:
        copy.wait()


def finish_stage(unit, sums, ortho, low, inv, share):
    rows, cols = sums.shape
    vmem = pl.BlockSpec(memory_space=pltpu.VMEM)
    hbm = pl.BlockSpec(memory_space=pltpu.HBM)
    return pl.pallas_call(
        functools.partial(finish_kernel, unit),
        name="finish",
        out_shape=(
            jax.ShapeDtypeStruct((rows, cols), BF16),
            jax.ShapeDtypeStruct((rows, cols), BF16),
            jax.ShapeDtypeStruct(share.shape, F32),
        ),
        in_specs=[vmem] * 5,
        out_specs=(hbm,) * 3,
        scratch_shapes=[
            pltpu.VMEM((rows, cols), BF16),
            pltpu.VMEM((rows, cols), BF16),
            pltpu.SemaphoreType.DMA((3, cols // 256)),
        ],
        compiler_params=pltpu.CompilerParams(vmem_limit_bytes=VMEM_LIMIT),
    )(sums, ortho, low, inv, share)


def body(n_dp, n_mp, momentum, tile_values, exponents, overflow, right_prev):
    rows, cols = momentum.shape
    rank = right_prev.shape[1]
    unit = math.sqrt(rows * n_mp * cols * n_dp / rank)
    args = [
        pltpu.with_memory_space_constraint(a, pltpu.HBM)
        for a in (momentum, tile_values, exponents, right_prev)
    ]
    ortho, low, inv, own, sums = mega_stage(n_dp, n_mp, *args, overflow)
    new, update, right_out = finish_stage(unit, sums, ortho, low, inv, own)
    return new, right_out, update


def solution(mesh):
    in_specs = (P("mp", "dp"), P("mp", "dp"), P("mp", "dp"), P("mp", "dp"), P(("dp", "mp"), None))
    out_specs = (P("mp", "dp"), P(("dp", "mp"), None), P("mp", "dp"))
    step = functools.partial(body, mesh.shape["dp"], mesh.shape["mp"])
    return jax.shard_map(step, mesh=mesh, in_specs=in_specs, out_specs=out_specs, check_vma=False)
```

```python
import functools
import math

import jax
import jax.numpy as jnp
from jax import lax
from jax.experimental import pallas as pl
from jax.experimental.pallas import tpu as pltpu
from jax.sharding import PartitionSpec as P

MESH = pl.DeviceIdType.MESH
F32 = jnp.float32
BF16 = jnp.bfloat16
HIGH = lax.Precision.HIGHEST
BLOCK = 128
EPSILON = 1e-06
RETAIN = 0.95
VMEM_LIMIT = 32 * 1024 * 1024


def torus(a, n):
    return min(a % n, -a % n)


class Place:
    def __init__(self, n_dp, n_mp):
        self.nz = n_dp
        self.chips = n_mp // 2
        self.ny = int(round(math.sqrt(self.chips)))
        self.nx = self.chips // self.ny
        self.half = self.chips // 2
        mp = lax.axis_index("mp")
        self.z = lax.axis_index("dp")
        self.core = lax.rem(mp, 2)
        self.other = 1 - self.core
        self.chip = mp // 2
        x = self.chip // self.ny
        y = lax.rem(self.chip, self.ny)
        xs = [lax.rem(x + d, self.nx) * self.ny for d in range(self.nx)]
        ys = [lax.rem(y + d, self.ny) for d in range(self.ny)]
        offsets = sorted(
            ((dx, dy) for dx in range(self.nx) for dy in range(self.ny)),
            key=lambda o: -torus(o[0], self.nx) - torus(o[1], self.ny),
        )
        chips = {o: xs[o[0]] + ys[o[1]] for o in offsets}
        def away(offset):
            return torus(offset[0], self.nx) + torus(offset[1], self.ny)

        def back(offset):
            return chips[-offset[0] % self.nx, -offset[1] % self.ny]

        self.sibling = (self.z, self.chip * 2 + self.other)
        self.plane = [chips[o] for o in offsets[:-1]]
        self.plane_from = [back(o) for o in offsets[:-1]]
        far = [o for o in offsets if away(o) > 1]
        near = [o for o in offsets if away(o) == 1]
        self.n_far, self.n_near = len(far), len(near)
        odd = far[0::2]
        even = far[1::2] + odd[-1:]
        self.far_to = [jnp.where(self.core == 0, chips[a], chips[b]) for a, b in zip(even, odd)]
        self.far_from = [jnp.where(self.core == 0, back(a), back(b)) for a, b in zip(even, odd)]
        self.far_passed = [jnp.where(self.core == 0, back(b), back(a)) for a, b in zip(even, odd)]
        self.near_to = [chips[o] for o in near]
        self.near_from = [back(o) for o in near]
        self.plane_peers = [(self.z, chip * 2 + self.core) for chip in self.plane]
        self.plane_all = [(self.z, chip * 2 + core) for chip in self.plane for core in (self.core, self.other)] + [self.sibling]
        self.z_order = sorted(range(1, self.nz), key=lambda d: -torus(d, self.nz))
        self.zs = [lax.rem(self.z + d, self.nz) for d in self.z_order]
        self.z_peers = [(z, self.chip * 2 + self.core) for z in self.zs]
        self.zc_peers = [
            (z, self.chip * 2 + core) for z in self.zs for core in (self.core, self.other)
        ] + [self.sibling]
        assert self.nx == self.ny
        self.steps = sorted(range(self.nx), key=lambda d: -torus(d, self.nx))

        def cross(core, a, b):
            return jnp.where(core == 0, chips[a, b], chips[b, a])

        self.group = [[cross(self.core, a, b) for b in range(self.nx)] for a in range(self.nx)]
        self.other_group = [[cross(self.other, a, b) for b in range(self.nx)] for a in range(self.nx)]
        self.step_one = [self.same_core(cross(self.core, a, 0)) for a in range(self.nx)]
        self.step_two = [self.same_core(cross(self.core, 0, a)) for a in range(self.nx)]
        self.zc_spots = [z * 2 + core for z in self.zs for core in (self.core, self.other)] + [self.z * 2 + self.other]

    def same_core(self, chip):
        return (self.z, chip * 2 + self.core)

    def other_core(self, chip):
        return (self.z, chip * 2 + self.other)


def remote(src, dst, send, recv, dev):
    return pltpu.make_async_remote_copy(
        src_ref=src, dst_ref=dst, send_sem=send, recv_sem=recv, device_id=dev, device_id_type=MESH
    )


def exchange(peers, src_of, dst, sems):
    for k, dev in enumerate(peers):
        remote(src_of(k), dst, sems.at[0], sems.at[1], dev).start()


def arrived(place, ref, sems):
    remote(ref, ref, sems.at[0], sems.at[1], place.sibling).wait_recv()


def sent(place, ref, sems):
    remote(ref, ref, sems.at[0], sems.at[1], place.sibling).wait_send()


class BlockGather:
    def __init__(self, place, buf, rows, sems):
        self.place = place

        def at(chip):
            return buf.at[pl.ds(pl.multiple_of(chip * rows, 16), rows)]

        self.buf, self.rows, self.sems = buf, rows, sems
        n = len(place.far_to)
        far_in, pass_in, near_in = 3, 3 + n, 3 + 2 * n
        mine = at(place.chip)
        self.far = [
            remote(mine, mine, sems.at[0], sems.at[far_in + i], place.same_core(chip))
            for i, chip in enumerate(place.far_to)
        ]
        self.arrivals = [
            remote(at(chip), at(chip), sems.at[0], sems.at[far_in + i], place.sibling)
            for i, chip in enumerate(place.far_from)
        ]
        self.passes = [
            remote(at(chip), at(chip), sems.at[1], sems.at[pass_in + i], place.sibling)
            for i, chip in enumerate(place.far_from)
        ]
        self.passed = [
            remote(at(chip), at(chip), sems.at[1], sems.at[pass_in + i], place.sibling)
            for i, chip in enumerate(place.far_passed)
        ]
        self.near = [
            remote(mine, mine, sems.at[2], sems.at[near_in + i], place.same_core(chip))
            for i, chip in enumerate(place.near_to)
        ]
        self.near_in = [
            remote(at(chip), at(chip), sems.at[2], sems.at[near_in + i], place.sibling)
            for i, chip in enumerate(place.near_from)
        ]

    def send(self):
        for copy in self.far[:-1]:
            copy.start()
        pl.when(self.place.core == 1)(self.far[-1].start)
        for copy in self.near:
            copy.start()

    def receive(self, use):
        place = self.place
        for arrival, onward, chip in list(zip(self.arrivals, self.passes, place.far_from))[:-1]:
            arrival.wait_recv()
            onward.start()
            use(chip)

        def go():
            self.arrivals[-1].wait_recv()
            self.passes[-1].start()

        pl.when(place.core == 1)(go)
        for copy, chip in zip(self.near_in, place.near_from):
            copy.wait_recv()
            use(chip)
        for copy, chip in list(zip(self.passed, place.far_passed))[:-1]:
            copy.wait_recv()
            use(chip)
        pl.when(place.core == 0)(self.passed[-1].wait_recv)
        use(jnp.where(place.core == 1, place.far_from[-1], place.far_passed[-1]))

    def drain(self):
        def left_here(which, count):
            ref = self.buf.at[pl.ds(0, count * self.rows)]
            remote(ref, ref, self.sems.at[which], self.sems.at[which], self.place.sibling).wait_send()

        left_here(2, len(self.near))

        def all_far(count):
            left_here(0, count)
            left_here(1, count)

        n = len(self.far)
        pl.when(self.place.core == 1)(lambda: all_far(n))
        if n > 1:
            pl.when(self.place.core == 0)(lambda: all_far(n - 1))


class WindowGather:
    def __init__(self, place, buf, block, window, sems):
        self.place = place
        keep = block - window

        def whole(chip):
            return buf.at[pl.ds(pl.multiple_of(chip * block + place.core * keep, 16), window)]

        def rest(chip, core):
            return buf.at[pl.ds(pl.multiple_of(chip * block + core * window, 16), keep)]

        self.buf, self.window, self.keep, self.sems = buf, window, keep, sems
        mine, lacking = whole(place.chip), rest(place.chip, place.core)
        first = 8
        far = place.plane_from[:place.n_far]
        self.copies = [
            remote(mine, mine, sems.at[0], sems.at[first + k if k < place.n_far else 7], dev)
            for k, dev in enumerate(place.plane_peers)
        ] + [
            remote(lacking, lacking, sems.at[3], sems.at[4], place.other_core(chip)) for chip in place.near_to
        ] + [remote(lacking, lacking, sems.at[5], sems.at[6], place.sibling)]
        self.arrivals = [
            remote(whole(chip), whole(chip), sems.at[0], sems.at[first + k], place.sibling)
            for k, chip in enumerate(far)
        ]
        self.passes = [
            remote(rest(chip, place.core), rest(chip, place.core), sems.at[1], sems.at[2], place.sibling)
            for chip in far
        ]

    def total(self, send, recv, rows):
        ref = self.buf.at[pl.ds(0, rows)]
        return remote(ref, ref, self.sems.at[send], self.sems.at[recv], self.place.sibling)

    def send(self):
        for copy in self.copies:
            copy.start()

    def receive(self):
        place = self.place
        for arrival, onward in zip(self.arrivals, self.passes):
            arrival.wait_recv()
            onward.start()
        self.total(0, 7, place.n_near * self.window).wait_recv()
        self.total(3, 4, place.n_near * self.keep).wait_recv()
        self.total(5, 6, self.keep).wait_recv()
        self.total(1, 2, place.n_far * self.keep).wait_recv()

    def drain(self):
        place = self.place
        self.total(0, 7, (place.n_far + place.n_near) * self.window).wait_send()
        self.total(1, 2, place.n_far * self.keep).wait_send()
        self.total(3, 4, place.n_near * self.keep).wait_send()
        self.total(5, 6, self.keep).wait_send()


def invert(work, out_ref):
    rank = work.shape[0]
    size = 8
    lanes = lax.broadcasted_iota(jnp.int32, (size, rank), 1)
    lane = lanes[0:1]
    for r in range(0, rank, size):
        row = [work[r + i:r + i + 1, :] for i in range(size)]
        a = [[jnp.broadcast_to(row[i][:, r + j:r + j + 1], (1, rank)) for j in range(i + 1)] for i in range(size)]
        inside = (lane >= r) & (lane < r + size)
        row = [jnp.where(inside, jnp.where(lane == r + i, 1.0, 0.0), row[i]) for i in range(size)]
        e = [[None] * size for _ in range(size)]
        pivot, recip = [], []
        for j in range(size):
            pivot.append(a[j][j])
            recip.append(1.0 / a[j][j])
            for i in range(j + 1, size):
                m = a[i][j] * recip[j]
                for k in range(j + 1, i + 1):
                    a[i][k] = a[i][k] - m * a[k][j]
                for k in range(j):
                    e[i][k] = e[i][k] - m * e[j][k]
                e[i][j] = -m
        z = []
        for i in range(size):
            t = row[i]
            for j in range(i):
                t = t + e[i][j] * row[j]
            z.append(t)
        y = []
        zq = [z[i] * recip[i] for i in range(size)]
        for i in range(size):
            t = zq[i]
            for k in range(i + 1, size):
                t = t + e[k][i] * zq[k]
            y.append(t)
        out = jnp.concatenate([z[i] * lax.rsqrt(pivot[i]) for i in range(size)], axis=0)
        out_ref[r:r + size, :] = jnp.where(lanes < r + size, out, 0.0)
        for s in range(r + size, rank, size):
            old = work[s:s + size, :]
            acc = jnp.where((lanes >= r) & (lanes < r + size), 0.0, old)
            for k in range(size):
                acc = acc - jnp.broadcast_to(old[:, r + k:r + k + 1], (size, rank)) * y[k]
            work[s:s + size, :] = acc


def mega_kernel(
    n_dp, n_mp,
    mom_hbm, tile_hbm, exps_hbm, prev_hbm, over_ref,
    ortho_ref, low_ref, inv_ref, share_ref, sum_ref,
    both, exps, scale, pair, right, both_t, flag_z, flag_p, left_t,
    part, left_in, left, left_hl, gram, gram_zc, gram_p, gram_all, work, tri,
    core_send, core_in, core_out, plane_in, step_out, step_in, mine, sq_z, sq_p,
    sem_in, sem_pair, sem_gather, sem_fz, sem_fp, sem_lr, sem_lg, sem_gz, sem_gp, sem_gg,
    sem_core, sem_plane, sem_step, sem_low, sem_sz, sem_sp,
):
    place = Place(n_dp, n_mp)
    rows, cols = mom_hbm.shape
    share, rank = share_ref.shape
    block = 2 * share
    my_share = pl.ds(pl.multiple_of(place.core * share, 8), share)
    loads = [
        pltpu.make_async_copy(src, dst, sem_in.at[k])
        for k, (src, dst) in enumerate(
            [
                (prev_hbm, pair.at[my_share]), (exps_hbm, exps),
                (mom_hbm, both.at[0:rows]), (tile_hbm, both.at[rows:2 * rows]),
            ]
        )
    ]
    for load in loads:
        load.start()
    barrier = pltpu.get_barrier_semaphore()
    friends = place.zc_peers[:-1] + place.plane_all
    for dev in friends:
        pl.semaphore_signal(barrier, inc=1, device_id=dev, device_id_type=MESH)
    kept = jnp.where(over_ref[0, 0] == 0, 1.0, 0.0).astype(F32)
    flag_z[place.z] = jnp.full((1, 128), kept, F32)
    loads[1].wait()
    scales = jnp.exp2(exps[...].astype(F32)).astype(BF16).astype(F32) * kept
    for j in range(cols // BLOCK):
        for b in range(rows // BLOCK):
            scale[b, :, j * BLOCK:(j + 1) * BLOCK] = jnp.broadcast_to(scales[b:b + 1, j:j + 1], (16, BLOCK)).astype(BF16)
    loads[0].wait()
    pl.semaphore_wait(barrier, len(friends))

    exchange(place.z_peers, lambda k: flag_z.at[place.z], flag_z.at[place.z], sem_fz)
    pair_copy = remote(pair.at[my_share], pair.at[my_share], sem_pair.at[0], sem_pair.at[1], place.sibling)
    pair_copy.start()
    pair_copy.wait_recv()
    right[pl.ds(pl.multiple_of(place.chip * block, 16), block)] = pair[...].astype(BF16)
    gather = BlockGather(place, right, block, sem_gather)
    gather.send()

    loads[2].wait()
    loads[3].wait()

    def decode(j, carry):
        at = pl.ds(pl.multiple_of(j * BLOCK, BLOCK), BLOCK)
        for b in range(rows // BLOCK):
            factor_of = scale[b, :, at]
            for r in range(rows + b * BLOCK, rows + (b + 1) * BLOCK, 16):
                both[r:r + 16, at] = both[r:r + 16, at] * factor_of
        return carry

    lax.fori_loop(0, cols // BLOCK, decode, 0)

    all_z = flag_z.at[pl.ds(0, n_dp - 1)]
    arrived(place, all_z, sem_fz)
    me = place.chip * 2 + place.core
    flag_p[me] = jnp.sum(flag_z[...], axis=0)
    exchange(place.plane_all, lambda k: flag_p.at[me], flag_p.at[me], sem_fp)

    def transpose(j, carry):
        at = pl.ds(pl.multiple_of(j * BLOCK, BLOCK), BLOCK)
        both_t[at, :rows] = both[0:rows, at].T
        both_t[at, rows:] = both[rows:2 * rows, at].T
        return carry

    lax.fori_loop(0, cols // BLOCK, transpose, 0, unroll=2)

    def rows_of(chip):
        return pl.ds(pl.multiple_of(chip * block, 16), block)

    left_t[...] = jnp.zeros_like(left_t)

    def use(chip):
        at = rows_of(chip)
        left_t[...] += jnp.dot(right[at, :].T, both_t[at, :], preferred_element_type=F32)

    use(place.chip)
    gather.receive(use)
    all_p = flag_p.at[pl.ds(0, n_mp - 1)]
    arrived(place, all_p, sem_fp)
    healthy = jnp.sum(flag_p[...], axis=0)
    factor = float(n_dp * n_mp) / jnp.maximum(healthy, 1.0)
    for r in range(0, rows, BLOCK):
        part[r:r + BLOCK, :] = (left_t[:, r:r + BLOCK] + factor * left_t[:, rows + r:rows + r + BLOCK]).T

    rz = rows // place.nz
    for k, z in enumerate(place.zs):
        remote(
            part.at[pl.ds(pl.multiple_of(z * rz, 8), rz)], left_in.at[k], sem_lr.at[0], sem_lr.at[1],
            place.z_peers[k],
        ).start()

    wide = jnp.broadcast_to(factor[:, 0:1], (16, BLOCK))

    def add(j, carry):
        at = pl.ds(pl.multiple_of(j * BLOCK, BLOCK), BLOCK)
        for r in range(0, rows, 16):
            sum_ref[r:r + 16, at] = both[r:r + 16, at].astype(F32) + wide * both[rows + r:rows + r + 16, at].astype(F32)
        return carry

    own = pl.ds(pl.multiple_of(place.z * rz, 8), rz)
    acc = part[own]
    arrived(place, left_in, sem_lr)
    for k in range(n_dp - 1):
        acc = acc + left_in[k]
    left[own] = acc
    exchange(place.z_peers, lambda k: left.at[own], left.at[own], sem_lg)
    gram[...] = lax.dot_general(acc, acc, (((0,), (0,)), ((), ())), precision=HIGH, preferred_element_type=F32)
    gs = rank // (2 * place.nz)
    for k, spot in enumerate(place.zc_spots):
        remote(
            gram.at[pl.ds(pl.multiple_of(spot * gs, 8), gs)], gram_zc.at[k], sem_gz.at[0], sem_gz.at[1],
            place.zc_peers[k],
        ).start()
    lax.fori_loop(0, cols // BLOCK, add, 0)
    piece = pl.ds(pl.multiple_of((place.z * 2 + place.core) * gs, 8), gs)
    acc = gram[piece]
    arrived(place, gram_zc, sem_gz)
    for k in range(2 * n_dp - 1):
        acc = acc + gram_zc[k]
    gram_p[place.chip] = acc
    exchange(place.plane_peers, lambda k: gram_p.at[place.chip], gram_p.at[place.chip], sem_gp)
    all_left = left.at[pl.ds(0, rows - rz)]
    arrived(place, all_left, sem_lg)

    high = left[...].astype(BF16)
    left_hl[:, :rank] = high
    left_hl[:, rank:] = (left[...] - high.astype(F32)).astype(BF16)
    window = share + -share % 16
    keep = block - window

    def raw_part(chip, core):
        at = pl.ds(pl.multiple_of(chip * block + core * keep, 16), window)
        mom_two = jnp.dot(both_t[at, :rows], left_hl[...], preferred_element_type=F32)
        grad_two = jnp.dot(both_t[at, rows:], left_hl[...], preferred_element_type=F32)
        return mom_two[:, :rank] + mom_two[:, rank:] + factor * (grad_two[:, :rank] + grad_two[:, rank:])

    core_copies = {}

    def for_sibling(a):
        for b, chip in enumerate(place.other_group[a]):
            core_send[a, b] = raw_part(chip, place.other)
        core_copies[a] = remote(core_send.at[a], core_in.at[a], sem_core.at[0], sem_core.at[1 + a], place.sibling)
        core_copies[a].start()

    def for_plane(a):
        parts = [raw_part(chip, place.core) for chip in place.group[a]]
        core_copies[a].wait_recv()
        for b, value in enumerate(parts):
            core_out[a, b] = value + core_in[a, b]
        if a:
            remote(core_out.at[a], plane_in.at[a - 1], sem_plane.at[0], sem_plane.at[1], place.step_one[a]).start()

    n_side = place.nx
    for_sibling(place.steps[0])
    for ahead, a in zip(place.steps[1:], place.steps):
        for_sibling(ahead)
        for_plane(a)
    last = place.chips - 1
    all_gp = gram_p.at[pl.ds(0, last)]
    arrived(place, all_gp, sem_gp)
    gram_all[piece] = jnp.sum(gram_p[...], axis=0)
    exchange(place.zc_peers, lambda k: gram_all.at[piece], gram_all.at[piece], sem_gg)
    for_plane(0)
    arrived(place, plane_in, sem_plane)
    for b in place.steps:
        total = core_out[0, b]
        for a in range(n_side - 1):
            total = total + plane_in[a, b]
        if b:
            step_out[b - 1] = total
            remote(step_out.at[b - 1], step_in.at[b - 1], sem_step.at[0], sem_step.at[1], place.step_two[b]).start()
    all_gram = gram_all.at[pl.ds(0, rank - gs)]
    arrived(place, all_gram, sem_gg)
    work[...] = gram_all[...]
    invert(work, tri)
    arrived(place, step_in, sem_step)
    for b in range(n_side - 1):
        total = total + step_in[b]
    by_rank = (((1,), (1,)), ((), ()))
    total = lax.dot_general(total, tri[...], by_rank, precision=HIGH, preferred_element_type=F32)
    mine[...] = total
    own_share = mine[pl.ds(pl.multiple_of(place.core * (window - share), 8), share)]
    sq_z[place.z] = jnp.sum(own_share * own_share, axis=0, keepdims=True)
    exchange(place.z_peers, lambda k: sq_z.at[place.z], sq_z.at[place.z], sem_sz)
    low_ref[pl.ds(pl.multiple_of(place.chip * block + place.core * keep, 16), window)] = total.astype(BF16)
    last_gather = WindowGather(place, low_ref, block, window, sem_low)
    last_gather.send()
    share_ref[...] = own_share
    ortho_ref[...] = lax.dot_general(
        left[...], tri[...], by_rank, precision=HIGH, preferred_element_type=F32
    ).astype(BF16)
    arrived(place, sq_z.at[pl.ds(0, n_dp - 1)], sem_sz)
    sq_p[me] = jnp.sum(sq_z[...], axis=0)
    exchange(place.plane_all, lambda k: sq_p.at[me], sq_p.at[me], sem_sp)
    last_gather.receive()
    arrived(place, sq_p.at[pl.ds(0, n_mp - 1)], sem_sp)
    squares = jnp.sum(sq_p[...], axis=0)
    inv_ref[...] = jnp.broadcast_to(lax.rsqrt(squares + EPSILON), inv_ref.shape)
    pair_copy.wait_send()
    for ref, sems in [
        (all_z, sem_fz), (all_p, sem_fp), (left_in, sem_lr), (all_left, sem_lg), (gram_zc, sem_gz), (all_gp, sem_gp),
        (all_gram, sem_gg), (plane_in, sem_plane), (step_in, sem_step), (core_send, sem_core),
        (sq_z.at[pl.ds(0, n_dp - 1)], sem_sz), (sq_p.at[pl.ds(0, n_mp - 1)], sem_sp),
    ]:
        sent(place, ref, sems)
    gather.drain()
    last_gather.drain()


def mega_stage(n_dp, n_mp, momentum, tile_values, exponents, right_prev, overflow):
    rows, cols = momentum.shape
    share, rank = right_prev.shape
    chips = n_mp // 2
    block = 2 * share
    window = share + -share % 16
    side = int(round(math.sqrt(chips)))
    n_near = 4 if side > 2 else 2
    n_far = chips - 1 - n_near
    vmem = pl.BlockSpec(memory_space=pltpu.VMEM)
    hbm = pl.BlockSpec(memory_space=pltpu.HBM)
    dma = pltpu.SemaphoreType.DMA
    return pl.pallas_call(
        functools.partial(mega_kernel, n_dp, n_mp),
        name="mega",
        out_shape=(
            jax.ShapeDtypeStruct((rows, rank), BF16),
            jax.ShapeDtypeStruct((cols, rank), BF16),
            jax.ShapeDtypeStruct((8, 128), F32),
            jax.ShapeDtypeStruct((share, rank), F32),
            jax.ShapeDtypeStruct((rows, cols), F32),
        ),
        in_specs=[hbm] * 4 + [pl.BlockSpec(memory_space=pltpu.SMEM)],
        out_specs=(vmem,) * 5,
        scratch_shapes=[
            pltpu.VMEM((2 * rows, cols), BF16),
            pltpu.VMEM(exponents.shape, jnp.int32),
            pltpu.VMEM((rows // BLOCK, 16, cols), BF16),
            pltpu.VMEM((block, rank), F32),
            pltpu.VMEM((cols, rank), BF16),
            pltpu.VMEM((cols, 2 * rows), BF16),
            pltpu.VMEM((n_dp, 1, 128), F32),
            pltpu.VMEM((n_mp, 1, 128), F32),
            pltpu.VMEM((rank, 2 * rows), F32),
            pltpu.VMEM((rows, rank), F32),
            pltpu.VMEM((n_dp - 1, rows // n_dp, rank), F32),
            pltpu.VMEM((rows, rank), F32),
            pltpu.VMEM((rows, 2 * rank), BF16),
            pltpu.VMEM((rank, rank), F32),
            pltpu.VMEM((2 * n_dp - 1, rank // (2 * n_dp), rank), F32),
            pltpu.VMEM((chips, rank // (2 * n_dp), rank), F32),
            pltpu.VMEM((rank, rank), F32),
            pltpu.VMEM((rank, rank), F32),
            pltpu.VMEM((rank, rank), F32),
            pltpu.VMEM((side, side, window, rank), F32),
            pltpu.VMEM((side, side, window, rank), F32),
            pltpu.VMEM((side, side, window, rank), F32),
            pltpu.VMEM((side - 1, side, window, rank), F32),
            pltpu.VMEM((side - 1, window, rank), F32),
            pltpu.VMEM((side - 1, window, rank), F32),
            pltpu.VMEM((window, rank), F32),
            pltpu.VMEM((n_dp, 1, 128), F32),
            pltpu.VMEM((n_mp, 1, 128), F32),
            dma((4,)),
            dma((2,)),
            dma((3 + 2 * ((n_far + 1) // 2) + n_near,)),
            dma((2,)),
            dma((2,)),
            dma((2,)),
            dma((2,)),
            dma((2,)),
            dma((2,)),
            dma((2,)),
            dma((1 + side,)),
            dma((2,)),
            dma((2,)),
            dma((8 + n_far,)),
            dma((2,)),
            dma((2,)),
        ],
        compiler_params=pltpu.CompilerParams(
            collective_id=0, has_side_effects=True, vmem_limit_bytes=VMEM_LIMIT
        ),
    )(momentum, tile_values, exponents, right_prev, overflow)


def finish_kernel(unit, sums, ortho, low, inv, share, new, upd, share_out, new_v, upd_v, sem):
    rows, cols = sums.shape
    step = 256
    base = ortho[...]
    scaled = (base.astype(F32) * inv[0:1, :]).astype(BF16)
    both = (((1,), (1,)), ((), ()))
    share_copy = pltpu.make_async_copy(share, share_out, sem.at[2])
    share_copy.start()
    for t in range(cols // step):
        at = slice(t * step, (t + 1) * step)
        piece = low[at, :]
        correction = lax.dot_general(base, piece, both, preferred_element_type=F32)
        new_v[:, at] = (sums[:, at] - (1.0 - RETAIN) * correction).astype(BF16)
        direction = lax.dot_general(scaled, piece, both, preferred_element_type=F32)
        upd_v[:, at] = (unit * direction).astype(BF16)
        for k, (src, dst) in enumerate([(new_v, new), (upd_v, upd)]):
            pltpu.make_async_copy(src.at[:, at], dst.at[:, at], sem.at[k]).start()
    share_copy.wait()
    for k, (src, dst) in enumerate([(new_v, new), (upd_v, upd)]):
        pltpu.make_async_copy(src, dst, sem.at[k]).wait()


def finish_stage(unit, sums, ortho, low, inv, share):
    rows, cols = sums.shape
    vmem = pl.BlockSpec(memory_space=pltpu.VMEM)
    hbm = pl.BlockSpec(memory_space=pltpu.HBM)
    return pl.pallas_call(
        functools.partial(finish_kernel, unit),
        name="finish",
        out_shape=(
            jax.ShapeDtypeStruct((rows, cols), BF16),
            jax.ShapeDtypeStruct((rows, cols), BF16),
            jax.ShapeDtypeStruct(share.shape, F32),
        ),
        in_specs=[vmem] * 5,
        out_specs=(hbm,) * 3,
        scratch_shapes=[
            pltpu.VMEM((rows, cols), BF16),
            pltpu.VMEM((rows, cols), BF16),
            pltpu.SemaphoreType.DMA((3,)),
        ],
        compiler_params=pltpu.CompilerParams(vmem_limit_bytes=VMEM_LIMIT),
    )(sums, ortho, low, inv, share)


def body(n_dp, n_mp, momentum, tile_values, exponents, overflow, right_prev):
    rows, cols = momentum.shape
    rank = right_prev.shape[1]
    unit = math.sqrt(rows * n_mp * cols * n_dp / rank)
    args = [
        pltpu.with_memory_space_constraint(a, pltpu.HBM)
        for a in (momentum, tile_values, exponents, right_prev)
    ]
    ortho, low, inv, own, sums = mega_stage(n_dp, n_mp, *args, overflow)
    new, update, right_out = finish_stage(unit, sums, ortho, low, inv, own)
    return new, right_out, update


def solution(mesh):
    in_specs = (P("mp", "dp"), P("mp", "dp"), P("mp", "dp"), P("mp", "dp"), P(("dp", "mp"), None))
    out_specs = (P("mp", "dp"), P(("dp", "mp"), None), P("mp", "dp"))
    step = functools.partial(body, mesh.shape["dp"], mesh.shape["mp"])
    return jax.shard_map(step, mesh=mesh, in_specs=in_specs, out_specs=out_specs, check_vma=False)
```

```python
import functools
import math

import jax
import jax.numpy as jnp
from jax import lax
from jax.experimental import pallas as pl
from jax.experimental.pallas import tpu as pltpu
from jax.sharding import PartitionSpec as P

MESH = pl.DeviceIdType.MESH
F32 = jnp.float32
BF16 = jnp.bfloat16
HIGH = lax.Precision.HIGHEST
BLOCK = 128
EPSILON = 1e-06
RETAIN = 0.95
VMEM_LIMIT = 32 * 1024 * 1024


def torus(a, n):
    return min(a % n, -a % n)


class Place:
    def __init__(self, n_dp, n_mp):
        self.nz = n_dp
        self.chips = n_mp // 2
        self.ny = int(round(math.sqrt(self.chips)))
        self.nx = self.chips // self.ny
        self.half = self.chips // 2
        mp = lax.axis_index("mp")
        self.z = lax.axis_index("dp")
        self.core = lax.rem(mp, 2)
        self.other = 1 - self.core
        self.chip = mp // 2
        x = self.chip // self.ny
        y = lax.rem(self.chip, self.ny)
        xs = [lax.rem(x + d, self.nx) * self.ny for d in range(self.nx)]
        ys = [lax.rem(y + d, self.ny) for d in range(self.ny)]
        offsets = sorted(
            ((dx, dy) for dx in range(self.nx) for dy in range(self.ny)),
            key=lambda o: -torus(o[0], self.nx) - torus(o[1], self.ny),
        )
        chips = {o: xs[o[0]] + ys[o[1]] for o in offsets}
        def away(offset):
            return torus(offset[0], self.nx) + torus(offset[1], self.ny)

        def back(offset):
            return chips[-offset[0] % self.nx, -offset[1] % self.ny]

        self.sibling = (self.z, self.chip * 2 + self.other)
        self.plane = [chips[o] for o in offsets[:-1]]
        self.plane_from = [back(o) for o in offsets[:-1]]
        far = [o for o in offsets if away(o) > 1]
        near = [o for o in offsets if away(o) == 1]
        self.n_far, self.n_near = len(far), len(near)
        self.near_to = [chips[o] for o in near]
        self.near_from = [back(o) for o in near]
        self.plane_peers = [(self.z, chip * 2 + self.core) for chip in self.plane]
        self.plane_all = [(self.z, chip * 2 + core) for chip in self.plane for core in (self.core, self.other)] + [self.sibling]
        self.z_order = sorted(range(1, self.nz), key=lambda d: -torus(d, self.nz))
        self.zs = [lax.rem(self.z + d, self.nz) for d in self.z_order]
        self.z_peers = [(z, self.chip * 2 + self.core) for z in self.zs]
        self.zc_peers = [
            (z, self.chip * 2 + core) for z in self.zs for core in (self.core, self.other)
        ] + [self.sibling]
        assert self.nx == self.ny
        self.steps = sorted(range(self.nx), key=lambda d: -torus(d, self.nx))

        def cross(core, a, b):
            return jnp.where(core == 0, chips[a, b], chips[b, a])

        self.group = [[cross(self.core, a, b) for b in range(self.nx)] for a in range(self.nx)]
        self.other_group = [[cross(self.other, a, b) for b in range(self.nx)] for a in range(self.nx)]
        self.step_one = [self.same_core(cross(self.core, a, 0)) for a in range(self.nx)]
        self.step_two = [self.same_core(cross(self.core, 0, a)) for a in range(self.nx)]
        self.zc_spots = [z * 2 + core for z in self.zs for core in (self.core, self.other)] + [self.z * 2 + self.other]

    def same_core(self, chip):
        return (self.z, chip * 2 + self.core)

    def other_core(self, chip):
        return (self.z, chip * 2 + self.other)


def remote(src, dst, send, recv, dev):
    return pltpu.make_async_remote_copy(
        src_ref=src, dst_ref=dst, send_sem=send, recv_sem=recv, device_id=dev, device_id_type=MESH
    )


def exchange(peers, src_of, dst, sems):
    for k, dev in enumerate(peers):
        remote(src_of(k), dst, sems.at[0], sems.at[1], dev).start()


def arrived(place, ref, sems):
    remote(ref, ref, sems.at[0], sems.at[1], place.sibling).wait_recv()


def sent(place, ref, sems):
    remote(ref, ref, sems.at[0], sems.at[1], place.sibling).wait_send()


class WindowGather:
    def __init__(self, place, buf, block, window, sems):
        self.place = place
        keep = block - window

        def whole(chip):
            return buf.at[pl.ds(pl.multiple_of(chip * block + place.core * keep, 16), window)]

        def rest(chip, core):
            return buf.at[pl.ds(pl.multiple_of(chip * block + core * window, 16), keep)]

        self.buf, self.window, self.keep, self.sems = buf, window, keep, sems
        mine, lacking = whole(place.chip), rest(place.chip, place.core)
        far = place.plane_from[:place.n_far]
        first, onward = 7, 7 + place.n_far
        self.copies = [
            remote(mine, mine, sems.at[0], sems.at[first + k if k < place.n_far else 6], dev)
            for k, dev in enumerate(place.plane_peers)
        ] + [
            remote(lacking, lacking, sems.at[2], sems.at[3], place.other_core(chip)) for chip in place.near_to
        ] + [remote(lacking, lacking, sems.at[4], sems.at[5], place.sibling)]
        self.arrivals = [
            remote(whole(chip), whole(chip), sems.at[0], sems.at[first + k], place.sibling)
            for k, chip in enumerate(far)
        ]
        self.passes = [
            remote(rest(chip, place.core), rest(chip, place.core), sems.at[1], sems.at[onward + k], place.sibling)
            for k, chip in enumerate(far)
        ]
        self.passed = [
            remote(rest(chip, place.other), rest(chip, place.other), sems.at[1], sems.at[onward + k], place.sibling)
            for k, chip in enumerate(far)
        ]

    def total(self, send, recv, rows):
        ref = self.buf.at[pl.ds(0, rows)]
        return remote(ref, ref, self.sems.at[send], self.sems.at[recv], self.place.sibling)

    def send(self):
        for copy in self.copies:
            copy.start()

    def receive(self, use=None):
        place = self.place
        for arrival, onward in zip(self.arrivals, self.passes):
            arrival.wait_recv()
            onward.start()
        self.total(0, 6, place.n_near * self.window).wait_recv()
        self.total(2, 3, place.n_near * self.keep).wait_recv()
        self.total(4, 5, self.keep).wait_recv()
        if use is not None:
            for chip in [place.chip] + place.near_from:
                use(chip)
        for copy, chip in zip(self.passed, place.plane_from):
            copy.wait_recv()
            if use is not None:
                use(chip)

    def drain(self):
        place = self.place
        self.total(0, 6, (place.n_far + place.n_near) * self.window).wait_send()
        self.total(1, 6, place.n_far * self.keep).wait_send()
        self.total(2, 3, place.n_near * self.keep).wait_send()
        self.total(4, 5, self.keep).wait_send()


def invert(work, out_ref):
    rank = work.shape[0]
    size = 8
    lanes = lax.broadcasted_iota(jnp.int32, (size, rank), 1)
    lane = lanes[0:1]
    for r in range(0, rank, size):
        row = [work[r + i:r + i + 1, :] for i in range(size)]
        a = [[jnp.broadcast_to(row[i][:, r + j:r + j + 1], (1, rank)) for j in range(i + 1)] for i in range(size)]
        inside = (lane >= r) & (lane < r + size)
        row = [jnp.where(inside, jnp.where(lane == r + i, 1.0, 0.0), row[i]) for i in range(size)]
        e = [[None] * size for _ in range(size)]
        pivot, recip = [], []
        for j in range(size):
            pivot.append(a[j][j])
            recip.append(1.0 / a[j][j])
            for i in range(j + 1, size):
                m = a[i][j] * recip[j]
                for k in range(j + 1, i + 1):
                    a[i][k] = a[i][k] - m * a[k][j]
                for k in range(j):
                    e[i][k] = e[i][k] - m * e[j][k]
                e[i][j] = -m
        z = []
        for i in range(size):
            t = row[i]
            for j in range(i):
                t = t + e[i][j] * row[j]
            z.append(t)
        y = []
        zq = [z[i] * recip[i] for i in range(size)]
        for i in range(size):
            t = zq[i]
            for k in range(i + 1, size):
                t = t + e[k][i] * zq[k]
            y.append(t)
        out = jnp.concatenate([z[i] * lax.rsqrt(pivot[i]) for i in range(size)], axis=0)
        out_ref[r:r + size, :] = jnp.where(lanes < r + size, out, 0.0)
        for s in range(r + size, rank, size):
            old = work[s:s + size, :]
            acc = jnp.where((lanes >= r) & (lanes < r + size), 0.0, old)
            for k in range(size):
                acc = acc - jnp.broadcast_to(old[:, r + k:r + k + 1], (size, rank)) * y[k]
            work[s:s + size, :] = acc


def mega_kernel(
    n_dp, n_mp,
    mom_hbm, tile_hbm, exps_hbm, prev_hbm, over_ref,
    ortho_ref, low_ref, inv_ref, share_ref, sum_ref,
    both, exps, scale, prev, right, both_t, flag_z, flag_p, left_t,
    part, left_in, left, left_hl, gram, gram_zc, gram_p, gram_all, work, tri,
    core_send, core_in, core_out, plane_in, step_out, step_in, mine, sq_z, sq_p,
    sem_in, sem_gather, sem_fz, sem_fp, sem_lr, sem_lg, sem_gz, sem_gp, sem_gg,
    sem_core, sem_plane, sem_step, sem_low, sem_sz, sem_sp,
):
    place = Place(n_dp, n_mp)
    rows, cols = mom_hbm.shape
    share, rank = share_ref.shape
    block = 2 * share
    window = share + -share % 16
    keep = block - window
    loads = [
        pltpu.make_async_copy(src, dst, sem_in.at[k])
        for k, (src, dst) in enumerate(
            [
                (prev_hbm, prev), (exps_hbm, exps),
                (mom_hbm, both.at[0:rows]), (tile_hbm, both.at[rows:2 * rows]),
            ]
        )
    ]
    for load in loads:
        load.start()
    barrier = pltpu.get_barrier_semaphore()
    friends = place.zc_peers[:-1] + place.plane_all
    for dev in friends:
        pl.semaphore_signal(barrier, inc=1, device_id=dev, device_id_type=MESH)
    kept = jnp.where(over_ref[0, 0] == 0, 1.0, 0.0).astype(F32)
    flag_z[place.z] = jnp.full((1, 128), kept, F32)
    loads[1].wait()
    scales = jnp.exp2(exps[...].astype(F32)).astype(BF16).astype(F32) * kept
    for j in range(cols // BLOCK):
        for b in range(rows // BLOCK):
            scale[b, :, j * BLOCK:(j + 1) * BLOCK] = jnp.broadcast_to(scales[b:b + 1, j:j + 1], (16, BLOCK)).astype(BF16)
    loads[0].wait()
    gather = WindowGather(place, right, 2 * window, window, sem_gather)
    mine_low = prev[...].astype(BF16).astype(F32)
    if window > share:
        mine_low = jnp.concatenate([mine_low, jnp.zeros((window - share, rank), F32)], axis=0)
    me = place.chip * 2 + place.core
    right[pl.ds(pl.multiple_of(me * window, 16), window)] = mine_low.astype(BF16)
    pl.semaphore_wait(barrier, len(friends))

    exchange(place.z_peers, lambda k: flag_z.at[place.z], flag_z.at[place.z], sem_fz)
    gather.send()

    loads[2].wait()
    loads[3].wait()

    def decode(j, carry):
        at = pl.ds(pl.multiple_of(j * BLOCK, BLOCK), BLOCK)
        for b in range(rows // BLOCK):
            factor_of = scale[b, :, at]
            for r in range(rows + b * BLOCK, rows + (b + 1) * BLOCK, 16):
                both[r:r + 16, at] = both[r:r + 16, at] * factor_of
        return carry

    lax.fori_loop(0, cols // BLOCK, decode, 0)

    all_z = flag_z.at[pl.ds(0, n_dp - 1)]
    arrived(place, all_z, sem_fz)
    flag_p[me] = jnp.sum(flag_z[...], axis=0)
    exchange(place.plane_all, lambda k: flag_p.at[me], flag_p.at[me], sem_fp)

    def transpose(j, carry):
        at = pl.ds(pl.multiple_of(j * BLOCK, BLOCK), BLOCK)
        both_t[at, :rows] = both[0:rows, at].T
        both_t[at, rows:] = both[rows:2 * rows, at].T
        return carry

    lax.fori_loop(0, cols // BLOCK, transpose, 0, unroll=2)

    def rows_of(chip):
        return pl.ds(pl.multiple_of(chip * block, 16), block)

    left_t[...] = jnp.zeros_like(left_t)

    def use(chip):
        got = right[pl.ds(pl.multiple_of(chip * 2 * window, 16), 2 * window), :].astype(F32)
        got = jnp.concatenate([got[:share], got[window:window + share]], axis=0).astype(BF16)
        left_t[...] += jnp.dot(got.T, both_t[rows_of(chip), :], preferred_element_type=F32)

    gather.receive(use)
    all_p = flag_p.at[pl.ds(0, n_mp - 1)]
    arrived(place, all_p, sem_fp)
    healthy = jnp.sum(flag_p[...], axis=0)
    factor = float(n_dp * n_mp) / jnp.maximum(healthy, 1.0)
    for r in range(0, rows, BLOCK):
        part[r:r + BLOCK, :] = (left_t[:, r:r + BLOCK] + factor * left_t[:, rows + r:rows + r + BLOCK]).T

    rz = rows // place.nz
    for k, z in enumerate(place.zs):
        remote(
            part.at[pl.ds(pl.multiple_of(z * rz, 8), rz)], left_in.at[k], sem_lr.at[0], sem_lr.at[1],
            place.z_peers[k],
        ).start()

    wide = jnp.broadcast_to(factor[:, 0:1], (16, BLOCK))

    def add(j, carry):
        at = pl.ds(pl.multiple_of(j * BLOCK, BLOCK), BLOCK)
        for r in range(0, rows, 16):
            sum_ref[r:r + 16, at] = both[r:r + 16, at].astype(F32) + wide * both[rows + r:rows + r + 16, at].astype(F32)
        return carry

    own = pl.ds(pl.multiple_of(place.z * rz, 8), rz)
    acc = part[own]
    arrived(place, left_in, sem_lr)
    for k in range(n_dp - 1):
        acc = acc + left_in[k]
    left[own] = acc
    gram[...] = lax.dot_general(acc, acc, (((0,), (0,)), ((), ())), precision=HIGH, preferred_element_type=F32)
    gs = rank // (2 * place.nz)
    for k, spot in enumerate(place.zc_spots):
        remote(
            gram.at[pl.ds(pl.multiple_of(spot * gs, 8), gs)], gram_zc.at[k], sem_gz.at[0], sem_gz.at[1],
            place.zc_peers[k],
        ).start()
    exchange(place.z_peers, lambda k: left.at[own], left.at[own], sem_lg)
    lax.fori_loop(0, cols // BLOCK, add, 0)
    piece = pl.ds(pl.multiple_of((place.z * 2 + place.core) * gs, 8), gs)
    acc = gram[piece]
    arrived(place, gram_zc, sem_gz)
    for k in range(2 * n_dp - 1):
        acc = acc + gram_zc[k]
    gram_p[place.chip] = acc
    exchange(place.plane_peers, lambda k: gram_p.at[place.chip], gram_p.at[place.chip], sem_gp)
    all_left = left.at[pl.ds(0, rows - rz)]
    arrived(place, all_left, sem_lg)

    high = left[...].astype(BF16)
    left_hl[:, :rank] = high
    left_hl[:, rank:] = (left[...] - high.astype(F32)).astype(BF16)
    def raw_part(chip, core):
        at = pl.ds(pl.multiple_of(chip * block + core * keep, 16), window)
        mom_two = jnp.dot(both_t[at, :rows], left_hl[...], preferred_element_type=F32)
        grad_two = jnp.dot(both_t[at, rows:], left_hl[...], preferred_element_type=F32)
        return mom_two[:, :rank] + mom_two[:, rank:] + factor * (grad_two[:, :rank] + grad_two[:, rank:])

    core_copies = {}

    def for_sibling(a):
        for b, chip in enumerate(place.other_group[a]):
            core_send[a, b] = raw_part(chip, place.other)
        core_copies[a] = remote(core_send.at[a], core_in.at[a], sem_core.at[0], sem_core.at[1 + a], place.sibling)
        core_copies[a].start()

    def for_plane(a):
        parts = [raw_part(chip, place.core) for chip in place.group[a]]
        core_copies[a].wait_recv()
        for b, value in enumerate(parts):
            core_out[a, b] = value + core_in[a, b]
        if a:
            remote(core_out.at[a], plane_in.at[a - 1], sem_plane.at[0], sem_plane.at[1], place.step_one[a]).start()

    n_side = place.nx
    for_sibling(place.steps[0])
    for ahead, a in zip(place.steps[1:], place.steps):
        for_sibling(ahead)
        for_plane(a)
    last = place.chips - 1
    all_gp = gram_p.at[pl.ds(0, last)]
    arrived(place, all_gp, sem_gp)
    gram_all[piece] = jnp.sum(gram_p[...], axis=0)
    exchange(place.zc_peers, lambda k: gram_all.at[piece], gram_all.at[piece], sem_gg)
    for_plane(0)
    arrived(place, plane_in, sem_plane)
    for b in place.steps:
        total = core_out[0, b]
        for a in range(n_side - 1):
            total = total + plane_in[a, b]
        if b:
            step_out[b - 1] = total
            remote(step_out.at[b - 1], step_in.at[b - 1], sem_step.at[0], sem_step.at[1], place.step_two[b]).start()
    all_gram = gram_all.at[pl.ds(0, rank - gs)]
    arrived(place, all_gram, sem_gg)
    work[...] = gram_all[...]
    invert(work, tri)
    arrived(place, step_in, sem_step)
    for b in range(n_side - 1):
        total = total + step_in[b]
    by_rank = (((1,), (1,)), ((), ()))
    total = lax.dot_general(total, tri[...], by_rank, precision=HIGH, preferred_element_type=F32)
    mine[...] = total
    own_share = mine[pl.ds(pl.multiple_of(place.core * (window - share), 8), share)]
    sq_z[place.z] = jnp.sum(own_share * own_share, axis=0, keepdims=True)
    exchange(place.z_peers, lambda k: sq_z.at[place.z], sq_z.at[place.z], sem_sz)
    low_ref[pl.ds(pl.multiple_of(place.chip * block + place.core * keep, 16), window)] = total.astype(BF16)
    last_gather = WindowGather(place, low_ref, block, window, sem_low)
    last_gather.send()
    share_ref[...] = own_share
    ortho_ref[...] = lax.dot_general(
        left[...], tri[...], by_rank, precision=HIGH, preferred_element_type=F32
    ).astype(BF16)
    arrived(place, sq_z.at[pl.ds(0, n_dp - 1)], sem_sz)
    sq_p[me] = jnp.sum(sq_z[...], axis=0)
    exchange(place.plane_all, lambda k: sq_p.at[me], sq_p.at[me], sem_sp)
    last_gather.receive()
    arrived(place, sq_p.at[pl.ds(0, n_mp - 1)], sem_sp)
    squares = jnp.sum(sq_p[...], axis=0)
    inv_ref[...] = jnp.broadcast_to(lax.rsqrt(squares + EPSILON), inv_ref.shape)
    for ref, sems in [
        (all_z, sem_fz), (all_p, sem_fp), (left_in, sem_lr), (all_left, sem_lg), (gram_zc, sem_gz), (all_gp, sem_gp),
        (all_gram, sem_gg), (plane_in, sem_plane), (step_in, sem_step), (core_send, sem_core),
        (sq_z.at[pl.ds(0, n_dp - 1)], sem_sz), (sq_p.at[pl.ds(0, n_mp - 1)], sem_sp),
    ]:
        sent(place, ref, sems)
    gather.drain()
    last_gather.drain()


def mega_stage(n_dp, n_mp, momentum, tile_values, exponents, right_prev, overflow):
    rows, cols = momentum.shape
    share, rank = right_prev.shape
    chips = n_mp // 2
    block = 2 * share
    window = share + -share % 16
    side = int(round(math.sqrt(chips)))
    n_near = 4 if side > 2 else 2
    n_far = chips - 1 - n_near
    vmem = pl.BlockSpec(memory_space=pltpu.VMEM)
    hbm = pl.BlockSpec(memory_space=pltpu.HBM)
    dma = pltpu.SemaphoreType.DMA
    return pl.pallas_call(
        functools.partial(mega_kernel, n_dp, n_mp),
        name="mega",
        out_shape=(
            jax.ShapeDtypeStruct((rows, rank), BF16),
            jax.ShapeDtypeStruct((cols, rank), BF16),
            jax.ShapeDtypeStruct((8, 128), F32),
            jax.ShapeDtypeStruct((share, rank), F32),
            jax.ShapeDtypeStruct((rows, cols), F32),
        ),
        in_specs=[hbm] * 4 + [pl.BlockSpec(memory_space=pltpu.SMEM)],
        out_specs=(vmem,) * 5,
        scratch_shapes=[
            pltpu.VMEM((2 * rows, cols), BF16),
            pltpu.VMEM(exponents.shape, jnp.int32),
            pltpu.VMEM((rows // BLOCK, 16, cols), BF16),
            pltpu.VMEM((share, rank), F32),
            pltpu.VMEM((n_mp * window, rank), BF16),
            pltpu.VMEM((cols, 2 * rows), BF16),
            pltpu.VMEM((n_dp, 1, 128), F32),
            pltpu.VMEM((n_mp, 1, 128), F32),
            pltpu.VMEM((rank, 2 * rows), F32),
            pltpu.VMEM((rows, rank), F32),
            pltpu.VMEM((n_dp - 1, rows // n_dp, rank), F32),
            pltpu.VMEM((rows, rank), F32),
            pltpu.VMEM((rows, 2 * rank), BF16),
            pltpu.VMEM((rank, rank), F32),
            pltpu.VMEM((2 * n_dp - 1, rank // (2 * n_dp), rank), F32),
            pltpu.VMEM((chips, rank // (2 * n_dp), rank), F32),
            pltpu.VMEM((rank, rank), F32),
            pltpu.VMEM((rank, rank), F32),
            pltpu.VMEM((rank, rank), F32),
            pltpu.VMEM((side, side, window, rank), F32),
            pltpu.VMEM((side, side, window, rank), F32),
            pltpu.VMEM((side, side, window, rank), F32),
            pltpu.VMEM((side - 1, side, window, rank), F32),
            pltpu.VMEM((side - 1, window, rank), F32),
            pltpu.VMEM((side - 1, window, rank), F32),
            pltpu.VMEM((window, rank), F32),
            pltpu.VMEM((n_dp, 1, 128), F32),
            pltpu.VMEM((n_mp, 1, 128), F32),
            dma((4,)),
            dma((7 + 2 * n_far,)),
            dma((2,)),
            dma((2,)),
            dma((2,)),
            dma((2,)),
            dma((2,)),
            dma((2,)),
            dma((2,)),
            dma((1 + side,)),
            dma((2,)),
            dma((2,)),
            dma((7 + 2 * n_far,)),
            dma((2,)),
            dma((2,)),
        ],
        compiler_params=pltpu.CompilerParams(
            collective_id=0, has_side_effects=True, vmem_limit_bytes=VMEM_LIMIT
        ),
    )(momentum, tile_values, exponents, right_prev, overflow)


def finish_kernel(unit, sums, ortho, low, inv, share, new, upd, share_out, new_v, upd_v, sem):
    rows, cols = sums.shape
    step = 256
    base = ortho[...]
    scaled = (base.astype(F32) * inv[0:1, :]).astype(BF16)
    both = (((1,), (1,)), ((), ()))
    share_copy = pltpu.make_async_copy(share, share_out, sem.at[2])
    share_copy.start()
    for t in range(cols // step):
        at = slice(t * step, (t + 1) * step)
        piece = low[at, :]
        correction = lax.dot_general(base, piece, both, preferred_element_type=F32)
        new_v[:, at] = (sums[:, at] - (1.0 - RETAIN) * correction).astype(BF16)
        direction = lax.dot_general(scaled, piece, both, preferred_element_type=F32)
        upd_v[:, at] = (unit * direction).astype(BF16)
        for k, (src, dst) in enumerate([(new_v, new), (upd_v, upd)]):
            pltpu.make_async_copy(src.at[:, at], dst.at[:, at], sem.at[k]).start()
    share_copy.wait()
    for k, (src, dst) in enumerate([(new_v, new), (upd_v, upd)]):
        pltpu.make_async_copy(src, dst, sem.at[k]).wait()


def finish_stage(unit, sums, ortho, low, inv, share):
    rows, cols = sums.shape
    vmem = pl.BlockSpec(memory_space=pltpu.VMEM)
    hbm = pl.BlockSpec(memory_space=pltpu.HBM)
    return pl.pallas_call(
        functools.partial(finish_kernel, unit),
        name="finish",
        out_shape=(
            jax.ShapeDtypeStruct((rows, cols), BF16),
            jax.ShapeDtypeStruct((rows, cols), BF16),
            jax.ShapeDtypeStruct(share.shape, F32),
        ),
        in_specs=[vmem] * 5,
        out_specs=(hbm,) * 3,
        scratch_shapes=[
            pltpu.VMEM((rows, cols), BF16),
            pltpu.VMEM((rows, cols), BF16),
            pltpu.SemaphoreType.DMA((3,)),
        ],
        compiler_params=pltpu.CompilerParams(vmem_limit_bytes=VMEM_LIMIT),
    )(sums, ortho, low, inv, share)


def body(n_dp, n_mp, momentum, tile_values, exponents, overflow, right_prev):
    rows, cols = momentum.shape
    rank = right_prev.shape[1]
    unit = math.sqrt(rows * n_mp * cols * n_dp / rank)
    args = [
        pltpu.with_memory_space_constraint(a, pltpu.HBM)
        for a in (momentum, tile_values, exponents, right_prev)
    ]
    ortho, low, inv, own, sums = mega_stage(n_dp, n_mp, *args, overflow)
    new, update, right_out = finish_stage(unit, sums, ortho, low, inv, own)
    return new, right_out, update


def solution(mesh):
    in_specs = (P("mp", "dp"), P("mp", "dp"), P("mp", "dp"), P("mp", "dp"), P(("dp", "mp"), None))
    out_specs = (P("mp", "dp"), P(("dp", "mp"), None), P("mp", "dp"))
    step = functools.partial(body, mesh.shape["dp"], mesh.shape["mp"])
    return jax.shard_map(step, mesh=mesh, in_specs=in_specs, out_specs=out_specs, check_vma=False)
```

```python
import functools
import math

import jax
import jax.numpy as jnp
from jax import lax
from jax.experimental import pallas as pl
from jax.experimental.pallas import tpu as pltpu
from jax.sharding import PartitionSpec as P

MESH = pl.DeviceIdType.MESH
F32 = jnp.float32
BF16 = jnp.bfloat16
HIGH = lax.Precision.HIGHEST
BLOCK = 128
EPSILON = 1e-06
RETAIN = 0.95
VMEM_LIMIT = 32 * 1024 * 1024


def torus(a, n):
    return min(a % n, -a % n)


class Place:
    def __init__(self, n_dp, n_mp):
        self.nz = n_dp
        self.chips = n_mp // 2
        self.ny = int(round(math.sqrt(self.chips)))
        self.nx = self.chips // self.ny
        self.half = self.chips // 2
        mp = lax.axis_index("mp")
        self.z = lax.axis_index("dp")
        self.core = lax.rem(mp, 2)
        self.other = 1 - self.core
        self.chip = mp // 2
        x = self.chip // self.ny
        y = lax.rem(self.chip, self.ny)
        xs = [lax.rem(x + d, self.nx) * self.ny for d in range(self.nx)]
        ys = [lax.rem(y + d, self.ny) for d in range(self.ny)]
        offsets = sorted(
            ((dx, dy) for dx in range(self.nx) for dy in range(self.ny)),
            key=lambda o: -torus(o[0], self.nx) - torus(o[1], self.ny),
        )
        chips = {o: xs[o[0]] + ys[o[1]] for o in offsets}
        def away(offset):
            return torus(offset[0], self.nx) + torus(offset[1], self.ny)

        def back(offset):
            return chips[-offset[0] % self.nx, -offset[1] % self.ny]

        self.sibling = (self.z, self.chip * 2 + self.other)
        self.plane = [chips[o] for o in offsets[:-1]]
        self.plane_from = [back(o) for o in offsets[:-1]]
        far = [o for o in offsets if away(o) > 1]
        near = [o for o in offsets if away(o) == 1]
        self.n_far, self.n_near = len(far), len(near)
        self.near_to = [chips[o] for o in near]
        self.near_from = [back(o) for o in near]
        self.plane_peers = [(self.z, chip * 2 + self.core) for chip in self.plane]
        self.plane_all = [(self.z, chip * 2 + core) for chip in self.plane for core in (self.core, self.other)] + [self.sibling]
        self.z_order = sorted(range(1, self.nz), key=lambda d: -torus(d, self.nz))
        self.zs = [lax.rem(self.z + d, self.nz) for d in self.z_order]
        self.z_peers = [(z, self.chip * 2 + self.core) for z in self.zs]
        self.zc_peers = [
            (z, self.chip * 2 + core) for z in self.zs for core in (self.core, self.other)
        ] + [self.sibling]
        assert self.nx == self.ny
        self.steps = sorted(range(self.nx), key=lambda d: -torus(d, self.nx))

        def cross(core, a, b):
            return jnp.where(core == 0, chips[a, b], chips[b, a])

        self.group = [[cross(self.core, a, b) for b in range(self.nx)] for a in range(self.nx)]
        self.other_group = [[cross(self.other, a, b) for b in range(self.nx)] for a in range(self.nx)]
        self.step_one = [self.same_core(cross(self.core, a, 0)) for a in range(self.nx)]
        self.step_two = [self.same_core(cross(self.core, 0, a)) for a in range(self.nx)]
        self.zc_spots = [z * 2 + core for z in self.zs for core in (self.core, self.other)] + [self.z * 2 + self.other]

    def same_core(self, chip):
        return (self.z, chip * 2 + self.core)

    def other_core(self, chip):
        return (self.z, chip * 2 + self.other)


def remote(src, dst, send, recv, dev):
    return pltpu.make_async_remote_copy(
        src_ref=src, dst_ref=dst, send_sem=send, recv_sem=recv, device_id=dev, device_id_type=MESH
    )


def exchange(peers, src_of, dst, sems):
    for k, dev in enumerate(peers):
        remote(src_of(k), dst, sems.at[0], sems.at[1], dev).start()


def arrived(place, ref, sems):
    remote(ref, ref, sems.at[0], sems.at[1], place.sibling).wait_recv()


def sent(place, ref, sems):
    remote(ref, ref, sems.at[0], sems.at[1], place.sibling).wait_send()


class WindowGather:
    def __init__(self, place, buf, block, window, sems):
        self.place = place
        keep = block - window

        def whole(chip):
            return buf.at[pl.ds(pl.multiple_of(chip * block + place.core * keep, 16), window)]

        def rest(chip, core):
            return buf.at[pl.ds(pl.multiple_of(chip * block + core * window, 16), keep)]

        self.buf, self.window, self.keep, self.sems = buf, window, keep, sems
        mine, lacking = whole(place.chip), rest(place.chip, place.core)
        far = place.plane_from[:place.n_far]
        first, onward = 7, 7 + place.n_far
        self.copies = [
            remote(mine, mine, sems.at[0], sems.at[first + k if k < place.n_far else 6], dev)
            for k, dev in enumerate(place.plane_peers)
        ] + [
            remote(lacking, lacking, sems.at[2], sems.at[3], place.other_core(chip)) for chip in place.near_to
        ] + [remote(lacking, lacking, sems.at[4], sems.at[5], place.sibling)]
        self.arrivals = [
            remote(whole(chip), whole(chip), sems.at[0], sems.at[first + k], place.sibling)
            for k, chip in enumerate(far)
        ]
        self.passes = [
            remote(rest(chip, place.core), rest(chip, place.core), sems.at[1], sems.at[onward + k], place.sibling)
            for k, chip in enumerate(far)
        ]
        self.passed = [
            remote(rest(chip, place.other), rest(chip, place.other), sems.at[1], sems.at[onward + k], place.sibling)
            for k, chip in enumerate(far)
        ]

    def total(self, send, recv, rows):
        ref = self.buf.at[pl.ds(0, rows)]
        return remote(ref, ref, self.sems.at[send], self.sems.at[recv], self.place.sibling)

    def send(self):
        for copy in self.copies:
            copy.start()

    def receive(self, use=None):
        place = self.place
        for arrival, onward in zip(self.arrivals, self.passes):
            arrival.wait_recv()
            onward.start()
        self.total(0, 6, place.n_near * self.window).wait_recv()
        self.total(2, 3, place.n_near * self.keep).wait_recv()
        self.total(4, 5, self.keep).wait_recv()
        if use is not None:
            for chip in [place.chip] + place.near_from:
                use(chip)
        for copy, chip in zip(self.passed, place.plane_from):
            copy.wait_recv()
            if use is not None:
                use(chip)

    def drain(self):
        place = self.place
        self.total(0, 6, (place.n_far + place.n_near) * self.window).wait_send()
        self.total(1, 6, place.n_far * self.keep).wait_send()
        self.total(2, 3, place.n_near * self.keep).wait_send()
        self.total(4, 5, self.keep).wait_send()


def invert(work, out_ref):
    rank = work.shape[0]
    size = 8
    lanes = lax.broadcasted_iota(jnp.int32, (size, rank), 1)
    lane = lanes[0:1]
    for r in range(0, rank, size):
        row = [work[r + i:r + i + 1, :] for i in range(size)]
        a = [[jnp.broadcast_to(row[i][:, r + j:r + j + 1], (1, rank)) for j in range(i + 1)] for i in range(size)]
        inside = (lane >= r) & (lane < r + size)
        row = [jnp.where(inside, jnp.where(lane == r + i, 1.0, 0.0), row[i]) for i in range(size)]
        e = [[None] * size for _ in range(size)]
        pivot, recip = [], []
        for j in range(size):
            pivot.append(a[j][j])
            recip.append(1.0 / a[j][j])
            for i in range(j + 1, size):
                m = a[i][j] * recip[j]
                for k in range(j + 1, i + 1):
                    a[i][k] = a[i][k] - m * a[k][j]
                for k in range(j):
                    e[i][k] = e[i][k] - m * e[j][k]
                e[i][j] = -m
        z = []
        for i in range(size):
            t = row[i]
            for j in range(i):
                t = t + e[i][j] * row[j]
            z.append(t)
        y = []
        zq = [z[i] * recip[i] for i in range(size)]
        for i in range(size):
            t = zq[i]
            for k in range(i + 1, size):
                t = t + e[k][i] * zq[k]
            y.append(t)
        out = jnp.concatenate([z[i] * lax.rsqrt(pivot[i]) for i in range(size)], axis=0)
        out_ref[r:r + size, :] = jnp.where(lanes < r + size, out, 0.0)
        for s in range(r + size, rank, size):
            old = work[s:s + size, :]
            acc = jnp.where((lanes >= r) & (lanes < r + size), 0.0, old)
            for k in range(size):
                acc = acc - jnp.broadcast_to(old[:, r + k:r + k + 1], (size, rank)) * y[k]
            work[s:s + size, :] = acc


def mega_kernel(
    n_dp, n_mp,
    mom_hbm, tile_hbm, exps_hbm, prev_hbm, over_ref,
    ortho_ref, low_ref, inv_ref, share_ref, sum_ref,
    both, exps, scale, prev, right, both_t, flag_z, flag_p, left_t,
    part, left_in, left, left_hl, gram, gram_zc, gram_p, gram_all, work, tri,
    core_send, core_in, core_out, plane_in, step_out, step_in, mine, sq_z, sq_p,
    sem_in, sem_gather, sem_fz, sem_fp, sem_lr, sem_lg, sem_gz, sem_gp, sem_gg,
    sem_core, sem_plane, sem_step, sem_low, sem_sz, sem_sp,
):
    place = Place(n_dp, n_mp)
    rows, cols = mom_hbm.shape
    share, rank = share_ref.shape
    block = 2 * share
    window = share + -share % 16
    keep = block - window
    loads = [
        pltpu.make_async_copy(src, dst, sem_in.at[k])
        for k, (src, dst) in enumerate(
            [
                (prev_hbm, prev), (exps_hbm, exps),
                (mom_hbm, both.at[0:rows]), (tile_hbm, both.at[rows:2 * rows]),
            ]
        )
    ]
    for load in loads:
        load.start()
    barrier = pltpu.get_barrier_semaphore()
    friends = place.zc_peers[:-1] + place.plane_all
    for dev in friends:
        pl.semaphore_signal(barrier, inc=1, device_id=dev, device_id_type=MESH)
    kept = jnp.where(over_ref[0, 0] == 0, 1.0, 0.0).astype(F32)
    flag_z[place.z] = jnp.full((1, 128), kept, F32)
    loads[1].wait()
    scales = jnp.exp2(exps[...].astype(F32)).astype(BF16).astype(F32) * kept
    for j in range(cols // BLOCK):
        for b in range(rows // BLOCK):
            scale[b, :, j * BLOCK:(j + 1) * BLOCK] = jnp.broadcast_to(scales[b:b + 1, j:j + 1], (16, BLOCK)).astype(BF16)
    loads[0].wait()
    gather = WindowGather(place, right, 2 * window, window, sem_gather)
    mine_low = prev[...].astype(BF16).astype(F32)
    if window > share:
        mine_low = jnp.concatenate([mine_low, jnp.zeros((window - share, rank), F32)], axis=0)
    me = place.chip * 2 + place.core
    right[pl.ds(pl.multiple_of(me * window, 16), window)] = mine_low.astype(BF16)
    pl.semaphore_wait(barrier, len(friends))

    exchange(place.z_peers, lambda k: flag_z.at[place.z], flag_z.at[place.z], sem_fz)
    gather.send()

    loads[2].wait()
    loads[3].wait()

    def decode(j, carry):
        at = pl.ds(pl.multiple_of(j * BLOCK, BLOCK), BLOCK)
        for b in range(rows // BLOCK):
            factor_of = scale[b, :, at]
            for r in range(rows + b * BLOCK, rows + (b + 1) * BLOCK, 16):
                both[r:r + 16, at] = both[r:r + 16, at] * factor_of
        return carry

    lax.fori_loop(0, cols // BLOCK, decode, 0)

    def transpose(j, carry):
        at = pl.ds(pl.multiple_of(j * BLOCK, BLOCK), BLOCK)
        both_t[at, :rows] = both[0:rows, at].T
        both_t[at, rows:] = both[rows:2 * rows, at].T
        return carry

    lax.fori_loop(0, cols // BLOCK, transpose, 0, unroll=2)

    left_t[...] = jnp.zeros_like(left_t)
    all_z = flag_z.at[pl.ds(0, n_dp - 1)]
    arrived(place, all_z, sem_fz)
    flag_p[me] = jnp.sum(flag_z[...], axis=0)
    exchange(place.plane_all, lambda k: flag_p.at[me], flag_p.at[me], sem_fp)

    def rows_of(chip):
        return pl.ds(pl.multiple_of(chip * block, 16), block)

    def use(chip):
        got = right[pl.ds(pl.multiple_of(chip * 2 * window, 16), 2 * window), :].astype(F32)
        got = jnp.concatenate([got[:share], got[window:window + share]], axis=0).astype(BF16)
        left_t[...] += jnp.dot(got.T, both_t[rows_of(chip), :], preferred_element_type=F32)

    gather.receive(use)
    all_p = flag_p.at[pl.ds(0, n_mp - 1)]
    arrived(place, all_p, sem_fp)
    healthy = jnp.sum(flag_p[...], axis=0)
    factor = float(n_dp * n_mp) / jnp.maximum(healthy, 1.0)
    for r in range(0, rows, BLOCK):
        part[r:r + BLOCK, :] = (left_t[:, r:r + BLOCK] + factor * left_t[:, rows + r:rows + r + BLOCK]).T

    rz = rows // place.nz
    for k, z in enumerate(place.zs):
        remote(
            part.at[pl.ds(pl.multiple_of(z * rz, 8), rz)], left_in.at[k], sem_lr.at[0], sem_lr.at[1],
            place.z_peers[k],
        ).start()

    wide = jnp.broadcast_to(factor[:, 0:1], (16, BLOCK))

    def add(j, carry):
        at = pl.ds(pl.multiple_of(j * BLOCK, BLOCK), BLOCK)
        for r in range(0, rows, 16):
            sum_ref[r:r + 16, at] = both[r:r + 16, at].astype(F32) + wide * both[rows + r:rows + r + 16, at].astype(F32)
        return carry

    own = pl.ds(pl.multiple_of(place.z * rz, 8), rz)
    acc = part[own]
    arrived(place, left_in, sem_lr)
    for k in range(n_dp - 1):
        acc = acc + left_in[k]
    left[own] = acc
    gram[...] = lax.dot_general(acc, acc, (((0,), (0,)), ((), ())), precision=HIGH, preferred_element_type=F32)
    gs = rank // (2 * place.nz)
    for k, spot in enumerate(place.zc_spots):
        remote(
            gram.at[pl.ds(pl.multiple_of(spot * gs, 8), gs)], gram_zc.at[k], sem_gz.at[0], sem_gz.at[1],
            place.zc_peers[k],
        ).start()
    exchange(place.z_peers, lambda k: left.at[own], left.at[own], sem_lg)
    lax.fori_loop(0, cols // BLOCK, add, 0)
    piece = pl.ds(pl.multiple_of((place.z * 2 + place.core) * gs, 8), gs)
    acc = gram[piece]
    arrived(place, gram_zc, sem_gz)
    for k in range(2 * n_dp - 1):
        acc = acc + gram_zc[k]
    gram_p[place.chip] = acc
    exchange(place.plane_peers, lambda k: gram_p.at[place.chip], gram_p.at[place.chip], sem_gp)
    all_left = left.at[pl.ds(0, rows - rz)]
    arrived(place, all_left, sem_lg)

    high = left[...].astype(BF16)
    left_hl[:, :rank] = high
    left_hl[:, rank:] = (left[...] - high.astype(F32)).astype(BF16)
    def raw_part(chip, core):
        at = pl.ds(pl.multiple_of(chip * block + core * keep, 16), window)
        mom_two = jnp.dot(both_t[at, :rows], left_hl[...], preferred_element_type=F32)
        grad_two = jnp.dot(both_t[at, rows:], left_hl[...], preferred_element_type=F32)
        return mom_two[:, :rank] + mom_two[:, rank:] + factor * (grad_two[:, :rank] + grad_two[:, rank:])

    core_copies = {}

    def for_sibling(a):
        for b, chip in enumerate(place.other_group[a]):
            core_send[a, b] = raw_part(chip, place.other)
        core_copies[a] = remote(core_send.at[a], core_in.at[a], sem_core.at[0], sem_core.at[1 + a], place.sibling)
        core_copies[a].start()

    def for_plane(a):
        parts = [raw_part(chip, place.core) for chip in place.group[a]]
        core_copies[a].wait_recv()
        for b, value in enumerate(parts):
            core_out[a, b] = value + core_in[a, b]
        if a:
            remote(core_out.at[a], plane_in.at[a - 1], sem_plane.at[0], sem_plane.at[1], place.step_one[a]).start()

    n_side = place.nx
    for_sibling(place.steps[0])
    for ahead, a in zip(place.steps[1:], place.steps):
        for_sibling(ahead)
        for_plane(a)
    last = place.chips - 1
    all_gp = gram_p.at[pl.ds(0, last)]
    arrived(place, all_gp, sem_gp)
    gram_all[piece] = jnp.sum(gram_p[...], axis=0)
    exchange(place.zc_peers, lambda k: gram_all.at[piece], gram_all.at[piece], sem_gg)
    for_plane(0)
    arrived(place, plane_in, sem_plane)
    for b in place.steps:
        total = core_out[0, b]
        for a in range(n_side - 1):
            total = total + plane_in[a, b]
        if b:
            step_out[b - 1] = total
            remote(step_out.at[b - 1], step_in.at[b - 1], sem_step.at[0], sem_step.at[1], place.step_two[b]).start()
    all_gram = gram_all.at[pl.ds(0, rank - gs)]
    arrived(place, all_gram, sem_gg)
    work[...] = gram_all[...]
    invert(work, tri)
    arrived(place, step_in, sem_step)
    for b in range(n_side - 1):
        total = total + step_in[b]
    by_rank = (((1,), (1,)), ((), ()))
    total = lax.dot_general(total, tri[...], by_rank, precision=HIGH, preferred_element_type=F32)
    mine[...] = total
    own_share = mine[pl.ds(pl.multiple_of(place.core * (window - share), 8), share)]
    sq_z[place.z] = jnp.sum(own_share * own_share, axis=0, keepdims=True)
    exchange(place.z_peers, lambda k: sq_z.at[place.z], sq_z.at[place.z], sem_sz)
    low_ref[pl.ds(pl.multiple_of(place.chip * block + place.core * keep, 16), window)] = total.astype(BF16)
    last_gather = WindowGather(place, low_ref, block, window, sem_low)
    last_gather.send()
    share_ref[...] = own_share
    ortho_ref[...] = lax.dot_general(
        left[...], tri[...], by_rank, precision=HIGH, preferred_element_type=F32
    ).astype(BF16)
    arrived(place, sq_z.at[pl.ds(0, n_dp - 1)], sem_sz)
    sq_p[me] = jnp.sum(sq_z[...], axis=0)
    exchange(place.plane_all, lambda k: sq_p.at[me], sq_p.at[me], sem_sp)
    last_gather.receive()
    arrived(place, sq_p.at[pl.ds(0, n_mp - 1)], sem_sp)
    squares = jnp.sum(sq_p[...], axis=0)
    inv_ref[...] = jnp.broadcast_to(lax.rsqrt(squares + EPSILON), inv_ref.shape)
    for ref, sems in [
        (all_z, sem_fz), (all_p, sem_fp), (left_in, sem_lr), (all_left, sem_lg), (gram_zc, sem_gz), (all_gp, sem_gp),
        (all_gram, sem_gg), (plane_in, sem_plane), (step_in, sem_step), (core_send, sem_core),
        (sq_z.at[pl.ds(0, n_dp - 1)], sem_sz), (sq_p.at[pl.ds(0, n_mp - 1)], sem_sp),
    ]:
        sent(place, ref, sems)
    gather.drain()
    last_gather.drain()


def mega_stage(n_dp, n_mp, momentum, tile_values, exponents, right_prev, overflow):
    rows, cols = momentum.shape
    share, rank = right_prev.shape
    chips = n_mp // 2
    block = 2 * share
    window = share + -share % 16
    side = int(round(math.sqrt(chips)))
    n_near = 4 if side > 2 else 2
    n_far = chips - 1 - n_near
    vmem = pl.BlockSpec(memory_space=pltpu.VMEM)
    hbm = pl.BlockSpec(memory_space=pltpu.HBM)
    dma = pltpu.SemaphoreType.DMA
    return pl.pallas_call(
        functools.partial(mega_kernel, n_dp, n_mp),
        name="mega",
        out_shape=(
            jax.ShapeDtypeStruct((rows, rank), BF16),
            jax.ShapeDtypeStruct((cols, rank), BF16),
            jax.ShapeDtypeStruct((8, 128), F32),
            jax.ShapeDtypeStruct((share, rank), F32),
            jax.ShapeDtypeStruct((rows, cols), F32),
        ),
        in_specs=[hbm] * 4 + [pl.BlockSpec(memory_space=pltpu.SMEM)],
        out_specs=(vmem,) * 5,
        scratch_shapes=[
            pltpu.VMEM((2 * rows, cols), BF16),
            pltpu.VMEM(exponents.shape, jnp.int32),
            pltpu.VMEM((rows // BLOCK, 16, cols), BF16),
            pltpu.VMEM((share, rank), F32),
            pltpu.VMEM((n_mp * window, rank), BF16),
            pltpu.VMEM((cols, 2 * rows), BF16),
            pltpu.VMEM((n_dp, 1, 128), F32),
            pltpu.VMEM((n_mp, 1, 128), F32),
            pltpu.VMEM((rank, 2 * rows), F32),
            pltpu.VMEM((rows, rank), F32),
            pltpu.VMEM((n_dp - 1, rows // n_dp, rank), F32),
            pltpu.VMEM((rows, rank), F32),
            pltpu.VMEM((rows, 2 * rank), BF16),
            pltpu.VMEM((rank, rank), F32),
            pltpu.VMEM((2 * n_dp - 1, rank // (2 * n_dp), rank), F32),
            pltpu.VMEM((chips, rank // (2 * n_dp), rank), F32),
            pltpu.VMEM((rank, rank), F32),
            pltpu.VMEM((rank, rank), F32),
            pltpu.VMEM((rank, rank), F32),
            pltpu.VMEM((side, side, window, rank), F32),
            pltpu.VMEM((side, side, window, rank), F32),
            pltpu.VMEM((side, side, window, rank), F32),
            pltpu.VMEM((side - 1, side, window, rank), F32),
            pltpu.VMEM((side - 1, window, rank), F32),
            pltpu.VMEM((side - 1, window, rank), F32),
            pltpu.VMEM((window, rank), F32),
            pltpu.VMEM((n_dp, 1, 128), F32),
            pltpu.VMEM((n_mp, 1, 128), F32),
            dma((4,)),
            dma((7 + 2 * n_far,)),
            dma((2,)),
            dma((2,)),
            dma((2,)),
            dma((2,)),
            dma((2,)),
            dma((2,)),
            dma((2,)),
            dma((1 + side,)),
            dma((2,)),
            dma((2,)),
            dma((7 + 2 * n_far,)),
            dma((2,)),
            dma((2,)),
        ],
        compiler_params=pltpu.CompilerParams(
            collective_id=0, has_side_effects=True, vmem_limit_bytes=VMEM_LIMIT
        ),
    )(momentum, tile_values, exponents, right_prev, overflow)


def finish_kernel(unit, sums, ortho, low, inv, share, new, upd, share_out, new_v, upd_v, sem):
    rows, cols = sums.shape
    step = 256
    base = ortho[...]
    scaled = (base.astype(F32) * inv[0:1, :]).astype(BF16)
    both = (((1,), (1,)), ((), ()))
    share_copy = pltpu.make_async_copy(share, share_out, sem.at[2])
    share_copy.start()
    for t in range(cols // step):
        at = slice(t * step, (t + 1) * step)
        piece = low[at, :]
        correction = lax.dot_general(base, piece, both, preferred_element_type=F32)
        new_v[:, at] = (sums[:, at] - (1.0 - RETAIN) * correction).astype(BF16)
        direction = lax.dot_general(scaled, piece, both, preferred_element_type=F32)
        upd_v[:, at] = (unit * direction).astype(BF16)
        for k, (src, dst) in enumerate([(new_v, new), (upd_v, upd)]):
            pltpu.make_async_copy(src.at[:, at], dst.at[:, at], sem.at[k]).start()
    share_copy.wait()
    for k, (src, dst) in enumerate([(new_v, new), (upd_v, upd)]):
        pltpu.make_async_copy(src, dst, sem.at[k]).wait()


def finish_stage(unit, sums, ortho, low, inv, share):
    rows, cols = sums.shape
    vmem = pl.BlockSpec(memory_space=pltpu.VMEM)
    hbm = pl.BlockSpec(memory_space=pltpu.HBM)
    return pl.pallas_call(
        functools.partial(finish_kernel, unit),
        name="finish",
        out_shape=(
            jax.ShapeDtypeStruct((rows, cols), BF16),
            jax.ShapeDtypeStruct((rows, cols), BF16),
            jax.ShapeDtypeStruct(share.shape, F32),
        ),
        in_specs=[vmem] * 5,
        out_specs=(hbm,) * 3,
        scratch_shapes=[
            pltpu.VMEM((rows, cols), BF16),
            pltpu.VMEM((rows, cols), BF16),
            pltpu.SemaphoreType.DMA((3,)),
        ],
        compiler_params=pltpu.CompilerParams(vmem_limit_bytes=VMEM_LIMIT),
    )(sums, ortho, low, inv, share)


def body(n_dp, n_mp, momentum, tile_values, exponents, overflow, right_prev):
    rows, cols = momentum.shape
    rank = right_prev.shape[1]
    unit = math.sqrt(rows * n_mp * cols * n_dp / rank)
    args = [
        pltpu.with_memory_space_constraint(a, pltpu.HBM)
        for a in (momentum, tile_values, exponents, right_prev)
    ]
    ortho, low, inv, own, sums = mega_stage(n_dp, n_mp, *args, overflow)
    new, update, right_out = finish_stage(unit, sums, ortho, low, inv, own)
    return new, right_out, update


def solution(mesh):
    in_specs = (P("mp", "dp"), P("mp", "dp"), P("mp", "dp"), P("mp", "dp"), P(("dp", "mp"), None))
    out_specs = (P("mp", "dp"), P(("dp", "mp"), None), P("mp", "dp"))
    step = functools.partial(body, mesh.shape["dp"], mesh.shape["mp"])
    return jax.shard_map(step, mesh=mesh, in_specs=in_specs, out_specs=out_specs, check_vma=False)
```

```python
import functools
import math

import jax
import jax.numpy as jnp
from jax import lax
from jax.experimental import pallas as pl
from jax.experimental.pallas import tpu as pltpu
from jax.sharding import PartitionSpec as P

MESH = pl.DeviceIdType.MESH
F32 = jnp.float32
BF16 = jnp.bfloat16
HIGH = lax.Precision.HIGHEST
BLOCK = 128
EPSILON = 1e-06
RETAIN = 0.95
VMEM_LIMIT = 32 * 1024 * 1024


def torus(a, n):
    return min(a % n, -a % n)


class Place:
    def __init__(self, n_dp, n_mp):
        self.nz = n_dp
        self.chips = n_mp // 2
        self.ny = int(round(math.sqrt(self.chips)))
        self.nx = self.chips // self.ny
        self.half = self.chips // 2
        mp = lax.axis_index("mp")
        self.z = lax.axis_index("dp")
        self.core = lax.rem(mp, 2)
        self.other = 1 - self.core
        self.chip = mp // 2
        x = self.chip // self.ny
        y = lax.rem(self.chip, self.ny)
        xs = [lax.rem(x + d, self.nx) * self.ny for d in range(self.nx)]
        ys = [lax.rem(y + d, self.ny) for d in range(self.ny)]
        offsets = sorted(
            ((dx, dy) for dx in range(self.nx) for dy in range(self.ny)),
            key=lambda o: -torus(o[0], self.nx) - torus(o[1], self.ny),
        )
        chips = {o: xs[o[0]] + ys[o[1]] for o in offsets}
        def away(offset):
            return torus(offset[0], self.nx) + torus(offset[1], self.ny)

        def back(offset):
            return chips[-offset[0] % self.nx, -offset[1] % self.ny]

        self.sibling = (self.z, self.chip * 2 + self.other)
        self.plane = [chips[o] for o in offsets[:-1]]
        self.plane_from = [back(o) for o in offsets[:-1]]
        far = [o for o in offsets if away(o) > 1]
        near = [o for o in offsets if away(o) == 1]
        self.n_far, self.n_near = len(far), len(near)
        self.near_to = [chips[o] for o in near]
        self.near_from = [back(o) for o in near]
        self.plane_peers = [(self.z, chip * 2 + self.core) for chip in self.plane]
        self.plane_all = [(self.z, chip * 2 + core) for chip in self.plane for core in (self.core, self.other)] + [self.sibling]
        self.z_order = sorted(range(1, self.nz), key=lambda d: -torus(d, self.nz))
        self.zs = [lax.rem(self.z + d, self.nz) for d in self.z_order]
        self.z_peers = [(z, self.chip * 2 + self.core) for z in self.zs]
        self.zc_peers = [
            (z, self.chip * 2 + core) for z in self.zs for core in (self.core, self.other)
        ] + [self.sibling]
        assert self.nx == self.ny
        self.steps = sorted(range(self.nx), key=lambda d: -torus(d, self.nx))

        def cross(core, a, b):
            return jnp.where(core == 0, chips[a, b], chips[b, a])

        self.group = [[cross(self.core, a, b) for b in range(self.nx)] for a in range(self.nx)]
        self.other_group = [[cross(self.other, a, b) for b in range(self.nx)] for a in range(self.nx)]
        self.step_one = [self.same_core(cross(self.core, a, 0)) for a in range(self.nx)]
        self.step_two = [self.same_core(cross(self.core, 0, a)) for a in range(self.nx)]
        self.zc_spots = [z * 2 + core for z in self.zs for core in (self.core, self.other)] + [self.z * 2 + self.other]

    def same_core(self, chip):
        return (self.z, chip * 2 + self.core)

    def other_core(self, chip):
        return (self.z, chip * 2 + self.other)


def remote(src, dst, send, recv, dev):
    return pltpu.make_async_remote_copy(
        src_ref=src, dst_ref=dst, send_sem=send, recv_sem=recv, device_id=dev, device_id_type=MESH
    )


def exchange(peers, src_of, dst, sems):
    for k, dev in enumerate(peers):
        remote(src_of(k), dst, sems.at[0], sems.at[1], dev).start()


def arrived(place, ref, sems):
    remote(ref, ref, sems.at[0], sems.at[1], place.sibling).wait_recv()


def sent(place, ref, sems):
    remote(ref, ref, sems.at[0], sems.at[1], place.sibling).wait_send()


class WindowGather:
    def __init__(self, place, buf, block, window, sems):
        self.place = place
        keep = block - window

        def whole(chip):
            return buf.at[pl.ds(pl.multiple_of(chip * block + place.core * keep, 16), window)]

        def rest(chip, core):
            return buf.at[pl.ds(pl.multiple_of(chip * block + core * window, 16), keep)]

        self.buf, self.window, self.keep, self.sems = buf, window, keep, sems
        mine, lacking = whole(place.chip), rest(place.chip, place.core)
        far = place.plane_from[:place.n_far]
        first, onward = 7, 7 + place.n_far
        self.copies = [
            remote(mine, mine, sems.at[0], sems.at[first + k if k < place.n_far else 6], dev)
            for k, dev in enumerate(place.plane_peers)
        ] + [
            remote(lacking, lacking, sems.at[2], sems.at[3], place.other_core(chip)) for chip in place.near_to
        ] + [remote(lacking, lacking, sems.at[4], sems.at[5], place.sibling)]
        self.arrivals = [
            remote(whole(chip), whole(chip), sems.at[0], sems.at[first + k], place.sibling)
            for k, chip in enumerate(far)
        ]
        self.passes = [
            remote(rest(chip, place.core), rest(chip, place.core), sems.at[1], sems.at[onward + k], place.sibling)
            for k, chip in enumerate(far)
        ]
        self.passed = [
            remote(rest(chip, place.other), rest(chip, place.other), sems.at[1], sems.at[onward + k], place.sibling)
            for k, chip in enumerate(far)
        ]

    def total(self, send, recv, rows):
        ref = self.buf.at[pl.ds(0, rows)]
        return remote(ref, ref, self.sems.at[send], self.sems.at[recv], self.place.sibling)

    def send(self):
        for copy in self.copies:
            copy.start()

    def receive(self, use=None):
        place = self.place
        for arrival, onward in zip(self.arrivals, self.passes):
            arrival.wait_recv()
            onward.start()
        self.total(0, 6, place.n_near * self.window).wait_recv()
        self.total(2, 3, place.n_near * self.keep).wait_recv()
        self.total(4, 5, self.keep).wait_recv()
        if use is not None:
            for chip in [place.chip] + place.near_from:
                use(chip)
        for copy, chip in zip(self.passed, place.plane_from):
            copy.wait_recv()
            if use is not None:
                use(chip)

    def drain(self):
        place = self.place
        self.total(0, 6, (place.n_far + place.n_near) * self.window).wait_send()
        self.total(1, 6, place.n_far * self.keep).wait_send()
        self.total(2, 3, place.n_near * self.keep).wait_send()
        self.total(4, 5, self.keep).wait_send()


def invert(work, out_ref):
    rank = work.shape[0]
    size = 8
    lanes = lax.broadcasted_iota(jnp.int32, (size, rank), 1)
    lane = lanes[0:1]
    for r in range(0, rank, size):
        row = [work[r + i:r + i + 1, :] for i in range(size)]
        a = [[jnp.broadcast_to(row[i][:, r + j:r + j + 1], (1, rank)) for j in range(i + 1)] for i in range(size)]
        inside = (lane >= r) & (lane < r + size)
        row = [jnp.where(inside, jnp.where(lane == r + i, 1.0, 0.0), row[i]) for i in range(size)]
        e = [[None] * size for _ in range(size)]
        pivot, recip = [], []
        for j in range(size):
            pivot.append(a[j][j])
            recip.append(1.0 / a[j][j])
            for i in range(j + 1, size):
                m = a[i][j] * recip[j]
                for k in range(j + 1, i + 1):
                    a[i][k] = a[i][k] - m * a[k][j]
                for k in range(j):
                    e[i][k] = e[i][k] - m * e[j][k]
                e[i][j] = -m
        z = []
        for i in range(size):
            t = row[i]
            for j in range(i):
                t = t + e[i][j] * row[j]
            z.append(t)
        y = []
        zq = [z[i] * recip[i] for i in range(size)]
        for i in range(size):
            t = zq[i]
            for k in range(i + 1, size):
                t = t + e[k][i] * zq[k]
            y.append(t)
        out = jnp.concatenate([z[i] * lax.rsqrt(pivot[i]) for i in range(size)], axis=0)
        out_ref[r:r + size, :] = jnp.where(lanes < r + size, out, 0.0)
        for s in range(r + size, rank, size):
            old = work[s:s + size, :]
            acc = jnp.where((lanes >= r) & (lanes < r + size), 0.0, old)
            for k in range(size):
                acc = acc - jnp.broadcast_to(old[:, r + k:r + k + 1], (size, rank)) * y[k]
            work[s:s + size, :] = acc


def mega_kernel(
    n_dp, n_mp,
    mom_hbm, tile_hbm, exps_hbm, prev_hbm, over_ref,
    ortho_ref, low_ref, inv_ref, share_ref, sum_ref,
    both, exps, scale, prev, right, both_t, flag_z, flag_p, left_t,
    part, left_in, left, left_hl, gram, gram_zc, gram_p, gram_all, work, tri,
    core_send, core_in, core_out, plane_in, step_out, step_in, mine, sq_z, sq_p,
    sem_in, sem_gather, sem_fz, sem_fp, sem_lr, sem_lg, sem_gz, sem_gp, sem_gg,
    sem_core, sem_plane, sem_step, sem_low, sem_sz, sem_sp,
):
    place = Place(n_dp, n_mp)
    rows, cols = mom_hbm.shape
    share, rank = share_ref.shape
    block = 2 * share
    window = share + -share % 16
    keep = block - window
    loads = [
        pltpu.make_async_copy(src, dst, sem_in.at[k])
        for k, (src, dst) in enumerate(
            [
                (prev_hbm, prev), (exps_hbm, exps),
                (mom_hbm, both.at[0:rows]), (tile_hbm, both.at[rows:2 * rows]),
            ]
        )
    ]
    for load in loads:
        load.start()
    barrier = pltpu.get_barrier_semaphore()
    friends = place.zc_peers[:-1] + place.plane_all
    for dev in friends:
        pl.semaphore_signal(barrier, inc=1, device_id=dev, device_id_type=MESH)
    kept = jnp.where(over_ref[0, 0] == 0, 1.0, 0.0).astype(F32)
    me = place.chip * 2 + place.core
    flag_p[me] = jnp.full((1, 128), kept, F32)
    loads[1].wait()
    scales = jnp.exp2(exps[...].astype(F32)).astype(BF16).astype(F32) * kept
    for j in range(cols // BLOCK):
        for b in range(rows // BLOCK):
            scale[b, :, j * BLOCK:(j + 1) * BLOCK] = jnp.broadcast_to(scales[b:b + 1, j:j + 1], (16, BLOCK)).astype(BF16)
    loads[0].wait()
    gather = WindowGather(place, right, 2 * window, window, sem_gather)
    mine_low = prev[...].astype(BF16).astype(F32)
    if window > share:
        mine_low = jnp.concatenate([mine_low, jnp.zeros((window - share, rank), F32)], axis=0)
    right[pl.ds(pl.multiple_of(me * window, 16), window)] = mine_low.astype(BF16)
    pl.semaphore_wait(barrier, len(friends))

    exchange(place.plane_all, lambda k: flag_p.at[me], flag_p.at[me], sem_fp)
    gather.send()

    loads[2].wait()
    loads[3].wait()

    def decode(j, carry):
        at = pl.ds(pl.multiple_of(j * BLOCK, BLOCK), BLOCK)
        for b in range(rows // BLOCK):
            factor_of = scale[b, :, at]
            for r in range(rows + b * BLOCK, rows + (b + 1) * BLOCK, 16):
                both[r:r + 16, at] = both[r:r + 16, at] * factor_of
        return carry

    lax.fori_loop(0, cols // BLOCK, decode, 0)

    def transpose(j, carry):
        at = pl.ds(pl.multiple_of(j * BLOCK, BLOCK), BLOCK)
        both_t[at, :rows] = both[0:rows, at].T
        both_t[at, rows:] = both[rows:2 * rows, at].T
        return carry

    lax.fori_loop(0, cols // BLOCK, transpose, 0, unroll=2)

    left_t[...] = jnp.zeros_like(left_t)
    all_p = flag_p.at[pl.ds(0, n_mp - 1)]
    arrived(place, all_p, sem_fp)
    flag_z[place.z] = jnp.sum(flag_p[...], axis=0)
    exchange(place.z_peers, lambda k: flag_z.at[place.z], flag_z.at[place.z], sem_fz)

    def rows_of(chip):
        return pl.ds(pl.multiple_of(chip * block, 16), block)

    def use(chip):
        got = right[pl.ds(pl.multiple_of(chip * 2 * window, 16), 2 * window), :].astype(F32)
        got = jnp.concatenate([got[:share], got[window:window + share]], axis=0).astype(BF16)
        left_t[...] += jnp.dot(got.T, both_t[rows_of(chip), :], preferred_element_type=F32)

    gather.receive(use)
    all_z = flag_z.at[pl.ds(0, n_dp - 1)]
    arrived(place, all_z, sem_fz)
    healthy = jnp.sum(flag_z[...], axis=0)
    factor = float(n_dp * n_mp) / jnp.maximum(healthy, 1.0)
    for r in range(0, rows, BLOCK):
        part[r:r + BLOCK, :] = (left_t[:, r:r + BLOCK] + factor * left_t[:, rows + r:rows + r + BLOCK]).T

    rz = rows // place.nz
    for k, z in enumerate(place.zs):
        remote(
            part.at[pl.ds(pl.multiple_of(z * rz, 8), rz)], left_in.at[k], sem_lr.at[0], sem_lr.at[1],
            place.z_peers[k],
        ).start()

    wide = jnp.broadcast_to(factor[:, 0:1], (16, BLOCK))

    def add(j, carry):
        at = pl.ds(pl.multiple_of(j * BLOCK, BLOCK), BLOCK)
        for r in range(0, rows, 16):
            sum_ref[r:r + 16, at] = both[r:r + 16, at].astype(F32) + wide * both[rows + r:rows + r + 16, at].astype(F32)
        return carry

    own = pl.ds(pl.multiple_of(place.z * rz, 8), rz)
    acc = part[own]
    arrived(place, left_in, sem_lr)
    for k in range(n_dp - 1):
        acc = acc + left_in[k]
    left[own] = acc
    gram[...] = lax.dot_general(acc, acc, (((0,), (0,)), ((), ())), precision=HIGH, preferred_element_type=F32)
    gs = rank // (2 * place.nz)
    for k, spot in enumerate(place.zc_spots):
        remote(
            gram.at[pl.ds(pl.multiple_of(spot * gs, 8), gs)], gram_zc.at[k], sem_gz.at[0], sem_gz.at[1],
            place.zc_peers[k],
        ).start()
    exchange(place.z_peers, lambda k: left.at[own], left.at[own], sem_lg)
    lax.fori_loop(0, cols // BLOCK, add, 0)
    piece = pl.ds(pl.multiple_of((place.z * 2 + place.core) * gs, 8), gs)
    acc = gram[piece]
    arrived(place, gram_zc, sem_gz)
    for k in range(2 * n_dp - 1):
        acc = acc + gram_zc[k]
    gram_p[place.chip] = acc
    exchange(place.plane_peers, lambda k: gram_p.at[place.chip], gram_p.at[place.chip], sem_gp)
    all_left = left.at[pl.ds(0, rows - rz)]
    arrived(place, all_left, sem_lg)

    high = left[...].astype(BF16)
    left_hl[:, :rank] = high
    left_hl[:, rank:] = (left[...] - high.astype(F32)).astype(BF16)
    def raw_part(chip, core):
        at = pl.ds(pl.multiple_of(chip * block + core * keep, 16), window)
        mom_two = jnp.dot(both_t[at, :rows], left_hl[...], preferred_element_type=F32)
        grad_two = jnp.dot(both_t[at, rows:], left_hl[...], preferred_element_type=F32)
        return mom_two[:, :rank] + mom_two[:, rank:] + factor * (grad_two[:, :rank] + grad_two[:, rank:])

    core_copies = {}

    def for_sibling(a):
        for b, chip in enumerate(place.other_group[a]):
            core_send[a, b] = raw_part(chip, place.other)
        core_copies[a] = remote(core_send.at[a], core_in.at[a], sem_core.at[0], sem_core.at[1 + a], place.sibling)
        core_copies[a].start()

    def for_plane(a):
        parts = [raw_part(chip, place.core) for chip in place.group[a]]
        core_copies[a].wait_recv()
        for b, value in enumerate(parts):
            core_out[a, b] = value + core_in[a, b]
        if a:
            remote(core_out.at[a], plane_in.at[a - 1], sem_plane.at[0], sem_plane.at[1], place.step_one[a]).start()

    n_side = place.nx
    for_sibling(place.steps[0])
    for ahead, a in zip(place.steps[1:], place.steps):
        for_sibling(ahead)
        for_plane(a)
    last = place.chips - 1
    all_gp = gram_p.at[pl.ds(0, last)]
    arrived(place, all_gp, sem_gp)
    gram_all[piece] = jnp.sum(gram_p[...], axis=0)
    exchange(place.zc_peers, lambda k: gram_all.at[piece], gram_all.at[piece], sem_gg)
    for_plane(0)
    arrived(place, plane_in, sem_plane)
    for b in place.steps:
        total = core_out[0, b]
        for a in range(n_side - 1):
            total = total + plane_in[a, b]
        if b:
            step_out[b - 1] = total
            remote(step_out.at[b - 1], step_in.at[b - 1], sem_step.at[0], sem_step.at[1], place.step_two[b]).start()
    all_gram = gram_all.at[pl.ds(0, rank - gs)]
    arrived(place, all_gram, sem_gg)
    work[...] = gram_all[...]
    invert(work, tri)
    arrived(place, step_in, sem_step)
    for b in range(n_side - 1):
        total = total + step_in[b]
    by_rank = (((1,), (1,)), ((), ()))
    total = lax.dot_general(total, tri[...], by_rank, precision=HIGH, preferred_element_type=F32)
    mine[...] = total
    own_share = mine[pl.ds(pl.multiple_of(place.core * (window - share), 8), share)]
    sq_p[me] = jnp.sum(own_share * own_share, axis=0, keepdims=True)
    exchange(place.plane_all, lambda k: sq_p.at[me], sq_p.at[me], sem_sp)
    low_ref[pl.ds(pl.multiple_of(place.chip * block + place.core * keep, 16), window)] = total.astype(BF16)
    last_gather = WindowGather(place, low_ref, block, window, sem_low)
    last_gather.send()
    share_ref[...] = own_share
    ortho_ref[...] = lax.dot_general(
        left[...], tri[...], by_rank, precision=HIGH, preferred_element_type=F32
    ).astype(BF16)
    arrived(place, sq_p.at[pl.ds(0, n_mp - 1)], sem_sp)
    sq_z[place.z] = jnp.sum(sq_p[...], axis=0)
    exchange(place.z_peers, lambda k: sq_z.at[place.z], sq_z.at[place.z], sem_sz)
    last_gather.receive()
    arrived(place, sq_z.at[pl.ds(0, n_dp - 1)], sem_sz)
    squares = jnp.sum(sq_z[...], axis=0)
    inv_ref[...] = jnp.broadcast_to(lax.rsqrt(squares + EPSILON), inv_ref.shape)
    for ref, sems in [
        (all_z, sem_fz), (all_p, sem_fp), (left_in, sem_lr), (all_left, sem_lg), (gram_zc, sem_gz), (all_gp, sem_gp),
        (all_gram, sem_gg), (plane_in, sem_plane), (step_in, sem_step), (core_send, sem_core),
        (sq_z.at[pl.ds(0, n_dp - 1)], sem_sz), (sq_p.at[pl.ds(0, n_mp - 1)], sem_sp),
    ]:
        sent(place, ref, sems)
    gather.drain()
    last_gather.drain()


def mega_stage(n_dp, n_mp, momentum, tile_values, exponents, right_prev, overflow):
    rows, cols = momentum.shape
    share, rank = right_prev.shape
    chips = n_mp // 2
    block = 2 * share
    window = share + -share % 16
    side = int(round(math.sqrt(chips)))
    n_near = 4 if side > 2 else 2
    n_far = chips - 1 - n_near
    vmem = pl.BlockSpec(memory_space=pltpu.VMEM)
    hbm = pl.BlockSpec(memory_space=pltpu.HBM)
    dma = pltpu.SemaphoreType.DMA
    return pl.pallas_call(
        functools.partial(mega_kernel, n_dp, n_mp),
        name="mega",
        out_shape=(
            jax.ShapeDtypeStruct((rows, rank), BF16),
            jax.ShapeDtypeStruct((cols, rank), BF16),
            jax.ShapeDtypeStruct((8, 128), F32),
            jax.ShapeDtypeStruct((share, rank), F32),
            jax.ShapeDtypeStruct((rows, cols), F32),
        ),
        in_specs=[hbm] * 4 + [pl.BlockSpec(memory_space=pltpu.SMEM)],
        out_specs=(vmem,) * 5,
        scratch_shapes=[
            pltpu.VMEM((2 * rows, cols), BF16),
            pltpu.VMEM(exponents.shape, jnp.int32),
            pltpu.VMEM((rows // BLOCK, 16, cols), BF16),
            pltpu.VMEM((share, rank), F32),
            pltpu.VMEM((n_mp * window, rank), BF16),
            pltpu.VMEM((cols, 2 * rows), BF16),
            pltpu.VMEM((n_dp, 1, 128), F32),
            pltpu.VMEM((n_mp, 1, 128), F32),
            pltpu.VMEM((rank, 2 * rows), F32),
            pltpu.VMEM((rows, rank), F32),
            pltpu.VMEM((n_dp - 1, rows // n_dp, rank), F32),
            pltpu.VMEM((rows, rank), F32),
            pltpu.VMEM((rows, 2 * rank), BF16),
            pltpu.VMEM((rank, rank), F32),
            pltpu.VMEM((2 * n_dp - 1, rank // (2 * n_dp), rank), F32),
            pltpu.VMEM((chips, rank // (2 * n_dp), rank), F32),
            pltpu.VMEM((rank, rank), F32),
            pltpu.VMEM((rank, rank), F32),
            pltpu.VMEM((rank, rank), F32),
            pltpu.VMEM((side, side, window, rank), F32),
            pltpu.VMEM((side, side, window, rank), F32),
            pltpu.VMEM((side, side, window, rank), F32),
            pltpu.VMEM((side - 1, side, window, rank), F32),
            pltpu.VMEM((side - 1, window, rank), F32),
            pltpu.VMEM((side - 1, window, rank), F32),
            pltpu.VMEM((window, rank), F32),
            pltpu.VMEM((n_dp, 1, 128), F32),
            pltpu.VMEM((n_mp, 1, 128), F32),
            dma((4,)),
            dma((7 + 2 * n_far,)),
            dma((2,)),
            dma((2,)),
            dma((2,)),
            dma((2,)),
            dma((2,)),
            dma((2,)),
            dma((2,)),
            dma((1 + side,)),
            dma((2,)),
            dma((2,)),
            dma((7 + 2 * n_far,)),
            dma((2,)),
            dma((2,)),
        ],
        compiler_params=pltpu.CompilerParams(
            collective_id=0, has_side_effects=True, vmem_limit_bytes=VMEM_LIMIT
        ),
    )(momentum, tile_values, exponents, right_prev, overflow)


def finish_kernel(unit, sums, ortho, low, inv, share, new, upd, share_out, new_v, upd_v, sem):
    rows, cols = sums.shape
    step = 256
    base = ortho[...]
    scaled = (base.astype(F32) * inv[0:1, :]).astype(BF16)
    both = (((1,), (1,)), ((), ()))
    share_copy = pltpu.make_async_copy(share, share_out, sem.at[2])
    share_copy.start()
    for t in range(cols // step):
        at = slice(t * step, (t + 1) * step)
        piece = low[at, :]
        correction = lax.dot_general(base, piece, both, preferred_element_type=F32)
        new_v[:, at] = (sums[:, at] - (1.0 - RETAIN) * correction).astype(BF16)
        direction = lax.dot_general(scaled, piece, both, preferred_element_type=F32)
        upd_v[:, at] = (unit * direction).astype(BF16)
        for k, (src, dst) in enumerate([(new_v, new), (upd_v, upd)]):
            pltpu.make_async_copy(src.at[:, at], dst.at[:, at], sem.at[k]).start()
    share_copy.wait()
    for k, (src, dst) in enumerate([(new_v, new), (upd_v, upd)]):
        pltpu.make_async_copy(src, dst, sem.at[k]).wait()


def finish_stage(unit, sums, ortho, low, inv, share):
    rows, cols = sums.shape
    vmem = pl.BlockSpec(memory_space=pltpu.VMEM)
    hbm = pl.BlockSpec(memory_space=pltpu.HBM)
    return pl.pallas_call(
        functools.partial(finish_kernel, unit),
        name="finish",
        out_shape=(
            jax.ShapeDtypeStruct((rows, cols), BF16),
            jax.ShapeDtypeStruct((rows, cols), BF16),
            jax.ShapeDtypeStruct(share.shape, F32),
        ),
        in_specs=[vmem] * 5,
        out_specs=(hbm,) * 3,
        scratch_shapes=[
            pltpu.VMEM((rows, cols), BF16),
            pltpu.VMEM((rows, cols), BF16),
            pltpu.SemaphoreType.DMA((3,)),
        ],
        compiler_params=pltpu.CompilerParams(vmem_limit_bytes=VMEM_LIMIT),
    )(sums, ortho, low, inv, share)


def body(n_dp, n_mp, momentum, tile_values, exponents, overflow, right_prev):
    rows, cols = momentum.shape
    rank = right_prev.shape[1]
    unit = math.sqrt(rows * n_mp * cols * n_dp / rank)
    args = [
        pltpu.with_memory_space_constraint(a, pltpu.HBM)
        for a in (momentum, tile_values, exponents, right_prev)
    ]
    ortho, low, inv, own, sums = mega_stage(n_dp, n_mp, *args, overflow)
    new, update, right_out = finish_stage(unit, sums, ortho, low, inv, own)
    return new, right_out, update


def solution(mesh):
    in_specs = (P("mp", "dp"), P("mp", "dp"), P("mp", "dp"), P("mp", "dp"), P(("dp", "mp"), None))
    out_specs = (P("mp", "dp"), P(("dp", "mp"), None), P("mp", "dp"))
    step = functools.partial(body, mesh.shape["dp"], mesh.shape["mp"])
    return jax.shard_map(step, mesh=mesh, in_specs=in_specs, out_specs=out_specs, check_vma=False)
```
